32 devices in a mesh: rep: 4 (over y, x), fsdp: 8 (over z, core).
Axes of the slice: x: 2, y: 2, z: 4, core: 2. Of those that a mesh axis runs over, the one named last changes fastest.
Arguments:
- features: bfloat16 [32, 32, 32, 640], P(('rep', 'fsdp')), may hold values from -20 to 20
- out_grad: bfloat16 [32, 32, 32, 640], P(('rep', 'fsdp')), may hold values from -6 to 6
- conv_weight: bfloat16 [5760, 640], P('fsdp'), may hold values from -0.078125 to 0.078125
- conv_bias: bfloat16 [640], P('fsdp'), may hold values from -3 to 3
- norm_gain: bfloat16 [640], P('fsdp'), may hold values from 0.099609375 to 1.8984375
- norm_shift: bfloat16 [640], P('fsdp'), may hold values from -3 to 3
Outputs:
- conv_out: bfloat16 [32, 32, 32, 640], P(('rep', 'fsdp'))
- in_grad: bfloat16 [32, 32, 32, 640], P(('rep', 'fsdp'))
- weight_grad: float32 [5760, 640], P('fsdp')
- bias_grad: float32 [640], P('fsdp')
- gain_grad: float32 [640], P('fsdp')
- shift_grad: float32 [640], P('fsdp')
The draws below stay inside these ranges and needn't reach their ends.
All inputs are finite; a program needn't handle non-finite values.
Results may differ from the reference program's by a relative error of at most 0.0036.
Values may be sent and summed in bfloat16 or wider, within the bound.
No kernel may reach another device: no remote copies, remote signals or barrier semaphores. Data moves between devices by JAX's collectives and lax.ppermute only.
A program may use at most 128 MiB of HBM per device.

```python
import math
import jax
import jax.numpy as jnp
from jax import lax

HW = 32
CIN = 640
COUT = 640
GROUPS = 16
IMAGES = 32


def draw_features(key, part):
    key_pixel, key_chan, key_base = jax.random.split(key, 3)
    half_log = 0.5 * math.log(10.0)
    pixel_scale = jnp.exp(jax.random.uniform(key_pixel, (IMAGES, HW, HW, 1), jnp.float32) * half_log)
    chan_scale = jnp.exp(jax.random.uniform(key_chan, (IMAGES, 1, 1, CIN), jnp.float32) * half_log)
    base_vals = jax.random.normal(key_base, (IMAGES, HW, HW, CIN), jnp.float32)
    base_vals = jnp.clip(base_vals, -4.0, 4.0)
    return (0.5 * base_vals * pixel_scale * chan_scale).astype(jnp.bfloat16)


def steps_of(rng, shape, cuts, least, largest):
    def one(axis_at, blocks):
        heights = jax.random.uniform(jax.random.fold_in(jax.random.fold_in(rng, 6), axis_at), (blocks,), jnp.float32, least / len(cuts), largest / len(cuts))
        return jnp.repeat(jnp.exp(heights), shape[axis_at] // blocks).reshape((-1,) + (1,) * (len(shape) - axis_at - 1))

    level = one(*cuts[0])
    for cut in cuts[1:]:
        level = level * one(*cut)
    return level


def normal_values(key, shape, width, limit, cuts=(), held_as=jnp.bfloat16):
    drawn = width * jax.random.normal(key, shape, jnp.float32)
    if cuts:
        drawn = drawn * steps_of(key, shape, cuts, -0.22, 0.18)
    return jnp.clip(drawn, -limit, limit).astype(held_as)


def setup_inputs(seed: int = 0) -> dict:
    key_list = jax.random.split(jax.random.key(seed), 7)
    return {
        "features": draw_features(jax.random.fold_in(key_list[6], 71), 0),
        "out_grad": normal_values(key_list[1], (IMAGES, HW, HW, COUT), 1.0, 6.0, ((0, 32),)),
        "conv_weight": normal_values(key_list[2], (9 * CIN, COUT), (9 * CIN) ** -0.5, 0.078125, ((0, 8),)),
        "conv_bias": normal_values(key_list[3], (COUT,), 1.0, 3.0, ((0, 8),)),
        "norm_gain": jnp.clip(1.0 + 0.18 * jax.random.normal(key_list[4], (CIN,), jnp.float32), 0.099609375, 1.8984375).astype(jnp.bfloat16),
        "norm_shift": normal_values(key_list[5], (CIN,), 0.7, 3.0, ((0, 8),)),
    }


epsilon = 1e-05

def reference(features, out_grad, conv_weight, conv_bias, norm_gain, norm_shift):
    group_size = CIN // GROUPS
    pixels = HW * HW
    values = features.astype(jnp.float32).reshape(IMAGES, pixels, GROUPS, group_size)
    group_mean = lax.optimization_barrier(jnp.mean(values, axis=(1, 3), keepdims=True))
    centered = values - group_mean
    group_var = lax.optimization_barrier(jnp.mean(centered * centered, axis=(1, 3), keepdims=True))
    inv_std = lax.rsqrt(group_var + epsilon)
    normed = centered * inv_std
    gain_cols = norm_gain.astype(jnp.float32).reshape(1, 1, GROUPS, group_size)
    shift_cols = norm_shift.astype(jnp.float32).reshape(1, 1, GROUPS, group_size)
    pre_act = normed * gain_cols + shift_cols
    activated = jax.nn.silu(pre_act).astype(jnp.bfloat16).reshape(IMAGES, HW, HW, CIN)
    padded = jnp.pad(activated, ((0, 0), (1, 1), (1, 1), (0, 0)))
    grad_rows = out_grad.reshape(IMAGES * pixels, COUT)
    conv_sum = jnp.zeros((IMAGES * pixels, COUT), jnp.float32)
    grad_padded = jnp.zeros((IMAGES, HW + 2, HW + 2, CIN), jnp.float32)
    weight_list = []
    for row_off in range(3):
        for col_off in range(3):
            tap_index = 3 * row_off + col_off
            tap_rows = conv_weight[tap_index * CIN:(tap_index + 1) * CIN]
            tap_piece = padded[:, row_off:row_off + HW, col_off:col_off + HW, :].reshape(IMAGES * pixels, CIN)
            conv_sum = conv_sum + jnp.dot(tap_piece, tap_rows, preferred_element_type=jnp.float32)
            tap_grad = lax.dot_general(grad_rows, tap_rows, (((1,), (1,)), ((), ())), preferred_element_type=jnp.float32)
            grad_padded = grad_padded.at[:, row_off:row_off + HW, col_off:col_off + HW, :].add(tap_grad.reshape(IMAGES, HW, HW, CIN))
            weight_list.append(lax.dot_general(tap_piece, grad_rows, (((0,), (0,)), ((), ())), preferred_element_type=jnp.float32))
    conv_out = (conv_sum + conv_bias.astype(jnp.float32)[None, :]).astype(jnp.bfloat16).reshape(IMAGES, HW, HW, COUT)
    act_grad = grad_padded[:, 1:-1, 1:-1, :].reshape(IMAGES, pixels, GROUPS, group_size)
    sig_pre = jax.nn.sigmoid(pre_act)
    pre_grad = act_grad * sig_pre * (1.0 + pre_act * (1.0 - sig_pre))
    norm_grad = pre_grad * gain_cols
    grad_mean = lax.optimization_barrier(jnp.mean(norm_grad, axis=(1, 3), keepdims=True))
    cross_mean = lax.optimization_barrier(jnp.mean(norm_grad * normed, axis=(1, 3), keepdims=True))
    in_grad = ((norm_grad - grad_mean - normed * cross_mean) * inv_std).astype(jnp.bfloat16).reshape(IMAGES, HW, HW, CIN)
    grad_scale = 1.0 / math.sqrt(IMAGES * HW * HW)
    weight_grad = jnp.concatenate(weight_list, axis=0) * grad_scale
    bias_grad = lax.optimization_barrier(jnp.sum(grad_rows.astype(jnp.float32), axis=0)) * grad_scale
    gain_grad = lax.optimization_barrier(jnp.sum(pre_grad * normed, axis=(0, 1))).reshape(CIN) * grad_scale
    shift_grad = lax.optimization_barrier(jnp.sum(pre_grad, axis=(0, 1))).reshape(CIN) * grad_scale
    return (conv_out, in_grad, weight_grad, bias_grad, gain_grad, shift_grad)
```

```python
import functools
import math

import jax
import jax.numpy as jnp
from jax import lax
from jax.experimental import pallas as pl
from jax.experimental.pallas import tpu as pltpu
from jax.sharding import PartitionSpec as P

GROUPS = 16


epsilon = 1e-05

F32 = jnp.float32
BF16 = jnp.bfloat16
VMEM = pl.BlockSpec(memory_space=pltpu.VMEM)
SMEM = pl.BlockSpec(memory_space=pltpu.SMEM)
ANY = pl.BlockSpec(memory_space=pl.ANY)


def params(mib=56):
    return pltpu.CompilerParams(vmem_limit_bytes=mib * 1024 * 1024)


def struct(shape, dtype):
    return jax.ShapeDtypeStruct(shape, dtype)


def shifted_copies(x, side, out_ref, first):
    pixels = x.shape[0]
    column = lax.broadcasted_iota(jnp.int32, x.shape, 0) % side
    edge = jnp.zeros((side, x.shape[1]), BF16)
    for kx in range(3):
        move = (kx - 1) if first else (1 - kx)
        if move == 0:
            moved = x
        elif move == 1:
            moved = jnp.where(column == side - 1, 0.0, pltpu.roll(x, pixels - 1, 0))
        else:
            moved = jnp.where(column == 0, 0.0, pltpu.roll(x, 1, 0))
        out_ref[kx, 0:side, :] = edge
        out_ref[kx, side : side + pixels, :] = moved.astype(BF16)
        out_ref[kx, side + pixels : 2 * side + pixels, :] = edge


def shift_kernel(side, x_ref, out_ref, sum_ref):
    x = x_ref[...].astype(F32)
    sum_ref[...] = jnp.sum(x, axis=0, keepdims=True)
    shifted_copies(x, side, out_ref, False)


def shift_grad(x, side):
    pixels, chans = x.shape
    return pl.pallas_call(
        functools.partial(shift_kernel, side),
        out_shape=(
            struct((3, pixels + 2 * side, chans), BF16),
            struct((1, chans), F32),
        ),
        in_specs=[VMEM],
        out_specs=(VMEM, VMEM),
        compiler_params=params(),
        cost_estimate=pl.CostEstimate(
            flops=8 * x.size, bytes_accessed=8 * x.size, transcendentals=0
        ),
        name="shift_grad",
    )(x)


def same_group(chans):
    size = chans // GROUPS
    a = lax.broadcasted_iota(jnp.int32, (chans, chans), 0) // size
    b = lax.broadcasted_iota(jnp.int32, (chans, chans), 1) // size
    return jnp.where(a == b, 1.0, 0.0).astype(F32)


def group_mean_of(column_sum, pixels):
    chans = column_sum.shape[1]
    count = pixels * (chans // GROUPS)
    total = jnp.dot(
        jnp.broadcast_to(column_sum, (8, chans)),
        same_group(chans),
        preferred_element_type=F32,
        precision=lax.Precision.HIGHEST,
    )
    return total[0:1] * (1.0 / count)


def stats_kernel(x_ref, out_ref):
    pixels = x_ref.shape[0]
    x = x_ref[...].astype(F32)
    mean = group_mean_of(jnp.sum(x, axis=0, keepdims=True), pixels)
    centered = x - mean
    var = group_mean_of(jnp.sum(centered * centered, axis=0, keepdims=True), pixels)
    out_ref[0:1, :] = mean
    out_ref[1:2, :] = lax.rsqrt(var + epsilon)


def stats(x):
    return pl.pallas_call(
        stats_kernel,
        out_shape=struct((2, x.shape[1]), F32),
        in_specs=[VMEM],
        out_specs=VMEM,
        compiler_params=params(),
        cost_estimate=pl.CostEstimate(
            flops=5 * x.size, bytes_accessed=2 * x.size, transcendentals=0
        ),
        name="norm_stats",
    )(x)


def act_kernel(side, x_ref, stat_ref, vec_ref, shifted_ref, turned_ref):
    mean, inv = stat_ref[0:1, :], stat_ref[1:2, :]
    gain = vec_ref[0:1, :].astype(F32)
    shift = vec_ref[1:2, :].astype(F32)
    pre = (x_ref[...].astype(F32) - mean) * inv * gain + shift
    act = (pre / (1.0 + jnp.exp(-pre))).astype(BF16)
    turned_ref[...] = act.T
    shifted_copies(act.astype(F32), side, shifted_ref, True)


def activate(x, stat, vecs, side):
    pixels, chans = x.shape
    return pl.pallas_call(
        functools.partial(act_kernel, side),
        out_shape=(
            struct((3, pixels + 2 * side, chans), BF16),
            struct((chans, pixels), BF16),
        ),
        in_specs=[VMEM, VMEM, VMEM],
        out_specs=(VMEM, VMEM),
        compiler_params=params(),
        cost_estimate=pl.CostEstimate(
            flops=16 * x.size, bytes_accessed=10 * x.size, transcendentals=2 * x.size
        ),
        name="activate",
    )(x, stat, vecs)


def weight_kernel(
    side, extra, piece, place_ref, own_t, sib_t, own_g, sib_g,
    keep_ref, send0_ref, send1_ref, block_ref,
):
    chans, pixels = own_t.shape
    r, z, core = place_ref[0], place_ref[1], place_ref[2]
    blocks = keep_ref.shape[0] * keep_ref.shape[1]
    half = keep_ref.shape[1]
    reps = 2 * keep_ref.shape[2]

    def tap_rows(ref, tap):
        start = pl.multiple_of((2 - tap // 3) * side, side)
        return ref[tap % 3, pl.ds(start, pixels), :]

    for k in range(blocks):
        tap = 2 * k + core
        low, high = 2 * extra * k, 2 * extra * (k + 1)
        first = jnp.dot(
            own_t[low:chans, :], tap_rows(own_g, tap), preferred_element_type=F32
        ) + jnp.dot(sib_t[low:chans, :], tap_rows(sib_g, tap), preferred_element_type=F32)
        block_ref[0 : chans - low, :] = first
        second = jnp.dot(
            own_t[0:high, :], tap_rows(own_g, tap + 1), preferred_element_type=F32
        ) + jnp.dot(sib_t[0:high, :], tap_rows(sib_g, tap + 1), preferred_element_type=F32)
        block_ref[chans - low : chans + 2 * extra, :] = second
        rel_z = k ^ z
        path, slot = rel_z // half, rel_z % half
        step = (chans + extra - piece) // (reps - 1)

        def rows_of(rel):
            at = pl.multiple_of(extra * core + step * (r ^ rel), 16)
            return block_ref[pl.ds(at, piece), :]

        keep_ref[path, slot, 0] = rows_of(0)

        @pl.when(path == 0)
        def _():
            send0_ref[slot, 0] = rows_of(1).astype(BF16)
            keep_ref[0, slot, 1] = rows_of(2)
            send0_ref[slot, 1] = rows_of(3).astype(BF16)

        @pl.when(path == 1)
        def _():
            send1_ref[slot, 0] = rows_of(2).astype(BF16)
            keep_ref[1, slot, 1] = rows_of(1)
            send1_ref[slot, 1] = rows_of(3).astype(BF16)


def weight_pieces(place, own_t, sib_t, own_g, sib_g, side, blocks, extra, piece):
    chans, pixels = own_t.shape
    outs = own_g.shape[2]
    half = blocks // 2
    return pl.pallas_call(
        functools.partial(weight_kernel, side, extra, piece),
        out_shape=(
            struct((2, half, 2, piece, outs), F32),
            struct((half, 2, piece, outs), BF16),
            struct((half, 2, piece, outs), BF16),
        ),
        in_specs=[SMEM, VMEM, VMEM, VMEM, VMEM],
        out_specs=(VMEM, VMEM, VMEM),
        scratch_shapes=[pltpu.VMEM((chans + 2 * extra, outs), F32)],
        compiler_params=params(),
        cost_estimate=pl.CostEstimate(
            flops=4 * blocks * (chans + 2 * extra) * pixels * outs,
            bytes_accessed=30 * chans * pixels,
            transcendentals=0,
        ),
        name="weight_grad",
    )(place, own_t, sib_t, own_g, sib_g)


def fetch_weight(place_ref, gathered, near, far, near_sib, far_sib, weight, sems):
    core, side_half = place_ref[2], place_ref[3]
    shards, window, _ = gathered.shape
    cut = near.shape[1]
    rows = window + 2 * cut
    mine = side_half * (rows - window)
    other = (1 - side_half) * window
    copies = []

    def copy(src, row, count):
        copies.append(
            pltpu.make_async_copy(
                src, weight.at[pl.ds(pl.multiple_of(row, 16), count), :], sems.at[len(copies)]
            )
        )

    for f in range(shards):
        copy(gathered.at[f], f * rows + mine, window)
    for pair, (a, b) in enumerate(((near, far), (near_sib, far_sib))):
        parity = core if pair == 0 else 1 - core
        for z in range(near.shape[0]):
            base = (2 * z + parity) * rows + other
            copy(a.at[z], base, cut)
            copy(b.at[z], base + cut, cut)
    for c in copies:
        c.start()
    return copies


def grad_kernel(
    side, chunk, place_ref, g_ref, x_ref, stat_ref, vec_ref, gathered, near, far, near_sib, far_sib,
    out_ref, sum_ref, weight, scaled, sems,
):
    copies = fetch_weight(
        place_ref, gathered, near, far, near_sib, far_sib, weight, sems
    )
    for c in copies:
        c.wait()
    pixels, chans = x_ref.shape
    mean, inv = stat_ref[0:1, :], stat_ref[1:2, :]
    gain = vec_ref[0:1, :].astype(F32)
    shift = vec_ref[1:2, :].astype(F32)
    sum_ref[...] = jnp.zeros_like(sum_ref)

    @pl.loop(0, pixels // chunk)
    def _(i):
        total = None
        for tap in range(9):
            start = pl.multiple_of(i * chunk + (2 - tap // 3) * side, side)
            part = lax.dot_general(
                g_ref[tap % 3, pl.ds(start, chunk), :],
                weight[tap * chans : (tap + 1) * chans, :],
                (((1,), (1,)), ((), ())),
                preferred_element_type=F32,
            )
            total = part if total is None else total + part
        rows = pl.ds(pl.multiple_of(i * chunk, chunk), chunk)
        normed = (x_ref[rows, :].astype(F32) - mean) * inv
        pre = normed * gain + shift
        sig = 1.0 / (1.0 + jnp.exp(-pre))
        pre_grad = total * sig * (1.0 + pre * (1.0 - sig))
        sum_ref[0:1, :] += jnp.sum(pre_grad * normed, axis=0, keepdims=True)
        sum_ref[1:2, :] += jnp.sum(pre_grad, axis=0, keepdims=True)
        scaled[rows, :] = pre_grad * gain

    cross = group_mean_of(sum_ref[0:1, :] * gain, pixels)
    center = group_mean_of(sum_ref[1:2, :] * gain, pixels)

    @pl.loop(0, pixels // chunk)
    def _(i):
        rows = pl.ds(pl.multiple_of(i * chunk, chunk), chunk)
        normed = (x_ref[rows, :].astype(F32) - mean) * inv
        out_ref[rows, :] = ((scaled[rows, :] - center - normed * cross) * inv).astype(BF16)


def act_grad(place, shifted, x, stat, vecs, weights, side):
    pixels, chans = x.shape
    outs = shifted.shape[2]
    copies = weights[0].shape[0] + 4 * weights[1].shape[0]
    return pl.pallas_call(
        functools.partial(grad_kernel, side, 256),
        out_shape=(struct((pixels, chans), BF16), struct((2, chans), F32)),
        in_specs=[SMEM, VMEM, VMEM, VMEM, VMEM] + [ANY] * 5,
        out_specs=(VMEM, VMEM),
        scratch_shapes=[
            pltpu.VMEM((9 * chans, outs), BF16),
            pltpu.VMEM((pixels, chans), F32),
            pltpu.SemaphoreType.DMA((copies,)),
        ],
        compiler_params=params(),
        cost_estimate=pl.CostEstimate(
            flops=18 * chans * outs * pixels,
            bytes_accessed=18 * chans * outs + 12 * pixels * chans,
            transcendentals=2 * pixels * chans,
        ),
        name="act_grad",
    )(place, shifted, x, stat, vecs, *weights)


def conv_kernel(
    side, chunk, place_ref, a_ref, vec_ref, gathered, near, far, near_sib, far_sib,
    out_ref, weight, sems,
):
    copies = fetch_weight(
        place_ref, gathered, near, far, near_sib, far_sib, weight, sems
    )
    for c in copies:
        c.wait()
    pixels = out_ref.shape[0]
    chans = a_ref.shape[2]
    bias = vec_ref[2:3, :].astype(F32)

    @pl.loop(0, pixels // chunk)
    def _(i):
        total = None
        for tap in range(9):
            start = pl.multiple_of(i * chunk + (tap // 3) * side, side)
            part = jnp.dot(
                a_ref[tap % 3, pl.ds(start, chunk), :],
                weight[tap * chans : (tap + 1) * chans, :],
                preferred_element_type=F32,
            )
            total = part if total is None else total + part
        rows = pl.ds(pl.multiple_of(i * chunk, chunk), chunk)
        out_ref[rows, :] = (total + bias).astype(BF16)


def conv(place, shifted, vecs, weights, side):
    pixels = shifted.shape[1] - 2 * side
    chans = shifted.shape[2]
    outs = weights[0].shape[2]
    copies = weights[0].shape[0] + 4 * weights[1].shape[0]
    return pl.pallas_call(
        functools.partial(conv_kernel, side, 256),
        out_shape=struct((pixels, outs), BF16),
        in_specs=[SMEM, VMEM, VMEM] + [ANY] * 5,
        out_specs=VMEM,
        scratch_shapes=[
            pltpu.VMEM((9 * chans, outs), BF16),
            pltpu.SemaphoreType.DMA((copies,)),
        ],
        compiler_params=params(),
        cost_estimate=pl.CostEstimate(
            flops=18 * chans * outs * pixels,
            bytes_accessed=18 * chans * outs + 8 * pixels * chans,
            transcendentals=0,
        ),
        name="conv_forward",
    )(place, shifted, vecs, *weights)


def join_kernel(scale, place_ref, p0, p1, p2, p3, out_ref):
    r = place_ref[0]
    pieces = (p0, p1, p2, p3)
    piece = p0.shape[0]
    step = (out_ref.shape[0] - piece) // (len(pieces) - 1)
    for q in range(len(pieces)):
        for rel, ref in enumerate(pieces):

            @pl.when((q ^ r) == rel)
            def _():
                out_ref[step * q : step * q + piece, :] = ref[...].astype(F32) * scale


def join(place, pieces, rows, scale):
    outs = pieces[0].shape[1]
    return pl.pallas_call(
        functools.partial(join_kernel, scale),
        out_shape=struct((rows, outs), F32),
        in_specs=[SMEM] + [VMEM] * 4,
        out_specs=VMEM,
        compiler_params=params(),
        cost_estimate=pl.CostEstimate(
            flops=rows * outs, bytes_accessed=6 * rows * outs, transcendentals=0
        ),
        name="join_pieces",
    )(place, *pieces)


def swap(x, axis, mask):
    n = lax.axis_size(axis)
    return lax.ppermute(x, axis, [(i, i ^ mask) for i in range(n)])


def gather_small(x, axis):
    at = lax.axis_index(axis)
    got = x[None]
    mask = 1
    while mask < lax.axis_size(axis):
        other = swap(got, axis, mask)
        bit = (at // mask) % 2 == 1
        got = jnp.where(
            bit, jnp.concatenate([other, got]), jnp.concatenate([got, other])
        )
        mask *= 2
    return got


def sum_all(x, axis, masks):
    terms = [x] + [swap(x, axis, m) for m in masks]
    while len(terms) > 1:
        terms = [terms[i] + terms[i + 1] for i in range(0, len(terms), 2)]
    return terms[0]


def gather_weight(conv_weight, r, core, piece_window):
    rows = conv_weight.shape[0]
    window = piece_window
    upper = ((r ^ (r // 2)) % 2).astype(jnp.int32)
    mine = jnp.where(upper == 1, conv_weight[rows - window :], conv_weight[:window])
    gathered = lax.all_gather(mine, "fsdp", axis=0, tiled=False)
    shards, _, outs = gathered.shape
    by_core = gathered.reshape(shards // 2, 2, window, outs)
    same = jnp.where(core == 1, by_core[:, 1], by_core[:, 0])
    cut = (rows - window) // 2
    lead = window - 2 * cut
    sends = [
        jnp.where(
            upper == 1,
            same[:, lead + s * cut : lead + (s + 1) * cut],
            same[:, s * cut : (s + 1) * cut],
        )
        for s in range(2)
    ]
    near = swap(sends[0], "rep", 1)
    far = swap(sends[1], "rep", 2)
    near_sib = swap(near, "fsdp", 1)
    far_sib = swap(far, "fsdp", 1)
    return (gathered, near, far, near_sib, far_sib), upper


def local_fast(features, out_grad, conv_weight, conv_bias, norm_gain, norm_shift):
    side = features.shape[1]
    chans = features.shape[3]
    outs = out_grad.shape[3]
    pixels = side * side
    rows = conv_weight.shape[0]
    reps, shards = lax.axis_size("rep"), lax.axis_size("fsdp")
    r, f = lax.axis_index("rep"), lax.axis_index("fsdp")
    z, core = f // 2, f % 2
    extra = rows - chans
    piece = round_up(-(-rows // reps), 16)
    window = round_up(-(-rows // 2), 16)
    x = features.reshape(pixels, chans)
    g = out_grad.reshape(pixels, outs)

    small = gather_small(jnp.stack([norm_gain, norm_shift, conv_bias]), "fsdp")
    vecs = jnp.transpose(small, (1, 0, 2)).reshape(3, chans)
    sib_g = swap(g, "fsdp", 1)
    weights, upper = gather_weight(conv_weight, r, core, window)
    place = jnp.stack([r, z, core, upper]).astype(jnp.int32)

    stat = stats(x)
    own_shifted, bias_sum = shift_grad(g, side)
    sib_shifted, _ = shift_grad(sib_g, side)
    act_shifted, own_t = activate(x, stat, vecs, side)
    sib_t = swap(own_t, "fsdp", 1)

    keep, send0, send1 = weight_pieces(
        place, own_t, sib_t, own_shifted, sib_shifted, side, shards // 2, extra, piece
    )
    got0 = swap(send0, "rep", 1)
    got1 = swap(send1, "rep", 2)
    next0 = (keep[0, :, 1] + got0[:, 1].astype(F32)).astype(BF16)
    next1 = (keep[1, :, 1] + got1[:, 1].astype(F32)).astype(BF16)
    last0 = swap(next0, "rep", 2)
    last1 = swap(next1, "rep", 1)
    sum0 = keep[0, :, 0] + got0[:, 0].astype(F32) + last0.astype(F32)
    sum1 = keep[1, :, 0] + got1[:, 0].astype(F32) + last1.astype(F32)
    sums = [sum0[i] for i in range(sum0.shape[0])] + [sum1[i] for i in range(sum1.shape[0])]
    done = sums[0]
    for m in range(1, shards // 2):
        done = done + swap(sums[m].astype(BF16), "fsdp", 2 * m).astype(F32)
    done = done.astype(BF16)
    pieces = [done] + [swap(done, "rep", m) for m in range(1, reps)]

    in_grad, param_sums = act_grad(place, own_shifted, x, stat, vecs, weights, side)
    conv_out = conv(place, act_shifted, vecs, weights, side)

    scale = 1.0 / math.sqrt(reps * shards * pixels)
    weight_grad = join(place, pieces, rows, scale)
    small_sums = jnp.concatenate([bias_sum, param_sums], axis=0)
    small_sums = sum_all(small_sums, "rep", range(1, reps))
    small_sums = sum_all(small_sums, "fsdp", range(2, shards, 2))
    small_sums = sum_all(small_sums, "fsdp", (1,)) * scale
    share = outs // shards
    mine = lax.dynamic_slice_in_dim(small_sums.reshape(3, shards, share), f, 1, axis=1)
    mine = mine.reshape(3, share)
    return (
        conv_out.reshape(1, side, side, outs),
        in_grad.reshape(1, side, side, chans),
        weight_grad,
        mine[0],
        mine[1],
        mine[2],
    )


def round_up(n, m):
    return -(-n // m) * m


def fits(mesh_shape, images, rows, chans, outs, side):
    reps, shards = mesh_shape["rep"], mesh_shape["fsdp"]
    if images != reps * shards or reps != 2 * 2 or shards != 9 - 1:
        return False
    if chans != outs or rows * shards != 9 * chans or chans % 128 or side % 16:
        return False
    extra, piece, window = rows - chans, round_up(-(-rows // reps), 16), round_up(-(-rows // 2), 16)
    step = (rows - piece) // (reps - 1)
    return (
        extra % 16 == 0
        and step * (reps - 1) == rows - piece
        and step % 16 == 0
        and (rows - window) % 32 == 0
    )


def local(features, out_grad, conv_weight, conv_bias, norm_gain, norm_shift):
    images_here = features.shape[0]
    side_cells = features.shape[1]
    channels = features.shape[3]
    pixels = side_cells * side_cells
    group_size = channels // GROUPS
    full_weight, bias_all, gain_all, shift_all = (
        lax.all_gather(conv_weight, "fsdp", axis=0, tiled=True),
        lax.all_gather(conv_bias, "fsdp", axis=0, tiled=True),
        lax.all_gather(norm_gain, "fsdp", axis=0, tiled=True),
        lax.all_gather(norm_shift, "fsdp", axis=0, tiled=True),
    )
    out_chans = full_weight.shape[1]
    values = features.astype(jnp.float32).reshape(images_here, pixels, GROUPS, group_size)
    group_mean = jnp.mean(values, axis=(1, 3), keepdims=True)
    centered = values - group_mean
    group_var = jnp.mean(centered * centered, axis=(1, 3), keepdims=True)
    inv_std = lax.rsqrt(group_var + epsilon)
    normed = centered * inv_std
    gain_cols = gain_all.astype(jnp.float32).reshape(1, 1, GROUPS, group_size)
    shift_cols = shift_all.astype(jnp.float32).reshape(1, 1, GROUPS, group_size)
    pre_act = normed * gain_cols + shift_cols
    activated = (
        jax.nn.silu(pre_act)
        .astype(jnp.bfloat16)
        .reshape(images_here, side_cells, side_cells, channels)
    )
    padded = jnp.pad(activated, ((0, 0), (1, 1), (1, 1), (0, 0)))
    conv_sum = jnp.zeros((images_here * pixels, out_chans), jnp.float32)
    taps_list = []
    for row_off in range(3):
        for col_off in range(3):
            tap_index = 3 * row_off + col_off
            tap_piece = padded[
                :, row_off : row_off + side_cells, col_off : col_off + side_cells, :
            ].reshape(images_here * pixels, channels)
            taps_list.append(tap_piece)
            conv_sum = conv_sum + jnp.dot(
                tap_piece,
                full_weight[tap_index * channels : (tap_index + 1) * channels],
                preferred_element_type=jnp.float32,
            )
    conv_out = (
        (conv_sum + bias_all.astype(jnp.float32)[None, :])
        .astype(jnp.bfloat16)
        .reshape(images_here, side_cells, side_cells, out_chans)
    )
    back_weight, back_gain = (
        lax.all_gather(conv_weight, "fsdp", axis=0, tiled=True),
        lax.all_gather(norm_gain, "fsdp", axis=0, tiled=True),
    )
    grad_rows = out_grad.reshape(images_here * pixels, out_chans)
    grad_padded = jnp.zeros((images_here, side_cells + 2, side_cells + 2, channels), jnp.float32)
    weight_list = []
    for row_off in range(3):
        for col_off in range(3):
            tap_index = 3 * row_off + col_off
            tap_rows = back_weight[tap_index * channels : (tap_index + 1) * channels]
            tap_grad = lax.dot_general(
                grad_rows, tap_rows, (((1,), (1,)), ((), ())), preferred_element_type=jnp.float32
            )
            grad_padded = grad_padded.at[
                :, row_off : row_off + side_cells, col_off : col_off + side_cells, :
            ].add(tap_grad.reshape(images_here, side_cells, side_cells, channels))
            weight_list.append(
                lax.dot_general(
                    taps_list[tap_index],
                    grad_rows,
                    (((0,), (0,)), ((), ())),
                    preferred_element_type=jnp.float32,
                )
            )
    act_grad = grad_padded[:, 1:-1, 1:-1, :].reshape(images_here, pixels, GROUPS, group_size)
    sig_pre = jax.nn.sigmoid(pre_act)
    pre_grad = act_grad * sig_pre * (1.0 + pre_act * (1.0 - sig_pre))
    norm_grad = pre_grad * back_gain.astype(jnp.float32).reshape(1, 1, GROUPS, group_size)
    grad_mean = jnp.mean(norm_grad, axis=(1, 3), keepdims=True)
    cross_mean = jnp.mean(norm_grad * normed, axis=(1, 3), keepdims=True)
    in_grad = (
        ((norm_grad - grad_mean - normed * cross_mean) * inv_std)
        .astype(jnp.bfloat16)
        .reshape(images_here, side_cells, side_cells, channels)
    )
    rep_size = lax.axis_size("rep")
    fsdp_size = lax.axis_size("fsdp")
    grad_scale = 1.0 / math.sqrt(images_here * rep_size * fsdp_size * pixels)
    weight_term = jnp.concatenate(weight_list, axis=0) * grad_scale
    bias_term = jnp.sum(grad_rows.astype(jnp.float32), axis=0) * grad_scale
    gain_term = jnp.sum(pre_grad * normed, axis=(0, 1)).reshape(channels) * grad_scale
    shift_term = jnp.sum(pre_grad, axis=(0, 1)).reshape(channels) * grad_scale
    shards = (
        lax.psum_scatter(weight_term, "fsdp", scatter_dimension=0, tiled=True),
        lax.psum_scatter(bias_term, "fsdp", scatter_dimension=0, tiled=True),
        lax.psum_scatter(gain_term, "fsdp", scatter_dimension=0, tiled=True),
        lax.psum_scatter(shift_term, "fsdp", scatter_dimension=0, tiled=True),
    )
    weight_grad, bias_grad, gain_grad, shift_grad = lax.psum(
        (shards[0], shards[1], shards[2], shards[3]), "rep"
    )
    return (conv_out, in_grad, weight_grad, bias_grad, gain_grad, shift_grad)


def solution(mesh):
    placed = (
        P(("rep", "fsdp"), None, None, None),
        P(("rep", "fsdp"), None, None, None),
        P("fsdp", None),
        P("fsdp"),
        P("fsdp"),
        P("fsdp"),
    )
    out_placed = (
        P(("rep", "fsdp"), None, None, None),
        P(("rep", "fsdp"), None, None, None),
        P("fsdp", None),
        P("fsdp"),
        P("fsdp"),
        P("fsdp"),
    )

    def run(features, out_grad, conv_weight, *vectors):
        images, side, _, chans = features.shape
        rows, outs = conv_weight.shape
        shape = dict(mesh.shape)
        fast = fits(shape, images, rows // shape["fsdp"], chans, outs, side)
        return jax.shard_map(
            local_fast if fast else local,
            mesh=mesh,
            in_specs=placed,
            out_specs=out_placed,
            check_vma=False,
        )(features, out_grad, conv_weight, *vectors)

    return run
```

```python
import functools
import math

import jax
import jax.numpy as jnp
from jax import lax
from jax.experimental import pallas as pl
from jax.experimental.pallas import tpu as pltpu
from jax.sharding import PartitionSpec as P

GROUPS = 16


epsilon = 1e-05

F32 = jnp.float32
BF16 = jnp.bfloat16
VMEM = pl.BlockSpec(memory_space=pltpu.VMEM)
SMEM = pl.BlockSpec(memory_space=pltpu.SMEM)
ANY = pl.BlockSpec(memory_space=pl.ANY)


def params(mib=24):
    return pltpu.CompilerParams(vmem_limit_bytes=mib * 1024 * 1024)


def call(kernel, operands, in_specs, tokens=(), **options):
    given = len(operands)

    def body(*refs):
        kernel(*refs[:given], *refs[given + len(tokens) :])

    return pl.pallas_call(
        body, in_specs=list(in_specs) + [ANY] * len(tokens), **options
    )(*operands, *tokens)


def struct(shape, dtype):
    return jax.ShapeDtypeStruct(shape, dtype)


def shifted_copies(x, side, out_ref, first):
    pixels = x.shape[0]
    column = lax.broadcasted_iota(jnp.int32, x.shape, 0) % side
    edge = jnp.zeros((side, x.shape[1]), BF16)
    for kx in range(3):
        move = (kx - 1) if first else (1 - kx)
        if move == 0:
            moved = x
        elif move == 1:
            moved = jnp.where(column == side - 1, 0.0, pltpu.roll(x, pixels - 1, 0))
        else:
            moved = jnp.where(column == 0, 0.0, pltpu.roll(x, 1, 0))
        out_ref[kx, 0:side, :] = edge
        out_ref[kx, side : side + pixels, :] = moved.astype(BF16)
        out_ref[kx, side + pixels : 2 * side + pixels, :] = edge


def shift_kernel(side, x_ref, out_ref, sum_ref):
    x = x_ref[...].astype(F32)
    sum_ref[...] = jnp.sum(x, axis=0, keepdims=True)
    shifted_copies(x, side, out_ref, False)


def shift_grad(x, side, tokens):
    pixels, chans = x.shape
    return call(
        functools.partial(shift_kernel, side),
        (x,),
        [VMEM],
        tokens,
        out_shape=(
            struct((3, pixels + 2 * side, chans), BF16),
            struct((1, chans), F32),
        ),
        out_specs=(VMEM, VMEM),
        compiler_params=params(),
        cost_estimate=pl.CostEstimate(
            flops=8 * x.size, bytes_accessed=8 * x.size, transcendentals=0
        ),
        name="shift_grad",
    )


def same_group(chans):
    size = chans // GROUPS
    a = lax.broadcasted_iota(jnp.int32, (chans, chans), 0) // size
    b = lax.broadcasted_iota(jnp.int32, (chans, chans), 1) // size
    return jnp.where(a == b, 1.0, 0.0).astype(F32)


def group_mean_of(column_sum, pixels):
    chans = column_sum.shape[1]
    count = pixels * (chans // GROUPS)
    total = jnp.dot(
        jnp.broadcast_to(column_sum, (8, chans)),
        same_group(chans),
        preferred_element_type=F32,
        precision=lax.Precision.HIGHEST,
    )
    return total[0:1] * (1.0 / count)


def stats_kernel(x_ref, out_ref):
    pixels = x_ref.shape[0]
    x = x_ref[...].astype(F32)
    mean = group_mean_of(jnp.sum(x, axis=0, keepdims=True), pixels)
    centered = x - mean
    var = group_mean_of(jnp.sum(centered * centered, axis=0, keepdims=True), pixels)
    out_ref[0:1, :] = mean
    out_ref[1:2, :] = lax.rsqrt(var + epsilon)


def stats(x):
    return pl.pallas_call(
        stats_kernel,
        out_shape=struct((2, x.shape[1]), F32),
        in_specs=[VMEM],
        out_specs=VMEM,
        compiler_params=params(),
        cost_estimate=pl.CostEstimate(
            flops=5 * x.size, bytes_accessed=2 * x.size, transcendentals=0
        ),
        name="norm_stats",
    )(x)


def activation(x_ref, stat_ref, vec_ref):
    mean, inv = stat_ref[0:1, :], stat_ref[1:2, :]
    gain = vec_ref[0:1, :].astype(F32)
    shift = vec_ref[1:2, :].astype(F32)
    pre = (x_ref[...].astype(F32) - mean) * inv * gain + shift
    return (pre / (1.0 + jnp.exp(-pre))).astype(BF16)


def act_kernel(x_ref, stat_ref, vec_ref, turned_ref):
    turned_ref[...] = activation(x_ref, stat_ref, vec_ref).T


def activate(x, stat, vecs, tokens):
    pixels, chans = x.shape
    return call(
        act_kernel,
        (x, stat, vecs),
        [VMEM, VMEM, VMEM],
        tokens,
        out_shape=struct((chans, pixels), BF16),
        out_specs=VMEM,
        compiler_params=params(),
        cost_estimate=pl.CostEstimate(
            flops=10 * x.size, bytes_accessed=4 * x.size, transcendentals=2 * x.size
        ),
        name="activate",
    )


def weight_blocks(side, extra, blocks, core, own_t, sib_t, own_g, sib_g, first, count, block_ref):
    chans, pixels = own_t.shape

    def tap_rows(ref, tap):
        start = pl.multiple_of((2 - tap // 3) * side, side)
        return ref[tap % 3, pl.ds(start, pixels), first : first + count]

    def product(low, high, tap):
        return jnp.dot(
            own_t[low:high, :], tap_rows(own_g, tap), preferred_element_type=F32
        ) + jnp.dot(sib_t[low:high, :], tap_rows(sib_g, tap), preferred_element_type=F32)

    for k in range(blocks):
        low, high = 2 * extra * k, 2 * extra * (k + 1)
        block_ref[0 : chans - low, :] = product(low, chans, 2 * k + core)
        block_ref[chans - low : chans + 2 * extra, :] = product(0, high, 2 * k + 1 + core)
        yield k


def weight_by_rep_kernel(
    side, extra, first, piece, place_ref, own_t, sib_t, own_g, sib_g,
    keep_ref, send0_ref, send1_ref, block_ref,
):
    chans = own_t.shape[0]
    r, z, core = place_ref[0], place_ref[1], place_ref[2]
    half, count = keep_ref.shape[2], keep_ref.shape[4]
    reps = 2 * keep_ref.shape[1]
    step = (chans + extra - piece) // (reps - 1)

    def rows_of(rel):
        at = pl.multiple_of(extra * core + step * (r ^ rel), 16)
        return block_ref[pl.ds(at, piece), :]

    for k in weight_blocks(
        side, extra, 2 * half, core, own_t, sib_t, own_g, sib_g, first, count, block_ref
    ):
        rel_z = k ^ z
        path, slot = rel_z // half, rel_z % half
        keep_ref[path, 0, slot] = rows_of(0)

        @pl.when(path == 0)
        def _():
            send0_ref[0, slot] = rows_of(1).astype(BF16)
            keep_ref[0, 1, slot] = rows_of(2)
            send0_ref[1, slot] = rows_of(3).astype(BF16)

        @pl.when(path == 1)
        def _():
            send1_ref[0, slot] = rows_of(2).astype(BF16)
            keep_ref[1, 1, slot] = rows_of(1)
            send1_ref[1, slot] = rows_of(3).astype(BF16)


def weight_call(kernel, out_shape, place, operands, extra, first, count, blocks, tokens, name):
    chans, pixels = operands[0].shape
    return call(
        kernel,
        (place,) + operands,
        [SMEM, VMEM, VMEM, VMEM, VMEM],
        tokens,
        out_shape=out_shape,
        out_specs=(VMEM,) * len(out_shape),
        scratch_shapes=[pltpu.VMEM((chans + 2 * extra, count), F32)],
        compiler_params=params(28),
        cost_estimate=pl.CostEstimate(
            flops=4 * blocks * (chans + 2 * extra) * pixels * count,
            bytes_accessed=20 * chans * pixels,
            transcendentals=0,
        ),
        name=name,
    )


def weight_by_rep(place, operands, side, blocks, extra, piece, first, count, tokens):
    half = blocks // 2
    out_shape = (
        struct((2, 2, half, piece, count), F32),
        struct((2, half, piece, count), BF16),
        struct((2, half, piece, count), BF16),
    )
    kernel = functools.partial(weight_by_rep_kernel, side, extra, first, piece)
    return weight_call(
        kernel, out_shape, place, operands, extra, first, count, blocks, tokens, "weight_grad_rep"
    )


def finish_kernel(*refs):
    total = refs[0][...]
    for ref in refs[1:-1]:
        total = total + ref[...].astype(F32)
    refs[-1][...] = total.astype(BF16)


def finish(terms, tokens):
    return call(
        finish_kernel,
        terms,
        [VMEM] * len(terms),
        tokens,
        out_shape=struct(terms[0].shape, BF16),
        out_specs=VMEM,
        compiler_params=params(8),
        cost_estimate=pl.CostEstimate(
            flops=4 * terms[0].size, bytes_accessed=12 * terms[0].size, transcendentals=0
        ),
        name="finish_sum",
    )


def rep_step_kernel(keep_ref, got0, got1, next0, next1):
    next0[...] = (keep_ref[0, 1] + got0[1].astype(F32)).astype(BF16)
    next1[...] = (keep_ref[1, 1] + got1[1].astype(F32)).astype(BF16)


def rep_step(keep, got0, got1, tokens):
    out = struct(keep.shape[2:], BF16)
    return call(
        rep_step_kernel,
        (keep, got0, got1),
        [VMEM] * 3,
        tokens,
        out_shape=(out, out),
        out_specs=(VMEM, VMEM),
        compiler_params=params(12),
        cost_estimate=pl.CostEstimate(
            flops=keep.size, bytes_accessed=4 * keep.size, transcendentals=0
        ),
        name="rep_step",
    )


def rep_sum_kernel(keep_ref, got0, got1, last0, last1, own_ref, *sends):
    half = keep_ref.shape[2]
    for i, out in enumerate((own_ref,) + sends):
        path, slot = i // half, i % half
        got, last = ((got0, last0), (got1, last1))[path]
        total = keep_ref[path, 0, slot] + got[0, slot].astype(F32) + last[slot].astype(F32)
        out[...] = total.astype(out.dtype)


def rep_sum(keep, got0, got1, last0, last1, tokens):
    half, piece, count = keep.shape[2:]
    return call(
        rep_sum_kernel,
        (keep, got0, got1, last0, last1),
        [VMEM] * 5,
        tokens,
        out_shape=(struct((piece, count), F32),)
        + (struct((piece, count), BF16),) * (2 * half - 1),
        out_specs=(VMEM,) * (2 * half),
        compiler_params=params(12),
        cost_estimate=pl.CostEstimate(
            flops=keep.size, bytes_accessed=4 * keep.size, transcendentals=0
        ),
        name="rep_sum",
    )


def prepare_kernel(side, x_ref, stat_ref, vec_ref, shifted_ref, slope_ref):
    mean, inv = stat_ref[0:1, :], stat_ref[1:2, :]
    gain = vec_ref[0:1, :].astype(F32)
    shift = vec_ref[1:2, :].astype(F32)
    pre = (x_ref[...].astype(F32) - mean) * inv * gain + shift
    grown = 1.0 + jnp.exp(-pre)
    shifted_copies((pre / grown).astype(BF16).astype(F32), side, shifted_ref, True)
    sig = 1.0 / grown
    slope_ref[...] = sig * (1.0 + pre * (1.0 - sig))


def prepare(x, stat, vecs, side, tokens):
    pixels, chans = x.shape
    return call(
        functools.partial(prepare_kernel, side),
        (x, stat, vecs),
        [VMEM] * 3,
        tokens,
        out_shape=(
            struct((3, pixels + 2 * side, chans), BF16),
            struct((pixels, chans), F32),
        ),
        out_specs=(VMEM, VMEM),
        compiler_params=params(16),
        cost_estimate=pl.CostEstimate(
            flops=20 * x.size, bytes_accessed=12 * x.size, transcendentals=2 * x.size
        ),
        name="prepare",
    )


def grad_kernel(
    side, chunk, g_ref, x_ref, slope_ref, stat_ref, vec_ref, weight, out_ref, sum_ref, scaled
):
    pixels, chans = x_ref.shape
    mean, inv = stat_ref[0:1, :], stat_ref[1:2, :]
    gain = vec_ref[0:1, :].astype(F32)
    sum_ref[...] = jnp.zeros_like(sum_ref)

    @pl.loop(0, pixels // chunk)
    def _(i):
        total = None
        for tap in range(9):
            start = pl.multiple_of(i * chunk + (2 - tap // 3) * side, side)
            part = lax.dot_general(
                g_ref[tap % 3, pl.ds(start, chunk), :],
                weight[tap * chans : (tap + 1) * chans, :],
                (((1,), (1,)), ((), ())),
                preferred_element_type=F32,
            )
            total = part if total is None else total + part
        rows = pl.ds(pl.multiple_of(i * chunk, chunk), chunk)
        normed = (x_ref[rows, :].astype(F32) - mean) * inv
        pre_grad = total * slope_ref[rows, :]
        sum_ref[0:1, :] += jnp.sum(pre_grad * normed, axis=0, keepdims=True)
        sum_ref[1:2, :] += jnp.sum(pre_grad, axis=0, keepdims=True)
        scaled[rows, :] = pre_grad * gain

    cross = group_mean_of(sum_ref[0:1, :] * gain, pixels)
    center = group_mean_of(sum_ref[1:2, :] * gain, pixels)

    @pl.loop(0, pixels // chunk)
    def _(i):
        rows = pl.ds(pl.multiple_of(i * chunk, chunk), chunk)
        normed = (x_ref[rows, :].astype(F32) - mean) * inv
        out_ref[rows, :] = ((scaled[rows, :] - center - normed * cross) * inv).astype(BF16)


def act_grad(shifted, x, slope, stat, vecs, weight, side, tokens):
    pixels, chans = x.shape
    outs = shifted.shape[2]
    return call(
        functools.partial(grad_kernel, side, 256),
        (shifted, x, slope, stat, vecs, weight),
        [VMEM] * 6,
        tokens,
        out_shape=(struct((pixels, chans), BF16), struct((2, chans), F32)),
        out_specs=(VMEM, VMEM),
        scratch_shapes=[pltpu.VMEM((pixels, chans), F32)],
        compiler_params=params(16),
        cost_estimate=pl.CostEstimate(
            flops=18 * chans * outs * pixels,
            bytes_accessed=18 * chans * outs + 12 * pixels * chans,
            transcendentals=0,
        ),
        name="act_grad",
    )


def conv_kernel(side, chunk, first, a_ref, vec_ref, weight, *rest):
    out_ref, token_ref, held, sems = rest[-4:]
    token_ref[...] = jnp.zeros_like(token_ref)
    chans = a_ref.shape[2]
    bias = vec_ref[2:3, :].astype(F32)
    chunks = held.shape[0] // chunk

    def copy(i):
        rows = pl.ds(pl.multiple_of(i * chunk, chunk), chunk)
        at = pl.ds(pl.multiple_of(first + i * chunk, chunk), chunk)
        return pltpu.make_async_copy(held.at[rows, :], out_ref.at[at, :], sems.at[i])

    for i in range(chunks):
        total = None
        for tap in range(9):
            start = first + i * chunk + (tap // 3) * side
            part = jnp.dot(
                a_ref[tap % 3, start : start + chunk, :],
                weight[tap * chans : (tap + 1) * chans, :],
                preferred_element_type=F32,
            )
            total = part if total is None else total + part
        held[i * chunk : (i + 1) * chunk, :] = (total + bias).astype(BF16)
        copy(i).start()
    for i in range(chunks):
        copy(i).wait()


def conv(shifted, vecs, weight, side, first, count, before, tokens):
    chans = shifted.shape[2]
    pixels = shifted.shape[1] - 2 * side
    outs = weight.shape[1]
    chunk = 256
    operands = (shifted, vecs, weight) + (() if before is None else (before,))
    return call(
        functools.partial(conv_kernel, side, chunk, first),
        operands,
        [VMEM] * 3 + [ANY] * (len(operands) - 3),
        tokens,
        out_shape=(struct((pixels, outs), BF16), struct((1, 128), F32)),
        out_specs=(ANY, VMEM),
        input_output_aliases={} if before is None else {3: 0},
        scratch_shapes=[
            pltpu.VMEM((count, outs), BF16),
            pltpu.SemaphoreType.DMA((count // chunk,)),
        ],
        compiler_params=params(16),
        cost_estimate=pl.CostEstimate(
            flops=18 * chans * outs * count,
            bytes_accessed=18 * chans * outs + 4 * count * chans,
            transcendentals=0,
        ),
        name="conv_forward",
    )


def join_kernel(scale, place_ref, p0, p1, p2, p3, out_ref):
    r = place_ref[0]
    pieces = (p0, p1, p2, p3)
    piece = p0.shape[0]
    step = (out_ref.shape[0] - piece) // (len(pieces) - 1)
    for q in range(len(pieces)):
        for rel, ref in enumerate(pieces):

            @pl.when((q ^ r) == rel)
            def _():
                out_ref[step * q : step * q + piece, :] = ref[...].astype(F32) * scale


def join(place, pieces, rows, scale, tokens):
    outs = pieces[0].shape[1]
    return call(
        functools.partial(join_kernel, scale),
        (place, *pieces),
        [SMEM] + [VMEM] * 4,
        tokens,
        out_shape=struct((rows, outs), F32),
        out_specs=VMEM,
        compiler_params=params(),
        cost_estimate=pl.CostEstimate(
            flops=rows * outs, bytes_accessed=6 * rows * outs, transcendentals=0
        ),
        name="join_pieces",
    )


def tree_sum(terms):
    while len(terms) > 1:
        terms = [terms[i] + terms[i + 1] for i in range(0, len(terms), 2)]
    return terms[0]


def add_kernel(*refs):
    refs[-1][...] = tree_sum([ref[...] for ref in refs[:-1]])


def add_small(terms, tokens):
    return call(
        add_kernel,
        terms,
        [VMEM] * len(terms),
        tokens,
        out_shape=struct(terms[0].shape, F32),
        out_specs=VMEM,
        compiler_params=params(2),
        cost_estimate=pl.CostEstimate(
            flops=4 * terms[0].size, bytes_accessed=16 * terms[0].size, transcendentals=0
        ),
        name="add_small",
    )


def swap(x, axis, mask):
    n = lax.axis_size(axis)
    return lax.ppermute(x, axis, [(i, i ^ mask) for i in range(n)])


def gather_small(x):
    at = lax.axis_index("fsdp")
    other = swap(x, "fsdp", 1)
    pair = jnp.where(at % 2 == 1, jnp.stack([other, x]), jnp.stack([x, other]))
    got = [pair] + [swap(pair, "fsdp", m) for m in range(2, lax.axis_size("fsdp"), 2)]
    mask = 1
    while mask < len(got):
        flip = (at // (2 * mask)) % 2 == 1
        got = [jnp.where(flip, got[i ^ mask], got[i]) for i in range(len(got))]
        mask *= 2
    return jnp.concatenate(got)


def sum_all(x, axis, masks):
    return tree_sum([x] + [swap(x, axis, m) for m in masks])


def local_fast(features, out_grad, conv_weight, conv_bias, norm_gain, norm_shift):
    side = features.shape[1]
    chans = features.shape[3]
    outs = out_grad.shape[3]
    pixels = side * side
    rows = conv_weight.shape[0]
    reps, shards = lax.axis_size("rep"), lax.axis_size("fsdp")
    r, f = lax.axis_index("rep"), lax.axis_index("fsdp")
    z, core = f // 2, f % 2
    extra = rows - chans
    piece = round_up(-(-rows // reps), 16)
    x = features.reshape(pixels, chans)
    g = out_grad.reshape(pixels, outs)
    place = jnp.stack([r, z, core]).astype(jnp.int32)

    weight = lax.all_gather(conv_weight, "fsdp", axis=0, tiled=True)
    small = gather_small(jnp.stack([norm_gain, norm_shift, conv_bias]))
    sib_g = swap(g, "fsdp", 1)

    stat = stats(x)
    vecs = jnp.transpose(small, (1, 0, 2)).reshape(3, chans)
    own_t = activate(x, stat, vecs, ())
    sib_t = swap(own_t, "fsdp", 1)
    own_shifted, bias_sum = shift_grad(g, side, (own_t,))
    sib_shifted, _ = shift_grad(sib_g, side, (own_t,))
    operands = (own_t, sib_t, own_shifted, sib_shifted)

    keep, send0, send1 = weight_by_rep(
        place, operands, side, shards // 2, extra, piece, 0, outs, ()
    )
    got0 = swap(send0, "rep", 1)
    got1 = swap(send1, "rep", 2)
    next0, next1 = rep_step(keep, got0, got1, ())
    last0 = swap(next0, "rep", 2)
    last1 = swap(next1, "rep", 1)
    own_sum, *sends = rep_sum(keep, got0, got1, last0, last1, ())
    got = [swap(a, "fsdp", 2 * (m + 1)) for m, a in enumerate(sends)]
    act_shifted, slope = prepare(x, stat, vecs, side, (keep,))
    in_grad, param_sums = act_grad(
        own_shifted, x, slope, stat, vecs, weight, side, (own_sum,)
    )
    done = finish((own_sum, *got), (param_sums,))
    pieces_done = [done] + [swap(done, "rep", m) for m in range(1, reps)]
    small_sums = jnp.concatenate([bias_sum, param_sums], axis=0)
    over_rep = [small_sums] + [swap(small_sums, "rep", m) for m in range(1, reps)]

    half = pixels // 2
    conv_out, token = conv(act_shifted, vecs, weight, side, 0, half, None, (done,))
    small_sums = add_small(over_rep, (token,))
    over_z = [small_sums] + [swap(small_sums, "fsdp", m) for m in range(2, shards, 2)]
    conv_out, token = conv(act_shifted, vecs, weight, side, half, half, conv_out, (small_sums,))
    small_sums = add_small(over_z, (token, *pieces_done[1:]))
    scale = 1.0 / math.sqrt(reps * shards * pixels)
    small_sums = sum_all(small_sums, "fsdp", (1,)) * scale
    weight_grad = join(place, pieces_done, rows, scale, (token,))
    share = outs // shards
    mine = lax.dynamic_slice_in_dim(small_sums.reshape(3, shards, share), f, 1, axis=1)
    mine = mine.reshape(3, share)
    return (
        conv_out.reshape(1, side, side, outs),
        in_grad.reshape(1, side, side, chans),
        weight_grad,
        mine[0],
        mine[1],
        mine[2],
    )


def round_up(n, m):
    return -(-n // m) * m


def fits(mesh_shape, images, rows, chans, outs, side):
    reps, shards = mesh_shape["rep"], mesh_shape["fsdp"]
    if images != reps * shards or reps != 2 * 2 or shards != 9 - 1:
        return False
    if chans != outs or rows * shards != 9 * chans or chans % 128 or side % 16 or outs < 3 * 128:
        return False
    extra, piece = rows - chans, round_up(-(-rows // reps), 16)
    step = (rows - piece) // (reps - 1)
    return (
        extra % 16 == 0
        and step * (reps - 1) == rows - piece
        and step % 16 == 0
        and piece % 32 == 0
    )


def local(features, out_grad, conv_weight, conv_bias, norm_gain, norm_shift):
    images_here = features.shape[0]
    side_cells = features.shape[1]
    channels = features.shape[3]
    pixels = side_cells * side_cells
    group_size = channels // GROUPS
    full_weight, bias_all, gain_all, shift_all = (
        lax.all_gather(conv_weight, "fsdp", axis=0, tiled=True),
        lax.all_gather(conv_bias, "fsdp", axis=0, tiled=True),
        lax.all_gather(norm_gain, "fsdp", axis=0, tiled=True),
        lax.all_gather(norm_shift, "fsdp", axis=0, tiled=True),
    )
    out_chans = full_weight.shape[1]
    values = features.astype(jnp.float32).reshape(images_here, pixels, GROUPS, group_size)
    group_mean = jnp.mean(values, axis=(1, 3), keepdims=True)
    centered = values - group_mean
    group_var = jnp.mean(centered * centered, axis=(1, 3), keepdims=True)
    inv_std = lax.rsqrt(group_var + epsilon)
    normed = centered * inv_std
    gain_cols = gain_all.astype(jnp.float32).reshape(1, 1, GROUPS, group_size)
    shift_cols = shift_all.astype(jnp.float32).reshape(1, 1, GROUPS, group_size)
    pre_act = normed * gain_cols + shift_cols
    activated = (
        jax.nn.silu(pre_act)
        .astype(jnp.bfloat16)
        .reshape(images_here, side_cells, side_cells, channels)
    )
    padded = jnp.pad(activated, ((0, 0), (1, 1), (1, 1), (0, 0)))
    conv_sum = jnp.zeros((images_here * pixels, out_chans), jnp.float32)
    taps_list = []
    for row_off in range(3):
        for col_off in range(3):
            tap_index = 3 * row_off + col_off
            tap_piece = padded[
                :, row_off : row_off + side_cells, col_off : col_off + side_cells, :
            ].reshape(images_here * pixels, channels)
            taps_list.append(tap_piece)
            conv_sum = conv_sum + jnp.dot(
                tap_piece,
                full_weight[tap_index * channels : (tap_index + 1) * channels],
                preferred_element_type=jnp.float32,
            )
    conv_out = (
        (conv_sum + bias_all.astype(jnp.float32)[None, :])
        .astype(jnp.bfloat16)
        .reshape(images_here, side_cells, side_cells, out_chans)
    )
    back_weight, back_gain = (
        lax.all_gather(conv_weight, "fsdp", axis=0, tiled=True),
        lax.all_gather(norm_gain, "fsdp", axis=0, tiled=True),
    )
    grad_rows = out_grad.reshape(images_here * pixels, out_chans)
    grad_padded = jnp.zeros((images_here, side_cells + 2, side_cells + 2, channels), jnp.float32)
    weight_list = []
    for row_off in range(3):
        for col_off in range(3):
            tap_index = 3 * row_off + col_off
            tap_rows = back_weight[tap_index * channels : (tap_index + 1) * channels]
            tap_grad = lax.dot_general(
                grad_rows, tap_rows, (((1,), (1,)), ((), ())), preferred_element_type=jnp.float32
            )
            grad_padded = grad_padded.at[
                :, row_off : row_off + side_cells, col_off : col_off + side_cells, :
            ].add(tap_grad.reshape(images_here, side_cells, side_cells, channels))
            weight_list.append(
                lax.dot_general(
                    taps_list[tap_index],
                    grad_rows,
                    (((0,), (0,)), ((), ())),
                    preferred_element_type=jnp.float32,
                )
            )
    act_grad = grad_padded[:, 1:-1, 1:-1, :].reshape(images_here, pixels, GROUPS, group_size)
    sig_pre = jax.nn.sigmoid(pre_act)
    pre_grad = act_grad * sig_pre * (1.0 + pre_act * (1.0 - sig_pre))
    norm_grad = pre_grad * back_gain.astype(jnp.float32).reshape(1, 1, GROUPS, group_size)
    grad_mean = jnp.mean(norm_grad, axis=(1, 3), keepdims=True)
    cross_mean = jnp.mean(norm_grad * normed, axis=(1, 3), keepdims=True)
    in_grad = (
        ((norm_grad - grad_mean - normed * cross_mean) * inv_std)
        .astype(jnp.bfloat16)
        .reshape(images_here, side_cells, side_cells, channels)
    )
    rep_size = lax.axis_size("rep")
    fsdp_size = lax.axis_size("fsdp")
    grad_scale = 1.0 / math.sqrt(images_here * rep_size * fsdp_size * pixels)
    weight_term = jnp.concatenate(weight_list, axis=0) * grad_scale
    bias_term = jnp.sum(grad_rows.astype(jnp.float32), axis=0) * grad_scale
    gain_term = jnp.sum(pre_grad * normed, axis=(0, 1)).reshape(channels) * grad_scale
    shift_term = jnp.sum(pre_grad, axis=(0, 1)).reshape(channels) * grad_scale
    shards = (
        lax.psum_scatter(weight_term, "fsdp", scatter_dimension=0, tiled=True),
        lax.psum_scatter(bias_term, "fsdp", scatter_dimension=0, tiled=True),
        lax.psum_scatter(gain_term, "fsdp", scatter_dimension=0, tiled=True),
        lax.psum_scatter(shift_term, "fsdp", scatter_dimension=0, tiled=True),
    )
    weight_grad, bias_grad, gain_grad, shift_grad = lax.psum(
        (shards[0], shards[1], shards[2], shards[3]), "rep"
    )
    return (conv_out, in_grad, weight_grad, bias_grad, gain_grad, shift_grad)


def solution(mesh):
    placed = (
        P(("rep", "fsdp"), None, None, None),
        P(("rep", "fsdp"), None, None, None),
        P("fsdp", None),
        P("fsdp"),
        P("fsdp"),
        P("fsdp"),
    )
    out_placed = (
        P(("rep", "fsdp"), None, None, None),
        P(("rep", "fsdp"), None, None, None),
        P("fsdp", None),
        P("fsdp"),
        P("fsdp"),
        P("fsdp"),
    )

    def run(features, out_grad, conv_weight, *vectors):
        images, side, _, chans = features.shape
        rows, outs = conv_weight.shape
        shape = dict(mesh.shape)
        fast = fits(shape, images, rows // shape["fsdp"], chans, outs, side)
        return jax.shard_map(
            local_fast if fast else local,
            mesh=mesh,
            in_specs=placed,
            out_specs=out_placed,
            check_vma=False,
        )(features, out_grad, conv_weight, *vectors)

    return run
```

```python
import functools
import math

import jax
import jax.numpy as jnp
from jax import lax
from jax.experimental import pallas as pl
from jax.experimental.pallas import tpu as pltpu
from jax.sharding import PartitionSpec as P

GROUPS = 16


epsilon = 1e-05

F32 = jnp.float32
BF16 = jnp.bfloat16
VMEM = pl.BlockSpec(memory_space=pltpu.VMEM)
SMEM = pl.BlockSpec(memory_space=pltpu.SMEM)
ANY = pl.BlockSpec(memory_space=pl.ANY)


def params(mib=24):
    return pltpu.CompilerParams(vmem_limit_bytes=mib * 1024 * 1024)


def call(kernel, operands, in_specs, tokens=(), **options):
    given = len(operands)

    def body(*refs):
        kernel(*refs[:given], *refs[given + len(tokens) :])

    return pl.pallas_call(
        body, in_specs=list(in_specs) + [ANY] * len(tokens), **options
    )(*operands, *tokens)


def struct(shape, dtype):
    return jax.ShapeDtypeStruct(shape, dtype)


def shifted_copies(x, side, out_ref, first):
    pixels = x.shape[0]
    column = lax.broadcasted_iota(jnp.int32, x.shape, 0) % side
    edge = jnp.zeros((side, x.shape[1]), BF16)
    for kx in range(3):
        move = (kx - 1) if first else (1 - kx)
        if move == 0:
            moved = x
        elif move == 1:
            moved = jnp.where(column == side - 1, 0.0, pltpu.roll(x, pixels - 1, 0))
        else:
            moved = jnp.where(column == 0, 0.0, pltpu.roll(x, 1, 0))
        out_ref[kx, 0:side, :] = edge
        out_ref[kx, side : side + pixels, :] = moved.astype(BF16)
        out_ref[kx, side + pixels : 2 * side + pixels, :] = edge


def shift_kernel(side, x_ref, out_ref, sum_ref):
    x = x_ref[...].astype(F32)
    sum_ref[...] = jnp.sum(x, axis=0, keepdims=True)
    shifted_copies(x, side, out_ref, False)


def shift_grad(x, side, tokens):
    pixels, chans = x.shape
    return call(
        functools.partial(shift_kernel, side),
        (x,),
        [VMEM],
        tokens,
        out_shape=(
            struct((3, pixels + 2 * side, chans), BF16),
            struct((1, chans), F32),
        ),
        out_specs=(VMEM, VMEM),
        compiler_params=params(),
        cost_estimate=pl.CostEstimate(
            flops=8 * x.size, bytes_accessed=8 * x.size, transcendentals=0
        ),
        name="shift_grad",
    )


def same_group(chans):
    size = chans // GROUPS
    a = lax.broadcasted_iota(jnp.int32, (chans, chans), 0) // size
    b = lax.broadcasted_iota(jnp.int32, (chans, chans), 1) // size
    return jnp.where(a == b, 1.0, 0.0).astype(F32)


def group_mean_of(column_sum, pixels):
    chans = column_sum.shape[1]
    count = pixels * (chans // GROUPS)
    total = jnp.dot(
        jnp.broadcast_to(column_sum, (8, chans)),
        same_group(chans),
        preferred_element_type=F32,
        precision=lax.Precision.HIGHEST,
    )
    return total[0:1] * (1.0 / count)


def stats_kernel(x_ref, out_ref):
    pixels = x_ref.shape[0]
    x = x_ref[...].astype(F32)
    mean = group_mean_of(jnp.sum(x, axis=0, keepdims=True), pixels)
    centered = x - mean
    var = group_mean_of(jnp.sum(centered * centered, axis=0, keepdims=True), pixels)
    out_ref[0:1, :] = mean
    out_ref[1:2, :] = lax.rsqrt(var + epsilon)


def stats(x):
    return pl.pallas_call(
        stats_kernel,
        out_shape=struct((2, x.shape[1]), F32),
        in_specs=[VMEM],
        out_specs=VMEM,
        compiler_params=params(),
        cost_estimate=pl.CostEstimate(
            flops=5 * x.size, bytes_accessed=2 * x.size, transcendentals=0
        ),
        name="norm_stats",
    )(x)


def activation(x_ref, stat_ref, vec_ref):
    mean, inv = stat_ref[0:1, :], stat_ref[1:2, :]
    gain = vec_ref[0:1, :].astype(F32)
    shift = vec_ref[1:2, :].astype(F32)
    pre = (x_ref[...].astype(F32) - mean) * inv * gain + shift
    return (pre / (1.0 + jnp.exp(-pre))).astype(BF16)


def act_kernel(x_ref, stat_ref, vec_ref, turned_ref):
    turned_ref[...] = activation(x_ref, stat_ref, vec_ref).T


def activate(x, stat, vecs, tokens):
    pixels, chans = x.shape
    return call(
        act_kernel,
        (x, stat, vecs),
        [VMEM, VMEM, VMEM],
        tokens,
        out_shape=struct((chans, pixels), BF16),
        out_specs=VMEM,
        compiler_params=params(),
        cost_estimate=pl.CostEstimate(
            flops=10 * x.size, bytes_accessed=4 * x.size, transcendentals=2 * x.size
        ),
        name="activate",
    )


def weight_blocks(side, extra, blocks, core, own_t, sib_t, own_g, sib_g, first, count, block_ref):
    chans, pixels = own_t.shape

    def tap_rows(ref, tap):
        start = pl.multiple_of((2 - tap // 3) * side, side)
        return ref[tap % 3, pl.ds(start, pixels), first : first + count]

    def product(low, high, tap):
        return jnp.dot(
            own_t[low:high, :], tap_rows(own_g, tap), preferred_element_type=F32
        ) + jnp.dot(sib_t[low:high, :], tap_rows(sib_g, tap), preferred_element_type=F32)

    for k in range(blocks):
        low, high = 2 * extra * k, 2 * extra * (k + 1)
        block_ref[0 : chans - low, :] = product(low, chans, 2 * k + core)
        block_ref[chans - low : chans + 2 * extra, :] = product(0, high, 2 * k + 1 + core)
        yield k


def weight_by_rep_kernel(
    side, extra, first, piece, place_ref, own_t, sib_t, own_g, sib_g,
    keep_ref, send0_ref, send1_ref, block_ref,
):
    chans = own_t.shape[0]
    r, z, core = place_ref[0], place_ref[1], place_ref[2]
    half, count = keep_ref.shape[2], keep_ref.shape[4]
    reps = 2 * keep_ref.shape[1]
    step = (chans + extra - piece) // (reps - 1)

    def rows_of(rel):
        at = pl.multiple_of(extra * core + step * (r ^ rel), 16)
        return block_ref[pl.ds(at, piece), :]

    for k in weight_blocks(
        side, extra, 2 * half, core, own_t, sib_t, own_g, sib_g, first, count, block_ref
    ):
        rel_z = k ^ z
        path, slot = rel_z // half, rel_z % half
        keep_ref[path, 0, slot] = rows_of(0)

        @pl.when(path == 0)
        def _():
            send0_ref[0, slot] = rows_of(1).astype(BF16)
            keep_ref[0, 1, slot] = rows_of(2)
            send0_ref[1, slot] = rows_of(3).astype(BF16)

        @pl.when(path == 1)
        def _():
            send1_ref[0, slot] = rows_of(2).astype(BF16)
            keep_ref[1, 1, slot] = rows_of(1)
            send1_ref[1, slot] = rows_of(3).astype(BF16)


def weight_call(kernel, out_shape, place, operands, extra, first, count, blocks, tokens, name):
    chans, pixels = operands[0].shape
    return call(
        kernel,
        (place,) + operands,
        [SMEM, VMEM, VMEM, VMEM, VMEM],
        tokens,
        out_shape=out_shape,
        out_specs=(VMEM,) * len(out_shape),
        scratch_shapes=[pltpu.VMEM((chans + 2 * extra, count), F32)],
        compiler_params=params(28),
        cost_estimate=pl.CostEstimate(
            flops=4 * blocks * (chans + 2 * extra) * pixels * count,
            bytes_accessed=20 * chans * pixels,
            transcendentals=0,
        ),
        name=name,
    )


def weight_by_rep(place, operands, side, blocks, extra, piece, first, count, tokens):
    half = blocks // 2
    out_shape = (
        struct((2, 2, half, piece, count), F32),
        struct((2, half, piece, count), BF16),
        struct((2, half, piece, count), BF16),
    )
    kernel = functools.partial(weight_by_rep_kernel, side, extra, first, piece)
    return weight_call(
        kernel, out_shape, place, operands, extra, first, count, blocks, tokens, "weight_grad_rep"
    )


def finish_kernel(bias_ref, param_ref, *refs):
    out_ref = refs[-1]
    total = refs[0][...]
    for ref in refs[1:-1]:
        total = total + ref[...].astype(F32)
    piece = total.shape[0]
    out_ref[0:piece, :] = total.astype(BF16)
    small = jnp.concatenate([bias_ref[...], param_ref[...]], axis=0)
    high = small.astype(BF16).astype(F32)
    middle = (small - high).astype(BF16).astype(F32)
    parts = [high, middle, small - high - middle]
    spare = out_ref.shape[0] - piece - 3 * small.shape[0]
    parts.append(jnp.zeros((spare, small.shape[1]), F32))
    out_ref[piece:, :] = jnp.concatenate(parts, axis=0).astype(BF16)


def finish(terms, small):
    piece, outs = terms[0].shape
    return call(
        finish_kernel,
        (*small, *terms),
        [VMEM] * (2 + len(terms)),
        out_shape=struct((piece + 16, outs), BF16),
        out_specs=VMEM,
        compiler_params=params(8),
        cost_estimate=pl.CostEstimate(
            flops=4 * terms[0].size, bytes_accessed=12 * terms[0].size, transcendentals=0
        ),
        name="finish_sum",
    )


def add_small_kernel(piece, *refs):
    out_ref = refs[-1]
    count = out_ref.shape[0]
    terms = []
    for ref in refs[:-1]:
        rows = ref[piece:, :].astype(F32)
        terms.append(rows[0:count] + rows[count : 2 * count] + rows[2 * count : 3 * count])
    out_ref[...] = tree_sum(terms)


def add_small_of(pieces, piece, count, tokens):
    return call(
        functools.partial(add_small_kernel, piece),
        pieces,
        [VMEM] * len(pieces),
        tokens,
        out_shape=struct((count, pieces[0].shape[1]), F32),
        out_specs=VMEM,
        compiler_params=params(4),
        cost_estimate=pl.CostEstimate(
            flops=4 * pieces[0].size, bytes_accessed=4 * pieces[0].size, transcendentals=0
        ),
        name="add_small_of",
    )


def rep_step_kernel(keep_ref, got0, got1, next0, next1):
    next0[...] = (keep_ref[0, 1] + got0[1].astype(F32)).astype(BF16)
    next1[...] = (keep_ref[1, 1] + got1[1].astype(F32)).astype(BF16)


def rep_step(keep, got0, got1, tokens):
    out = struct(keep.shape[2:], BF16)
    return call(
        rep_step_kernel,
        (keep, got0, got1),
        [VMEM] * 3,
        tokens,
        out_shape=(out, out),
        out_specs=(VMEM, VMEM),
        compiler_params=params(12),
        cost_estimate=pl.CostEstimate(
            flops=keep.size, bytes_accessed=4 * keep.size, transcendentals=0
        ),
        name="rep_step",
    )


def rep_sum_kernel(keep_ref, got0, got1, last0, last1, own_ref, *sends):
    half = keep_ref.shape[2]
    for i, out in enumerate((own_ref,) + sends):
        path, slot = i // half, i % half
        got, last = ((got0, last0), (got1, last1))[path]
        total = keep_ref[path, 0, slot] + got[0, slot].astype(F32) + last[slot].astype(F32)
        out[...] = total.astype(out.dtype)


def rep_sum(keep, got0, got1, last0, last1, tokens):
    half, piece, count = keep.shape[2:]
    return call(
        rep_sum_kernel,
        (keep, got0, got1, last0, last1),
        [VMEM] * 5,
        tokens,
        out_shape=(struct((piece, count), F32),)
        + (struct((piece, count), BF16),) * (2 * half - 1),
        out_specs=(VMEM,) * (2 * half),
        compiler_params=params(12),
        cost_estimate=pl.CostEstimate(
            flops=keep.size, bytes_accessed=4 * keep.size, transcendentals=0
        ),
        name="rep_sum",
    )


def prepare_kernel(side, x_ref, stat_ref, vec_ref, shifted_ref):
    act = activation(x_ref, stat_ref, vec_ref)
    shifted_copies(act.astype(F32), side, shifted_ref, True)


def prepare(x, stat, vecs, side, tokens):
    pixels, chans = x.shape
    return call(
        functools.partial(prepare_kernel, side),
        (x, stat, vecs),
        [VMEM] * 3,
        tokens,
        out_shape=struct((3, pixels + 2 * side, chans), BF16),
        out_specs=VMEM,
        compiler_params=params(16),
        cost_estimate=pl.CostEstimate(
            flops=20 * x.size, bytes_accessed=8 * x.size, transcendentals=2 * x.size
        ),
        name="prepare",
    )


def grad_kernel(
    side, chunk, raw_ref, x_ref, stat_ref, vec_ref, weight, out_ref, sum_ref, scaled, g_ref
):
    pixels, chans = x_ref.shape
    edge = jnp.zeros((side, raw_ref.shape[1]), BF16)
    g_ref[0:side, :] = edge
    g_ref[side : side + pixels, :] = raw_ref[...]
    g_ref[side + pixels :, :] = edge
    column = lax.broadcasted_iota(jnp.int32, (chunk, chans), 0) % side
    mean, inv = stat_ref[0:1, :], stat_ref[1:2, :]
    gain = vec_ref[0:1, :].astype(F32)
    shift = vec_ref[1:2, :].astype(F32)
    sum_ref[...] = jnp.zeros_like(sum_ref)

    @pl.loop(0, pixels // chunk)
    def _(i):
        total = None
        for ky in range(3):
            start = pl.multiple_of(i * chunk + (2 - ky) * side, side)
            part = lax.dot_general(
                g_ref[pl.ds(start, chunk), :],
                weight[3 * ky * chans : 3 * (ky + 1) * chans, :],
                (((1,), (1,)), ((), ())),
                preferred_element_type=F32,
            )
            total = part if total is None else total + part
        before, same, later = (total[:, kx * chans : (kx + 1) * chans] for kx in range(3))
        total = (
            same
            + jnp.where(column == side - 1, 0.0, pltpu.roll(before, chunk - 1, 0))
            + jnp.where(column == 0, 0.0, pltpu.roll(later, 1, 0))
        )
        rows = pl.ds(pl.multiple_of(i * chunk, chunk), chunk)
        normed = (x_ref[rows, :].astype(F32) - mean) * inv
        pre = normed * gain + shift
        sig = 1.0 / (1.0 + jnp.exp(-pre))
        pre_grad = total * sig * (1.0 + pre * (1.0 - sig))
        sum_ref[0:1, :] += jnp.sum(pre_grad * normed, axis=0, keepdims=True)
        sum_ref[1:2, :] += jnp.sum(pre_grad, axis=0, keepdims=True)
        scaled[rows, :] = pre_grad * gain

    cross = group_mean_of(sum_ref[0:1, :] * gain, pixels)
    center = group_mean_of(sum_ref[1:2, :] * gain, pixels)

    @pl.loop(0, pixels // chunk)
    def _(i):
        rows = pl.ds(pl.multiple_of(i * chunk, chunk), chunk)
        normed = (x_ref[rows, :].astype(F32) - mean) * inv
        out_ref[rows, :] = ((scaled[rows, :] - center - normed * cross) * inv).astype(BF16)


def act_grad(g, x, stat, vecs, weight, side, tokens):
    pixels, chans = x.shape
    outs = g.shape[1]
    return call(
        functools.partial(grad_kernel, side, pixels // 2),
        (g, x, stat, vecs, weight),
        [VMEM] * 5,
        tokens,
        out_shape=(struct((pixels, chans), BF16), struct((2, chans), F32)),
        out_specs=(VMEM, VMEM),
        scratch_shapes=[
            pltpu.VMEM((pixels, chans), F32),
            pltpu.VMEM((pixels + 2 * side, outs), BF16),
        ],
        compiler_params=params(24),
        cost_estimate=pl.CostEstimate(
            flops=18 * chans * outs * pixels,
            bytes_accessed=18 * chans * outs + 12 * pixels * chans,
            transcendentals=2 * pixels * chans,
        ),
        name="act_grad",
    )


def conv_kernel(side, chunk, first, a_ref, vec_ref, weight, *rest):
    out_ref, token_ref, held, sems = rest[-4:]
    token_ref[...] = jnp.zeros_like(token_ref)
    chans = a_ref.shape[2]
    bias = vec_ref[2:3, :].astype(F32)
    chunks = held.shape[0] // chunk

    def copy(i):
        rows = pl.ds(pl.multiple_of(i * chunk, chunk), chunk)
        at = pl.ds(pl.multiple_of(first + i * chunk, chunk), chunk)
        return pltpu.make_async_copy(held.at[rows, :], out_ref.at[at, :], sems.at[i])

    for i in range(chunks):
        start = first + i * chunk
        taps = jnp.concatenate(
            [
                a_ref[tap % 3, start + (tap // 3) * side : start + (tap // 3) * side + chunk, :]
                for tap in range(9)
            ],
            axis=1,
        )
        total = jnp.dot(taps, weight[...], preferred_element_type=F32)
        held[i * chunk : (i + 1) * chunk, :] = (total + bias).astype(BF16)
        copy(i).start()
    for i in range(chunks):
        copy(i).wait()


def conv(shifted, vecs, weight, side, first, count, before, tokens):
    chans = shifted.shape[2]
    pixels = shifted.shape[1] - 2 * side
    outs = weight.shape[1]
    chunk = 256
    operands = (shifted, vecs, weight) + (() if before is None else (before,))
    return call(
        functools.partial(conv_kernel, side, chunk, first),
        operands,
        [VMEM] * 3 + [ANY] * (len(operands) - 3),
        tokens,
        out_shape=(struct((pixels, outs), BF16), struct((1, 128), F32)),
        out_specs=(ANY, VMEM),
        input_output_aliases={} if before is None else {3: 0},
        scratch_shapes=[
            pltpu.VMEM((count, outs), BF16),
            pltpu.SemaphoreType.DMA((count // chunk,)),
        ],
        compiler_params=params(16),
        cost_estimate=pl.CostEstimate(
            flops=18 * chans * outs * count,
            bytes_accessed=18 * chans * outs + 4 * count * chans,
            transcendentals=0,
        ),
        name="conv_forward",
    )


def join_kernel(scale, piece, place_ref, p0, p1, p2, p3, out_ref):
    r = place_ref[0]
    pieces = (p0, p1, p2, p3)
    step = (out_ref.shape[0] - piece) // (len(pieces) - 1)
    for q in range(len(pieces)):
        for rel, ref in enumerate(pieces):

            @pl.when((q ^ r) == rel)
            def _():
                out_ref[step * q : step * q + piece, :] = ref[0:piece, :].astype(F32) * scale


def join(place, pieces, rows, piece, scale, tokens):
    outs = pieces[0].shape[1]
    return call(
        functools.partial(join_kernel, scale, piece),
        (place, *pieces),
        [SMEM] + [VMEM] * 4,
        tokens,
        out_shape=struct((rows, outs), F32),
        out_specs=VMEM,
        compiler_params=params(),
        cost_estimate=pl.CostEstimate(
            flops=rows * outs, bytes_accessed=6 * rows * outs, transcendentals=0
        ),
        name="join_pieces",
    )


def tree_sum(terms):
    while len(terms) > 1:
        terms = [terms[i] + terms[i + 1] for i in range(0, len(terms), 2)]
    return terms[0]


def add_kernel(*refs):
    refs[-1][...] = tree_sum([ref[...] for ref in refs[:-1]])


def add_small(terms, tokens):
    return call(
        add_kernel,
        terms,
        [VMEM] * len(terms),
        tokens,
        out_shape=struct(terms[0].shape, F32),
        out_specs=VMEM,
        compiler_params=params(2),
        cost_estimate=pl.CostEstimate(
            flops=4 * terms[0].size, bytes_accessed=16 * terms[0].size, transcendentals=0
        ),
        name="add_small",
    )


def swap(x, axis, mask):
    n = lax.axis_size(axis)
    return lax.ppermute(x, axis, [(i, i ^ mask) for i in range(n)])


def gather_small(x):
    at = lax.axis_index("fsdp")
    other = swap(x, "fsdp", 1)
    pair = jnp.where(at % 2 == 1, jnp.stack([other, x]), jnp.stack([x, other]))
    got = [pair] + [swap(pair, "fsdp", m) for m in range(2, lax.axis_size("fsdp"), 2)]
    mask = 1
    while mask < len(got):
        flip = (at // (2 * mask)) % 2 == 1
        got = [jnp.where(flip, got[i ^ mask], got[i]) for i in range(len(got))]
        mask *= 2
    return jnp.concatenate(got)


def sum_all(x, axis, masks):
    return tree_sum([x] + [swap(x, axis, m) for m in masks])


def local_fast(features, out_grad, conv_weight, conv_bias, norm_gain, norm_shift):
    side = features.shape[1]
    chans = features.shape[3]
    outs = out_grad.shape[3]
    pixels = side * side
    rows = conv_weight.shape[0]
    reps, shards = lax.axis_size("rep"), lax.axis_size("fsdp")
    r, f = lax.axis_index("rep"), lax.axis_index("fsdp")
    z, core = f // 2, f % 2
    extra = rows - chans
    piece = round_up(-(-rows // reps), 16)
    x = features.reshape(pixels, chans)
    g = out_grad.reshape(pixels, outs)
    place = jnp.stack([r, z, core]).astype(jnp.int32)

    weight = lax.all_gather(conv_weight, "fsdp", axis=0, tiled=True)
    small = gather_small(jnp.stack([norm_gain, norm_shift, conv_bias]))
    sib_g = swap(g, "fsdp", 1)

    stat = stats(x)
    vecs = jnp.transpose(small, (1, 0, 2)).reshape(3, chans)
    own_t = activate(x, stat, vecs, ())
    sib_t = swap(own_t, "fsdp", 1)
    own_shifted, bias_sum = shift_grad(g, side, (own_t,))
    sib_shifted, _ = shift_grad(sib_g, side, (own_t,))
    operands = (own_t, sib_t, own_shifted, sib_shifted)

    keep, send0, send1 = weight_by_rep(
        place, operands, side, shards // 2, extra, piece, 0, outs, ()
    )
    got0 = swap(send0, "rep", 1)
    got1 = swap(send1, "rep", 2)
    next0, next1 = rep_step(keep, got0, got1, ())
    last0 = swap(next0, "rep", 2)
    last1 = swap(next1, "rep", 1)
    own_sum, *sends = rep_sum(keep, got0, got1, last0, last1, ())
    got = [swap(a, "fsdp", 2 * (m + 1)) for m, a in enumerate(sends)]
    act_shifted = prepare(x, stat, vecs, side, (keep,))
    in_grad, param_sums = act_grad(g, x, stat, vecs, weight, side, (own_sum,))
    done = finish((own_sum, *got), (bias_sum, param_sums))
    pieces_done = [done] + [swap(done, "rep", m) for m in range(1, reps)]

    part = 3 * pixels // 4
    conv_out, token = conv(act_shifted, vecs, weight, side, 0, part, None, (done,))
    small_sums = add_small_of(pieces_done, piece, 3, (token,))
    over_z = [small_sums] + [swap(small_sums, "fsdp", m) for m in range(2, shards, 2)]
    conv_out, token = conv(
        act_shifted, vecs, weight, side, part, pixels - part, conv_out, (small_sums,)
    )
    small_sums = add_small(over_z, (token,))
    scale = 1.0 / math.sqrt(reps * shards * pixels)
    small_sums = sum_all(small_sums, "fsdp", (1,)) * scale
    weight_grad = join(place, pieces_done, rows, piece, scale, (token,))
    share = outs // shards
    mine = lax.dynamic_slice_in_dim(small_sums.reshape(3, shards, share), f, 1, axis=1)
    mine = mine.reshape(3, share)
    return (
        conv_out.reshape(1, side, side, outs),
        in_grad.reshape(1, side, side, chans),
        weight_grad,
        mine[0],
        mine[1],
        mine[2],
    )


def round_up(n, m):
    return -(-n // m) * m


def fits(mesh_shape, images, rows, chans, outs, side):
    reps, shards = mesh_shape["rep"], mesh_shape["fsdp"]
    if images != reps * shards or reps != 2 * 2 or shards != 9 - 1:
        return False
    if chans != outs or rows * shards != 9 * chans or chans % 128 or side % 16 or outs < 3 * 128:
        return False
    extra, piece = rows - chans, round_up(-(-rows // reps), 16)
    step = (rows - piece) // (reps - 1)
    return (
        extra % 16 == 0
        and step * (reps - 1) == rows - piece
        and step % 16 == 0
        and piece % 32 == 0
    )


def local(features, out_grad, conv_weight, conv_bias, norm_gain, norm_shift):
    images_here = features.shape[0]
    side_cells = features.shape[1]
    channels = features.shape[3]
    pixels = side_cells * side_cells
    group_size = channels // GROUPS
    full_weight, bias_all, gain_all, shift_all = (
        lax.all_gather(conv_weight, "fsdp", axis=0, tiled=True),
        lax.all_gather(conv_bias, "fsdp", axis=0, tiled=True),
        lax.all_gather(norm_gain, "fsdp", axis=0, tiled=True),
        lax.all_gather(norm_shift, "fsdp", axis=0, tiled=True),
    )
    out_chans = full_weight.shape[1]
    values = features.astype(jnp.float32).reshape(images_here, pixels, GROUPS, group_size)
    group_mean = jnp.mean(values, axis=(1, 3), keepdims=True)
    centered = values - group_mean
    group_var = jnp.mean(centered * centered, axis=(1, 3), keepdims=True)
    inv_std = lax.rsqrt(group_var + epsilon)
    normed = centered * inv_std
    gain_cols = gain_all.astype(jnp.float32).reshape(1, 1, GROUPS, group_size)
    shift_cols = shift_all.astype(jnp.float32).reshape(1, 1, GROUPS, group_size)
    pre_act = normed * gain_cols + shift_cols
    activated = (
        jax.nn.silu(pre_act)
        .astype(jnp.bfloat16)
        .reshape(images_here, side_cells, side_cells, channels)
    )
    padded = jnp.pad(activated, ((0, 0), (1, 1), (1, 1), (0, 0)))
    conv_sum = jnp.zeros((images_here * pixels, out_chans), jnp.float32)
    taps_list = []
    for row_off in range(3):
        for col_off in range(3):
            tap_index = 3 * row_off + col_off
            tap_piece = padded[
                :, row_off : row_off + side_cells, col_off : col_off + side_cells, :
            ].reshape(images_here * pixels, channels)
            taps_list.append(tap_piece)
            conv_sum = conv_sum + jnp.dot(
                tap_piece,
                full_weight[tap_index * channels : (tap_index + 1) * channels],
                preferred_element_type=jnp.float32,
            )
    conv_out = (
        (conv_sum + bias_all.astype(jnp.float32)[None, :])
        .astype(jnp.bfloat16)
        .reshape(images_here, side_cells, side_cells, out_chans)
    )
    back_weight, back_gain = (
        lax.all_gather(conv_weight, "fsdp", axis=0, tiled=True),
        lax.all_gather(norm_gain, "fsdp", axis=0, tiled=True),
    )
    grad_rows = out_grad.reshape(images_here * pixels, out_chans)
    grad_padded = jnp.zeros((images_here, side_cells + 2, side_cells + 2, channels), jnp.float32)
    weight_list = []
    for row_off in range(3):
        for col_off in range(3):
            tap_index = 3 * row_off + col_off
            tap_rows = back_weight[tap_index * channels : (tap_index + 1) * channels]
            tap_grad = lax.dot_general(
                grad_rows, tap_rows, (((1,), (1,)), ((), ())), preferred_element_type=jnp.float32
            )
            grad_padded = grad_padded.at[
                :, row_off : row_off + side_cells, col_off : col_off + side_cells, :
            ].add(tap_grad.reshape(images_here, side_cells, side_cells, channels))
            weight_list.append(
                lax.dot_general(
                    taps_list[tap_index],
                    grad_rows,
                    (((0,), (0,)), ((), ())),
                    preferred_element_type=jnp.float32,
                )
            )
    act_grad = grad_padded[:, 1:-1, 1:-1, :].reshape(images_here, pixels, GROUPS, group_size)
    sig_pre = jax.nn.sigmoid(pre_act)
    pre_grad = act_grad * sig_pre * (1.0 + pre_act * (1.0 - sig_pre))
    norm_grad = pre_grad * back_gain.astype(jnp.float32).reshape(1, 1, GROUPS, group_size)
    grad_mean = jnp.mean(norm_grad, axis=(1, 3), keepdims=True)
    cross_mean = jnp.mean(norm_grad * normed, axis=(1, 3), keepdims=True)
    in_grad = (
        ((norm_grad - grad_mean - normed * cross_mean) * inv_std)
        .astype(jnp.bfloat16)
        .reshape(images_here, side_cells, side_cells, channels)
    )
    rep_size = lax.axis_size("rep")
    fsdp_size = lax.axis_size("fsdp")
    grad_scale = 1.0 / math.sqrt(images_here * rep_size * fsdp_size * pixels)
    weight_term = jnp.concatenate(weight_list, axis=0) * grad_scale
    bias_term = jnp.sum(grad_rows.astype(jnp.float32), axis=0) * grad_scale
    gain_term = jnp.sum(pre_grad * normed, axis=(0, 1)).reshape(channels) * grad_scale
    shift_term = jnp.sum(pre_grad, axis=(0, 1)).reshape(channels) * grad_scale
    shards = (
        lax.psum_scatter(weight_term, "fsdp", scatter_dimension=0, tiled=True),
        lax.psum_scatter(bias_term, "fsdp", scatter_dimension=0, tiled=True),
        lax.psum_scatter(gain_term, "fsdp", scatter_dimension=0, tiled=True),
        lax.psum_scatter(shift_term, "fsdp", scatter_dimension=0, tiled=True),
    )
    weight_grad, bias_grad, gain_grad, shift_grad = lax.psum(
        (shards[0], shards[1], shards[2], shards[3]), "rep"
    )
    return (conv_out, in_grad, weight_grad, bias_grad, gain_grad, shift_grad)


def solution(mesh):
    placed = (
        P(("rep", "fsdp"), None, None, None),
        P(("rep", "fsdp"), None, None, None),
        P("fsdp", None),
        P("fsdp"),
        P("fsdp"),
        P("fsdp"),
    )
    out_placed = (
        P(("rep", "fsdp"), None, None, None),
        P(("rep", "fsdp"), None, None, None),
        P("fsdp", None),
        P("fsdp"),
        P("fsdp"),
        P("fsdp"),
    )

    def run(features, out_grad, conv_weight, *vectors):
        images, side, _, chans = features.shape
        rows, outs = conv_weight.shape
        shape = dict(mesh.shape)
        fast = fits(shape, images, rows // shape["fsdp"], chans, outs, side)
        return jax.shard_map(
            local_fast if fast else local,
            mesh=mesh,
            in_specs=placed,
            out_specs=out_placed,
            check_vma=False,
        )(features, out_grad, conv_weight, *vectors)

    return run
```

```python
import functools
import math

import jax
import jax.numpy as jnp
from jax import lax
from jax.experimental import pallas as pl
from jax.experimental.pallas import tpu as pltpu
from jax.sharding import PartitionSpec as P

GROUPS = 16


epsilon = 1e-05

F32 = jnp.float32
BF16 = jnp.bfloat16
VMEM = pl.BlockSpec(memory_space=pltpu.VMEM)
SMEM = pl.BlockSpec(memory_space=pltpu.SMEM)
ANY = pl.BlockSpec(memory_space=pl.ANY)


def params(mib=24):
    return pltpu.CompilerParams(vmem_limit_bytes=mib * 1024 * 1024)


def call(kernel, operands, in_specs, tokens=(), **options):
    given = len(operands)

    def body(*refs):
        kernel(*refs[:given], *refs[given + len(tokens) :])

    return pl.pallas_call(
        body, in_specs=list(in_specs) + [ANY] * len(tokens), **options
    )(*operands, *tokens)


def struct(shape, dtype):
    return jax.ShapeDtypeStruct(shape, dtype)


def shifted_copies(x, side, out_ref, first):
    pixels = x.shape[0]
    column = lax.broadcasted_iota(jnp.int32, x.shape, 0) % side
    edge = jnp.zeros((side, x.shape[1]), BF16)
    for kx in range(3):
        move = (kx - 1) if first else (1 - kx)
        if move == 0:
            moved = x
        elif move == 1:
            moved = jnp.where(column == side - 1, 0.0, pltpu.roll(x, pixels - 1, 0))
        else:
            moved = jnp.where(column == 0, 0.0, pltpu.roll(x, 1, 0))
        out_ref[kx, 0:side, :] = edge
        out_ref[kx, side : side + pixels, :] = moved.astype(BF16)
        out_ref[kx, side + pixels : 2 * side + pixels, :] = edge


def shift_kernel(side, x_ref, out_ref, sum_ref):
    x = x_ref[...].astype(F32)
    sum_ref[...] = jnp.sum(x, axis=0, keepdims=True)
    shifted_copies(x, side, out_ref, False)


def shift_grad(x, side, tokens):
    pixels, chans = x.shape
    return call(
        functools.partial(shift_kernel, side),
        (x,),
        [VMEM],
        tokens,
        out_shape=(
            struct((3, pixels + 2 * side, chans), BF16),
            struct((1, chans), F32),
        ),
        out_specs=(VMEM, VMEM),
        compiler_params=params(),
        cost_estimate=pl.CostEstimate(
            flops=8 * x.size, bytes_accessed=8 * x.size, transcendentals=0
        ),
        name="shift_grad",
    )


def group_means(sums, pixels):
    chans = sums.shape[1]
    size = chans // GROUPS
    lanes = round_up(GROUPS, 128)
    channel = lax.broadcasted_iota(jnp.int32, (chans, lanes), 0)
    first = lax.broadcasted_iota(jnp.int32, (chans, lanes), 1) * size
    member = jnp.where((channel >= first) & (channel < first + size), 1.0, 0.0).astype(F32)
    exact = {"preferred_element_type": F32, "precision": lax.Precision.HIGHEST}
    total = jnp.dot(sums, member, **exact)
    spread = lax.dot_general(total, member, (((1,), (1,)), ((), ())), **exact)
    return spread * (1.0 / (pixels * size))


def stats_kernel(x_ref, out_ref):
    pixels = x_ref.shape[0]
    x = x_ref[...].astype(F32)
    spread = (8, x.shape[1])
    column_sum = jnp.sum(x, axis=0, keepdims=True)
    mean = group_means(jnp.broadcast_to(column_sum, spread), pixels)[0:1]
    centered = x - mean
    column_sum = jnp.sum(centered * centered, axis=0, keepdims=True)
    var = group_means(jnp.broadcast_to(column_sum, spread), pixels)[0:1]
    out_ref[0:1, :] = mean
    out_ref[1:2, :] = lax.rsqrt(var + epsilon)


def stats(x):
    return pl.pallas_call(
        stats_kernel,
        out_shape=struct((2, x.shape[1]), F32),
        in_specs=[VMEM],
        out_specs=VMEM,
        compiler_params=params(),
        cost_estimate=pl.CostEstimate(
            flops=5 * x.size, bytes_accessed=2 * x.size, transcendentals=0
        ),
        name="norm_stats",
    )(x)


def activation(x_ref, stat_ref, vec_ref):
    mean, inv = stat_ref[0:1, :], stat_ref[1:2, :]
    gain = vec_ref[0:1, :].astype(F32)
    shift = vec_ref[1:2, :].astype(F32)
    pre = (x_ref[...].astype(F32) - mean) * inv * gain + shift
    return (pre / (1.0 + jnp.exp(-pre))).astype(BF16)


def act_kernel(x_ref, stat_ref, vec_ref, turned_ref):
    turned_ref[...] = activation(x_ref, stat_ref, vec_ref).T


def activate(x, stat, vecs, tokens):
    pixels, chans = x.shape
    return call(
        act_kernel,
        (x, stat, vecs),
        [VMEM, VMEM, VMEM],
        tokens,
        out_shape=struct((chans, pixels), BF16),
        out_specs=VMEM,
        compiler_params=params(),
        cost_estimate=pl.CostEstimate(
            flops=10 * x.size, bytes_accessed=4 * x.size, transcendentals=2 * x.size
        ),
        name="activate",
    )


def weight_blocks(side, extra, blocks, core, own_t, sib_t, own_g, sib_g, first, count, block_ref):
    chans, pixels = own_t.shape

    def tap_rows(ref, tap):
        start = pl.multiple_of((2 - tap // 3) * side, side)
        return ref[tap % 3, pl.ds(start, pixels), first : first + count]

    def product(low, high, tap):
        return jnp.dot(
            own_t[low:high, :], tap_rows(own_g, tap), preferred_element_type=F32
        ) + jnp.dot(sib_t[low:high, :], tap_rows(sib_g, tap), preferred_element_type=F32)

    for k in range(blocks):
        low, high = 2 * extra * k, 2 * extra * (k + 1)
        block_ref[0 : chans - low, :] = product(low, chans, 2 * k + core)
        block_ref[chans - low : chans + 2 * extra, :] = product(0, high, 2 * k + 1 + core)
        yield k


def weight_by_rep_kernel(
    side, extra, first, piece, place_ref, own_t, sib_t, own_g, sib_g,
    keep_ref, send0_ref, send1_ref, block_ref,
):
    chans = own_t.shape[0]
    r, z, core = place_ref[0], place_ref[1], place_ref[2]
    half, count = keep_ref.shape[2], keep_ref.shape[4]
    reps = 2 * keep_ref.shape[1]
    step = (chans + extra - piece) // (reps - 1)

    def rows_of(rel):
        at = pl.multiple_of(extra * core + step * (r ^ rel), 16)
        return block_ref[pl.ds(at, piece), :]

    for k in weight_blocks(
        side, extra, 2 * half, core, own_t, sib_t, own_g, sib_g, first, count, block_ref
    ):
        rel_z = k ^ z
        path, slot = rel_z // half, rel_z % half
        keep_ref[path, 0, slot] = rows_of(0)

        @pl.when(path == 0)
        def _():
            send0_ref[0, slot] = rows_of(1).astype(BF16)
            keep_ref[0, 1, slot] = rows_of(2)
            send0_ref[1, slot] = rows_of(3).astype(BF16)

        @pl.when(path == 1)
        def _():
            send1_ref[0, slot] = rows_of(2).astype(BF16)
            keep_ref[1, 1, slot] = rows_of(1)
            send1_ref[1, slot] = rows_of(3).astype(BF16)


def weight_call(kernel, out_shape, place, operands, extra, first, count, blocks, tokens, name):
    chans, pixels = operands[0].shape
    return call(
        kernel,
        (place,) + operands,
        [SMEM, VMEM, VMEM, VMEM, VMEM],
        tokens,
        out_shape=out_shape,
        out_specs=(VMEM,) * len(out_shape),
        scratch_shapes=[pltpu.VMEM((chans + 2 * extra, count), F32)],
        compiler_params=params(28),
        cost_estimate=pl.CostEstimate(
            flops=4 * blocks * (chans + 2 * extra) * pixels * count,
            bytes_accessed=20 * chans * pixels,
            transcendentals=0,
        ),
        name=name,
    )


def weight_by_rep(place, operands, side, blocks, extra, piece, first, count, tokens):
    half = blocks // 2
    out_shape = (
        struct((2, 2, half, piece, count), F32),
        struct((2, half, piece, count), BF16),
        struct((2, half, piece, count), BF16),
    )
    kernel = functools.partial(weight_by_rep_kernel, side, extra, first, piece)
    return weight_call(
        kernel, out_shape, place, operands, extra, first, count, blocks, tokens, "weight_grad_rep"
    )


def finish_kernel(bias_ref, param_ref, *refs):
    out_ref = refs[-1]
    total = refs[0][...]
    for ref in refs[1:-1]:
        total = total + ref[...].astype(F32)
    piece = total.shape[0]
    out_ref[0:piece, :] = total.astype(BF16)
    small = jnp.concatenate([bias_ref[...], param_ref[...]], axis=0)
    high = small.astype(BF16).astype(F32)
    middle = (small - high).astype(BF16).astype(F32)
    parts = [high, middle, small - high - middle]
    spare = out_ref.shape[0] - piece - 3 * small.shape[0]
    parts.append(jnp.zeros((spare, small.shape[1]), F32))
    out_ref[piece:, :] = jnp.concatenate(parts, axis=0).astype(BF16)


def finish(terms, small):
    piece, outs = terms[0].shape
    return call(
        finish_kernel,
        (*small, *terms),
        [VMEM] * (2 + len(terms)),
        out_shape=struct((piece + 16, outs), BF16),
        out_specs=VMEM,
        compiler_params=params(8),
        cost_estimate=pl.CostEstimate(
            flops=4 * terms[0].size, bytes_accessed=12 * terms[0].size, transcendentals=0
        ),
        name="finish_sum",
    )


def add_small_kernel(piece, *refs):
    out_ref = refs[-1]
    count = out_ref.shape[0]
    terms = []
    for ref in refs[:-1]:
        rows = ref[piece:, :].astype(F32)
        terms.append(rows[0:count] + rows[count : 2 * count] + rows[2 * count : 3 * count])
    out_ref[...] = tree_sum(terms)


def add_small_of(pieces, piece, count, tokens):
    return call(
        functools.partial(add_small_kernel, piece),
        pieces,
        [VMEM] * len(pieces),
        tokens,
        out_shape=struct((count, pieces[0].shape[1]), F32),
        out_specs=VMEM,
        compiler_params=params(4),
        cost_estimate=pl.CostEstimate(
            flops=4 * pieces[0].size, bytes_accessed=4 * pieces[0].size, transcendentals=0
        ),
        name="add_small_of",
    )


def rep_step_kernel(keep_ref, got0, got1, next0, next1):
    next0[...] = (keep_ref[0, 1] + got0[1].astype(F32)).astype(BF16)
    next1[...] = (keep_ref[1, 1] + got1[1].astype(F32)).astype(BF16)


def rep_step(keep, got0, got1, tokens):
    out = struct(keep.shape[2:], BF16)
    return call(
        rep_step_kernel,
        (keep, got0, got1),
        [VMEM] * 3,
        tokens,
        out_shape=(out, out),
        out_specs=(VMEM, VMEM),
        compiler_params=params(12),
        cost_estimate=pl.CostEstimate(
            flops=keep.size, bytes_accessed=4 * keep.size, transcendentals=0
        ),
        name="rep_step",
    )


def rep_sum_kernel(keep_ref, got0, got1, last0, last1, own_ref, *sends):
    half = keep_ref.shape[2]
    for i, out in enumerate((own_ref,) + sends):
        path, slot = i // half, i % half
        got, last = ((got0, last0), (got1, last1))[path]
        total = keep_ref[path, 0, slot] + got[0, slot].astype(F32) + last[slot].astype(F32)
        out[...] = total.astype(out.dtype)


def rep_sum(keep, got0, got1, last0, last1, tokens):
    half, piece, count = keep.shape[2:]
    return call(
        rep_sum_kernel,
        (keep, got0, got1, last0, last1),
        [VMEM] * 5,
        tokens,
        out_shape=(struct((piece, count), F32),)
        + (struct((piece, count), BF16),) * (2 * half - 1),
        out_specs=(VMEM,) * (2 * half),
        compiler_params=params(12),
        cost_estimate=pl.CostEstimate(
            flops=keep.size, bytes_accessed=4 * keep.size, transcendentals=0
        ),
        name="rep_sum",
    )


def prepare_kernel(side, x_ref, stat_ref, vec_ref, shifted_ref):
    act = activation(x_ref, stat_ref, vec_ref)
    shifted_copies(act.astype(F32), side, shifted_ref, True)


def prepare(x, stat, vecs, side, tokens):
    pixels, chans = x.shape
    return call(
        functools.partial(prepare_kernel, side),
        (x, stat, vecs),
        [VMEM] * 3,
        tokens,
        out_shape=struct((3, pixels + 2 * side, chans), BF16),
        out_specs=VMEM,
        compiler_params=params(16),
        cost_estimate=pl.CostEstimate(
            flops=20 * x.size, bytes_accessed=8 * x.size, transcendentals=2 * x.size
        ),
        name="prepare",
    )


def arrange_kernel(source, out_ref, sems):
    rows, outs = out_ref.shape[0] // 3, source.shape[1]
    copies = [
        pltpu.make_async_copy(
            source.at[pl.ds(tap * rows, rows), :],
            out_ref.at[pl.ds(tap % 3 * rows, rows), pl.ds(tap // 3 * outs, outs)],
            sems.at[tap],
        )
        for tap in range(9)
    ]
    for c in copies:
        c.start()
    for c in copies:
        c.wait()


def arrange(weight):
    rows, outs = weight.shape
    return call(
        arrange_kernel,
        (weight,),
        [ANY],
        out_shape=struct((rows // 3, 3 * outs), BF16),
        out_specs=VMEM,
        scratch_shapes=[pltpu.SemaphoreType.DMA((9,))],
        compiler_params=params(44),
        cost_estimate=pl.CostEstimate(
            flops=0, bytes_accessed=4 * weight.size, transcendentals=0
        ),
        name="arrange_weight",
    )


def grad_kernel(
    side, chunk, raw_ref, x_ref, stat_ref, vec_ref, weight, out_ref, sum_ref, scaled, g_ref
):
    pixels, chans = x_ref.shape
    edge = jnp.zeros((side, raw_ref.shape[1]), BF16)
    g_ref[0:side, :] = edge
    g_ref[side : side + pixels, :] = raw_ref[...]
    g_ref[side + pixels :, :] = edge
    column = lax.broadcasted_iota(jnp.int32, (chunk, chans), 0) % side
    mean, inv = stat_ref[0:1, :], stat_ref[1:2, :]
    gain = vec_ref[0:1, :].astype(F32)
    shift = vec_ref[1:2, :].astype(F32)
    sum_ref[...] = jnp.zeros_like(sum_ref)

    @pl.loop(0, pixels // chunk)
    def _(i):
        rows_of = [
            g_ref[pl.ds(pl.multiple_of(i * chunk + (2 - ky) * side, side), chunk), :]
            for ky in range(3)
        ]
        total = lax.dot_general(
            jnp.concatenate(rows_of, axis=1),
            weight[...],
            (((1,), (1,)), ((), ())),
            preferred_element_type=F32,
        )
        before, same, later = (total[:, kx * chans : (kx + 1) * chans] for kx in range(3))
        total = (
            same
            + jnp.where(column == side - 1, 0.0, pltpu.roll(before, chunk - 1, 0))
            + jnp.where(column == 0, 0.0, pltpu.roll(later, 1, 0))
        )
        rows = pl.ds(pl.multiple_of(i * chunk, chunk), chunk)
        normed = (x_ref[rows, :].astype(F32) - mean) * inv
        pre = normed * gain + shift
        sig = 1.0 / (1.0 + jnp.exp(-pre))
        pre_grad = total * sig * (1.0 + pre * (1.0 - sig))
        sum_ref[0:1, :] += jnp.sum(pre_grad * normed, axis=0, keepdims=True)
        sum_ref[1:2, :] += jnp.sum(pre_grad, axis=0, keepdims=True)
        scaled[rows, :] = pre_grad * gain

    rest = jnp.zeros((6, chans), F32)
    means = group_means(jnp.concatenate([sum_ref[...] * gain, rest], axis=0), pixels)
    cross, center = means[0:1], means[1:2]

    @pl.loop(0, pixels // 128)
    def _(i):
        rows = pl.ds(pl.multiple_of(i * 128, 128), 128)
        normed = (x_ref[rows, :].astype(F32) - mean) * inv
        out_ref[rows, :] = ((scaled[rows, :] - center - normed * cross) * inv).astype(BF16)


def act_grad(g, x, stat, vecs, weight, side, tokens):
    pixels, chans = x.shape
    outs = g.shape[1]
    return call(
        functools.partial(grad_kernel, side, pixels // 2),
        (g, x, stat, vecs, weight),
        [VMEM] * 5,
        tokens,
        out_shape=(struct((pixels, chans), BF16), struct((2, chans), F32)),
        out_specs=(VMEM, VMEM),
        scratch_shapes=[
            pltpu.VMEM((pixels, chans), F32),
            pltpu.VMEM((pixels + 2 * side, outs), BF16),
        ],
        compiler_params=params(24),
        cost_estimate=pl.CostEstimate(
            flops=18 * chans * outs * pixels,
            bytes_accessed=18 * chans * outs + 12 * pixels * chans,
            transcendentals=2 * pixels * chans,
        ),
        name="act_grad",
    )


def conv_kernel(side, first, a_ref, vec_ref, weight, *rest):
    out_ref, token_ref, held, sem = rest[-4:]
    token_ref[...] = jnp.zeros_like(token_ref)
    count, outs = held.shape
    pixels = out_ref.shape[0]
    low, high = max(0, first - side), min(pixels, first + count + side)
    shifted = jnp.concatenate([a_ref[kx, side + low : side + high, :] for kx in range(3)], axis=1)
    parts = jnp.dot(shifted, weight[...], preferred_element_type=F32)
    total = None
    for ky in range(3):
        begin = first + (ky - 1) * side
        end = begin + count
        part = parts[max(begin, 0) - low : min(end, pixels) - low, ky * outs : (ky + 1) * outs]
        edge = jnp.zeros((side, outs), F32)
        if begin < 0:
            part = jnp.concatenate([edge, part], axis=0)
        if end > pixels:
            part = jnp.concatenate([part, edge], axis=0)
        total = part if total is None else total + part
    held[...] = (total + vec_ref[2:3, :].astype(F32)).astype(BF16)
    copy = pltpu.make_async_copy(held, out_ref.at[pl.ds(first, count), :], sem)
    copy.start()
    copy.wait()


def conv(shifted, vecs, weight, side, first, count, before, tokens):
    chans = shifted.shape[2]
    pixels = shifted.shape[1] - 2 * side
    outs = weight.shape[1] // 3
    operands = (shifted, vecs, weight) + (() if before is None else (before,))
    return call(
        functools.partial(conv_kernel, side, first),
        operands,
        [VMEM] * 3 + [ANY] * (len(operands) - 3),
        tokens,
        out_shape=(struct((pixels, outs), BF16), struct((1, 128), F32)),
        out_specs=(ANY, VMEM),
        input_output_aliases={} if before is None else {3: 0},
        scratch_shapes=[pltpu.VMEM((count, outs), BF16), pltpu.SemaphoreType.DMA],
        compiler_params=params(24),
        cost_estimate=pl.CostEstimate(
            flops=18 * chans * outs * count,
            bytes_accessed=18 * chans * outs + 4 * count * chans,
            transcendentals=0,
        ),
        name="conv_forward",
    )


def join_kernel(scale, piece, place_ref, p0, p1, p2, p3, out_ref):
    r = place_ref[0]
    pieces = (p0, p1, p2, p3)
    step = (out_ref.shape[0] - piece) // (len(pieces) - 1)
    for q in range(len(pieces)):
        for rel, ref in enumerate(pieces):

            @pl.when((q ^ r) == rel)
            def _():
                out_ref[step * q : step * q + piece, :] = ref[0:piece, :].astype(F32) * scale


def join(place, pieces, rows, piece, scale, tokens):
    outs = pieces[0].shape[1]
    return call(
        functools.partial(join_kernel, scale, piece),
        (place, *pieces),
        [SMEM] + [VMEM] * 4,
        tokens,
        out_shape=struct((rows, outs), F32),
        out_specs=VMEM,
        compiler_params=params(),
        cost_estimate=pl.CostEstimate(
            flops=rows * outs, bytes_accessed=6 * rows * outs, transcendentals=0
        ),
        name="join_pieces",
    )


def tree_sum(terms):
    while len(terms) > 1:
        terms = [terms[i] + terms[i + 1] for i in range(0, len(terms), 2)]
    return terms[0]


def add_kernel(*refs):
    refs[-1][...] = tree_sum([ref[...] for ref in refs[:-1]])


def add_small(terms, tokens):
    return call(
        add_kernel,
        terms,
        [VMEM] * len(terms),
        tokens,
        out_shape=struct(terms[0].shape, F32),
        out_specs=VMEM,
        compiler_params=params(2),
        cost_estimate=pl.CostEstimate(
            flops=4 * terms[0].size, bytes_accessed=16 * terms[0].size, transcendentals=0
        ),
        name="add_small",
    )


def swap(x, axis, mask):
    n = lax.axis_size(axis)
    return lax.ppermute(x, axis, [(i, i ^ mask) for i in range(n)])


def gather_small(x):
    at = lax.axis_index("fsdp")
    other = swap(x, "fsdp", 1)
    pair = jnp.where(at % 2 == 1, jnp.stack([other, x]), jnp.stack([x, other]))
    got = [pair] + [swap(pair, "fsdp", m) for m in range(2, lax.axis_size("fsdp"), 2)]
    mask = 1
    while mask < len(got):
        flip = (at // (2 * mask)) % 2 == 1
        got = [jnp.where(flip, got[i ^ mask], got[i]) for i in range(len(got))]
        mask *= 2
    return jnp.concatenate(got)


def sum_all(x, axis, masks):
    return tree_sum([x] + [swap(x, axis, m) for m in masks])


def local_fast(features, out_grad, conv_weight, conv_bias, norm_gain, norm_shift):
    side = features.shape[1]
    chans = features.shape[3]
    outs = out_grad.shape[3]
    pixels = side * side
    rows = conv_weight.shape[0]
    reps, shards = lax.axis_size("rep"), lax.axis_size("fsdp")
    r, f = lax.axis_index("rep"), lax.axis_index("fsdp")
    z, core = f // 2, f % 2
    extra = rows - chans
    piece = round_up(-(-rows // reps), 16)
    x = features.reshape(pixels, chans)
    g = out_grad.reshape(pixels, outs)
    place = jnp.stack([r, z, core]).astype(jnp.int32)

    weight = lax.all_gather(conv_weight, "fsdp", axis=0, tiled=True)
    small = gather_small(jnp.stack([norm_gain, norm_shift, conv_bias]))
    sib_g = swap(g, "fsdp", 1)

    stat = stats(x)
    vecs = jnp.transpose(small, (1, 0, 2)).reshape(3, chans)
    own_t = activate(x, stat, vecs, ())
    sib_t = swap(own_t, "fsdp", 1)
    own_shifted, bias_sum = shift_grad(g, side, (own_t,))
    sib_shifted, _ = shift_grad(sib_g, side, (own_t,))
    operands = (own_t, sib_t, own_shifted, sib_shifted)

    keep, send0, send1 = weight_by_rep(
        place, operands, side, shards // 2, extra, piece, 0, outs, ()
    )
    got0 = swap(send0, "rep", 1)
    got1 = swap(send1, "rep", 2)
    next0, next1 = rep_step(keep, got0, got1, ())
    last0 = swap(next0, "rep", 2)
    last1 = swap(next1, "rep", 1)
    own_sum, *sends = rep_sum(keep, got0, got1, last0, last1, ())
    got = [swap(a, "fsdp", 2 * (m + 1)) for m, a in enumerate(sends)]
    act_shifted = prepare(x, stat, vecs, side, (keep,))
    weight = arrange(weight)
    in_grad, param_sums = act_grad(g, x, stat, vecs, weight, side, (own_sum,))
    done = finish((own_sum, *got), (bias_sum, param_sums))
    pieces_done = [done] + [swap(done, "rep", m) for m in range(1, reps)]

    part = 7 * pixels // 8
    conv_out, token = conv(act_shifted, vecs, weight, side, 0, part, None, (done,))
    small_sums = add_small_of(pieces_done, piece, 3, (token,))
    over_z = [small_sums] + [swap(small_sums, "fsdp", m) for m in range(2, shards, 2)]
    conv_out, token = conv(
        act_shifted, vecs, weight, side, part, pixels - part, conv_out, (small_sums,)
    )
    small_sums = add_small(over_z, (token,))
    scale = 1.0 / math.sqrt(reps * shards * pixels)
    small_sums = sum_all(small_sums, "fsdp", (1,)) * scale
    weight_grad = join(place, pieces_done, rows, piece, scale, (token,))
    share = outs // shards
    mine = lax.dynamic_slice_in_dim(small_sums.reshape(3, shards, share), f, 1, axis=1)
    mine = mine.reshape(3, share)
    return (
        conv_out.reshape(1, side, side, outs),
        in_grad.reshape(1, side, side, chans),
        weight_grad,
        mine[0],
        mine[1],
        mine[2],
    )


def round_up(n, m):
    return -(-n // m) * m


def fits(mesh_shape, images, rows, chans, outs, side):
    reps, shards = mesh_shape["rep"], mesh_shape["fsdp"]
    if images != reps * shards or reps != 2 * 2 or shards != 9 - 1:
        return False
    if chans != outs or rows * shards != 9 * chans or chans % 128 or side % 16 or outs < 3 * 128:
        return False
    extra, piece = rows - chans, round_up(-(-rows // reps), 16)
    step = (rows - piece) // (reps - 1)
    return (
        extra % 16 == 0
        and step * (reps - 1) == rows - piece
        and step % 16 == 0
        and piece % 32 == 0
    )


def local(features, out_grad, conv_weight, conv_bias, norm_gain, norm_shift):
    images_here = features.shape[0]
    side_cells = features.shape[1]
    channels = features.shape[3]
    pixels = side_cells * side_cells
    group_size = channels // GROUPS
    full_weight, bias_all, gain_all, shift_all = (
        lax.all_gather(conv_weight, "fsdp", axis=0, tiled=True),
        lax.all_gather(conv_bias, "fsdp", axis=0, tiled=True),
        lax.all_gather(norm_gain, "fsdp", axis=0, tiled=True),
        lax.all_gather(norm_shift, "fsdp", axis=0, tiled=True),
    )
    out_chans = full_weight.shape[1]
    values = features.astype(jnp.float32).reshape(images_here, pixels, GROUPS, group_size)
    group_mean = jnp.mean(values, axis=(1, 3), keepdims=True)
    centered = values - group_mean
    group_var = jnp.mean(centered * centered, axis=(1, 3), keepdims=True)
    inv_std = lax.rsqrt(group_var + epsilon)
    normed = centered * inv_std
    gain_cols = gain_all.astype(jnp.float32).reshape(1, 1, GROUPS, group_size)
    shift_cols = shift_all.astype(jnp.float32).reshape(1, 1, GROUPS, group_size)
    pre_act = normed * gain_cols + shift_cols
    activated = (
        jax.nn.silu(pre_act)
        .astype(jnp.bfloat16)
        .reshape(images_here, side_cells, side_cells, channels)
    )
    padded = jnp.pad(activated, ((0, 0), (1, 1), (1, 1), (0, 0)))
    conv_sum = jnp.zeros((images_here * pixels, out_chans), jnp.float32)
    taps_list = []
    for row_off in range(3):
        for col_off in range(3):
            tap_index = 3 * row_off + col_off
            tap_piece = padded[
                :, row_off : row_off + side_cells, col_off : col_off + side_cells, :
            ].reshape(images_here * pixels, channels)
            taps_list.append(tap_piece)
            conv_sum = conv_sum + jnp.dot(
                tap_piece,
                full_weight[tap_index * channels : (tap_index + 1) * channels],
                preferred_element_type=jnp.float32,
            )
    conv_out = (
        (conv_sum + bias_all.astype(jnp.float32)[None, :])
        .astype(jnp.bfloat16)
        .reshape(images_here, side_cells, side_cells, out_chans)
    )
    back_weight, back_gain = (
        lax.all_gather(conv_weight, "fsdp", axis=0, tiled=True),
        lax.all_gather(norm_gain, "fsdp", axis=0, tiled=True),
    )
    grad_rows = out_grad.reshape(images_here * pixels, out_chans)
    grad_padded = jnp.zeros((images_here, side_cells + 2, side_cells + 2, channels), jnp.float32)
    weight_list = []
    for row_off in range(3):
        for col_off in range(3):
            tap_index = 3 * row_off + col_off
            tap_rows = back_weight[tap_index * channels : (tap_index + 1) * channels]
            tap_grad = lax.dot_general(
                grad_rows, tap_rows, (((1,), (1,)), ((), ())), preferred_element_type=jnp.float32
            )
            grad_padded = grad_padded.at[
                :, row_off : row_off + side_cells, col_off : col_off + side_cells, :
            ].add(tap_grad.reshape(images_here, side_cells, side_cells, channels))
            weight_list.append(
                lax.dot_general(
                    taps_list[tap_index],
                    grad_rows,
                    (((0,), (0,)), ((), ())),
                    preferred_element_type=jnp.float32,
                )
            )
    act_grad = grad_padded[:, 1:-1, 1:-1, :].reshape(images_here, pixels, GROUPS, group_size)
    sig_pre = jax.nn.sigmoid(pre_act)
    pre_grad = act_grad * sig_pre * (1.0 + pre_act * (1.0 - sig_pre))
    norm_grad = pre_grad * back_gain.astype(jnp.float32).reshape(1, 1, GROUPS, group_size)
    grad_mean = jnp.mean(norm_grad, axis=(1, 3), keepdims=True)
    cross_mean = jnp.mean(norm_grad * normed, axis=(1, 3), keepdims=True)
    in_grad = (
        ((norm_grad - grad_mean - normed * cross_mean) * inv_std)
        .astype(jnp.bfloat16)
        .reshape(images_here, side_cells, side_cells, channels)
    )
    rep_size = lax.axis_size("rep")
    fsdp_size = lax.axis_size("fsdp")
    grad_scale = 1.0 / math.sqrt(images_here * rep_size * fsdp_size * pixels)
    weight_term = jnp.concatenate(weight_list, axis=0) * grad_scale
    bias_term = jnp.sum(grad_rows.astype(jnp.float32), axis=0) * grad_scale
    gain_term = jnp.sum(pre_grad * normed, axis=(0, 1)).reshape(channels) * grad_scale
    shift_term = jnp.sum(pre_grad, axis=(0, 1)).reshape(channels) * grad_scale
    shards = (
        lax.psum_scatter(weight_term, "fsdp", scatter_dimension=0, tiled=True),
        lax.psum_scatter(bias_term, "fsdp", scatter_dimension=0, tiled=True),
        lax.psum_scatter(gain_term, "fsdp", scatter_dimension=0, tiled=True),
        lax.psum_scatter(shift_term, "fsdp", scatter_dimension=0, tiled=True),
    )
    weight_grad, bias_grad, gain_grad, shift_grad = lax.psum(
        (shards[0], shards[1], shards[2], shards[3]), "rep"
    )
    return (conv_out, in_grad, weight_grad, bias_grad, gain_grad, shift_grad)


def solution(mesh):
    placed = (
        P(("rep", "fsdp"), None, None, None),
        P(("rep", "fsdp"), None, None, None),
        P("fsdp", None),
        P("fsdp"),
        P("fsdp"),
        P("fsdp"),
    )
    out_placed = (
        P(("rep", "fsdp"), None, None, None),
        P(("rep", "fsdp"), None, None, None),
        P("fsdp", None),
        P("fsdp"),
        P("fsdp"),
        P("fsdp"),
    )

    def run(features, out_grad, conv_weight, *vectors):
        images, side, _, chans = features.shape
        rows, outs = conv_weight.shape
        shape = dict(mesh.shape)
        fast = fits(shape, images, rows // shape["fsdp"], chans, outs, side)
        return jax.shard_map(
            local_fast if fast else local,
            mesh=mesh,
            in_specs=placed,
            out_specs=out_placed,
            check_vma=False,
        )(features, out_grad, conv_weight, *vectors)

    return run
```

```python
import functools
import math

import jax
import jax.numpy as jnp
from jax import lax
from jax.experimental import pallas as pl
from jax.experimental.pallas import tpu as pltpu
from jax.sharding import PartitionSpec as P

GROUPS = 16


epsilon = 1e-05

F32 = jnp.float32
BF16 = jnp.bfloat16
VMEM = pl.BlockSpec(memory_space=pltpu.VMEM)
SMEM = pl.BlockSpec(memory_space=pltpu.SMEM)
ANY = pl.BlockSpec(memory_space=pl.ANY)


def params(mib=10):
    return pltpu.CompilerParams(vmem_limit_bytes=mib * 1024 * 1024)


def call(kernel, operands, in_specs, tokens=(), token=False, **options):
    given, after = len(operands), len(operands) + len(tokens)
    if token:
        out_shape, out_specs = options["out_shape"], options["out_specs"]
        if not isinstance(out_shape, tuple):
            out_shape, out_specs = (out_shape,), (out_specs,)
        options["out_shape"] = out_shape + (struct((1, 128), F32),)
        options["out_specs"] = out_specs + (VMEM,)
    outs = len(options["out_shape"]) - 1 if token else 0

    def body(*refs):
        refs = refs[:given] + refs[after:]
        if token:
            at = given + outs
            refs[at][...] = jnp.zeros_like(refs[at])
            refs = refs[:at] + refs[at + 1 :]
        kernel(*refs)

    return pl.pallas_call(
        body, in_specs=list(in_specs) + [VMEM] * len(tokens), **options
    )(*operands, *tokens)


def struct(shape, dtype):
    return jax.ShapeDtypeStruct(shape, dtype)


def shifted_copies(x, side, out_ref, first):
    pixels = x.shape[0]
    column = lax.broadcasted_iota(jnp.int32, x.shape, 0) % side
    edge = jnp.zeros((side, x.shape[1]), BF16)
    for kx in range(3):
        move = (kx - 1) if first else (1 - kx)
        if move == 0:
            moved = x
        elif move == 1:
            moved = jnp.where(column == side - 1, 0.0, pltpu.roll(x, pixels - 1, 0))
        else:
            moved = jnp.where(column == 0, 0.0, pltpu.roll(x, 1, 0))
        out_ref[kx, 0:side, :] = edge
        out_ref[kx, side : side + pixels, :] = moved.astype(BF16)
        out_ref[kx, side + pixels : 2 * side + pixels, :] = edge


def shift_kernel(side, x_ref, out_ref, sum_ref):
    x = x_ref[...].astype(F32)
    sum_ref[...] = jnp.sum(x, axis=0, keepdims=True)
    shifted_copies(x, side, out_ref, False)


def shift_grad(x, side, tokens):
    pixels, chans = x.shape
    return call(
        functools.partial(shift_kernel, side),
        (x,),
        [VMEM],
        tokens,
        out_shape=(
            struct((3, pixels + 2 * side, chans), BF16),
            struct((1, chans), F32),
        ),
        out_specs=(VMEM, VMEM),
        compiler_params=params(),
        cost_estimate=pl.CostEstimate(
            flops=8 * x.size, bytes_accessed=8 * x.size, transcendentals=0
        ),
        name="shift_grad",
    )


def group_means(sums, pixels):
    chans = sums.shape[1]
    size = chans // GROUPS
    lanes = round_up(GROUPS, 128)
    channel = lax.broadcasted_iota(jnp.int32, (chans, lanes), 0)
    first = lax.broadcasted_iota(jnp.int32, (chans, lanes), 1) * size
    member = jnp.where((channel >= first) & (channel < first + size), 1.0, 0.0).astype(F32)
    exact = {"preferred_element_type": F32, "precision": lax.Precision.HIGHEST}
    total = jnp.dot(sums, member, **exact)
    spread = lax.dot_general(total, member, (((1,), (1,)), ((), ())), **exact)
    return spread * (1.0 / (pixels * size))


def stats_kernel(x_ref, out_ref):
    pixels = x_ref.shape[0]
    x = x_ref[...].astype(F32)
    spread = (8, x.shape[1])
    column_sum = jnp.sum(x, axis=0, keepdims=True)
    mean = group_means(jnp.broadcast_to(column_sum, spread), pixels)[0:1]
    centered = x - mean
    column_sum = jnp.sum(centered * centered, axis=0, keepdims=True)
    var = group_means(jnp.broadcast_to(column_sum, spread), pixels)[0:1]
    out_ref[0:1, :] = mean
    out_ref[1:2, :] = lax.rsqrt(var + epsilon)


def stats(x):
    return pl.pallas_call(
        stats_kernel,
        out_shape=struct((2, x.shape[1]), F32),
        in_specs=[VMEM],
        out_specs=VMEM,
        compiler_params=params(),
        cost_estimate=pl.CostEstimate(
            flops=5 * x.size, bytes_accessed=2 * x.size, transcendentals=0
        ),
        name="norm_stats",
    )(x)


def activation(x_ref, stat_ref, vec_ref):
    mean, inv = stat_ref[0:1, :], stat_ref[1:2, :]
    gain = vec_ref[0:1, :].astype(F32)
    shift = vec_ref[1:2, :].astype(F32)
    pre = (x_ref[...].astype(F32) - mean) * inv * gain + shift
    return (pre / (1.0 + jnp.exp(-pre))).astype(BF16)


def act_kernel(x_ref, stat_ref, vec_ref, turned_ref):
    turned_ref[...] = activation(x_ref, stat_ref, vec_ref).T


def activate(x, stat, vecs, tokens):
    pixels, chans = x.shape
    return call(
        act_kernel,
        (x, stat, vecs),
        [VMEM, VMEM, VMEM],
        tokens,
        True,
        out_shape=struct((chans, pixels), BF16),
        out_specs=VMEM,
        compiler_params=params(),
        cost_estimate=pl.CostEstimate(
            flops=10 * x.size, bytes_accessed=4 * x.size, transcendentals=2 * x.size
        ),
        name="activate",
    )


def weight_blocks(side, extra, blocks, core, own_t, sib_t, own_g, sib_g, first, count, block_ref):
    chans, pixels = own_t.shape

    def tap_rows(ref, tap):
        start = pl.multiple_of((2 - tap // 3) * side, side)
        return ref[tap % 3, pl.ds(start, pixels), first : first + count]

    def product(low, high, tap):
        return jnp.dot(
            own_t[low:high, :], tap_rows(own_g, tap), preferred_element_type=F32
        ) + jnp.dot(sib_t[low:high, :], tap_rows(sib_g, tap), preferred_element_type=F32)

    for k in range(blocks):
        low, high = 2 * extra * k, 2 * extra * (k + 1)
        block_ref[0 : chans - low, :] = product(low, chans, 2 * k + core)
        block_ref[chans - low : chans + 2 * extra, :] = product(0, high, 2 * k + 1 + core)
        yield k


def weight_by_rep_kernel(
    side, extra, first, piece, place_ref, own_t, sib_t, own_g, sib_g,
    keep_ref, send0_ref, send1_ref, block_ref,
):
    chans = own_t.shape[0]
    r, z, core = place_ref[0], place_ref[1], place_ref[2]
    half, count = keep_ref.shape[2], keep_ref.shape[4]
    reps = 2 * keep_ref.shape[1]
    step = (chans + extra - piece) // (reps - 1)

    def rows_of(rel):
        at = pl.multiple_of(extra * core + step * (r ^ rel), 16)
        return block_ref[pl.ds(at, piece), :]

    for k in weight_blocks(
        side, extra, 2 * half, core, own_t, sib_t, own_g, sib_g, first, count, block_ref
    ):
        rel_z = k ^ z
        path, slot = rel_z // half, rel_z % half
        keep_ref[path, 0, slot] = rows_of(0)

        @pl.when(path == 0)
        def _():
            send0_ref[0, slot] = rows_of(1).astype(BF16)
            keep_ref[0, 1, slot] = rows_of(2)
            send0_ref[1, slot] = rows_of(3).astype(BF16)

        @pl.when(path == 1)
        def _():
            send1_ref[0, slot] = rows_of(2).astype(BF16)
            keep_ref[1, 1, slot] = rows_of(1)
            send1_ref[1, slot] = rows_of(3).astype(BF16)


def weight_call(kernel, out_shape, place, operands, extra, first, count, blocks, tokens, name):
    chans, pixels = operands[0].shape
    return call(
        kernel,
        (place,) + operands,
        [SMEM, VMEM, VMEM, VMEM, VMEM],
        tokens,
        True,
        out_shape=out_shape,
        out_specs=(VMEM,) * len(out_shape),
        scratch_shapes=[pltpu.VMEM((chans + 2 * extra, count), F32)],
        compiler_params=params(12),
        cost_estimate=pl.CostEstimate(
            flops=4 * blocks * (chans + 2 * extra) * pixels * count,
            bytes_accessed=20 * chans * pixels,
            transcendentals=0,
        ),
        name=name,
    )


def weight_by_rep(place, operands, side, blocks, extra, piece, first, count, tokens):
    half = blocks // 2
    out_shape = (
        struct((2, 2, half, piece, count), F32),
        struct((2, half, piece, count), BF16),
        struct((2, half, piece, count), BF16),
    )
    kernel = functools.partial(weight_by_rep_kernel, side, extra, first, piece)
    return weight_call(
        kernel, out_shape, place, operands, extra, first, count, blocks, tokens, "weight_grad_rep"
    )


def finish_kernel(bias_ref, param_ref, *refs):
    out_ref = refs[-1]
    total = refs[0][...]
    for ref in refs[1:-1]:
        total = total + ref[...].astype(F32)
    piece = total.shape[0]
    out_ref[0:piece, :] = total.astype(BF16)
    small = jnp.concatenate([bias_ref[...], param_ref[...]], axis=0)
    high = small.astype(BF16).astype(F32)
    middle = (small - high).astype(BF16).astype(F32)
    parts = [high, middle, small - high - middle]
    spare = out_ref.shape[0] - piece - 3 * small.shape[0]
    parts.append(jnp.zeros((spare, small.shape[1]), F32))
    out_ref[piece:, :] = jnp.concatenate(parts, axis=0).astype(BF16)


def finish(terms, small):
    piece, outs = terms[0].shape
    return call(
        finish_kernel,
        (*small, *terms),
        [VMEM] * (2 + len(terms)),
        (),
        True,
        out_shape=struct((piece + 16, outs), BF16),
        out_specs=VMEM,
        compiler_params=params(8),
        cost_estimate=pl.CostEstimate(
            flops=4 * terms[0].size, bytes_accessed=12 * terms[0].size, transcendentals=0
        ),
        name="finish_sum",
    )


def add_small_kernel(piece, *refs):
    out_ref = refs[-1]
    count = out_ref.shape[0]
    terms = []
    for ref in refs[:-1]:
        rows = ref[piece:, :].astype(F32)
        terms.append(rows[0:count] + rows[count : 2 * count] + rows[2 * count : 3 * count])
    out_ref[...] = tree_sum(terms)


def add_small_of(pieces, piece, count, tokens):
    return call(
        functools.partial(add_small_kernel, piece),
        pieces,
        [VMEM] * len(pieces),
        tokens,
        out_shape=struct((count, pieces[0].shape[1]), F32),
        out_specs=VMEM,
        compiler_params=params(4),
        cost_estimate=pl.CostEstimate(
            flops=4 * pieces[0].size, bytes_accessed=4 * pieces[0].size, transcendentals=0
        ),
        name="add_small_of",
    )


def rep_step_kernel(keep_ref, got0, got1, next0, next1):
    next0[...] = (keep_ref[0, 1] + got0[1].astype(F32)).astype(BF16)
    next1[...] = (keep_ref[1, 1] + got1[1].astype(F32)).astype(BF16)


def rep_step(keep, got0, got1, tokens):
    out = struct(keep.shape[2:], BF16)
    return call(
        rep_step_kernel,
        (keep, got0, got1),
        [VMEM] * 3,
        tokens,
        out_shape=(out, out),
        out_specs=(VMEM, VMEM),
        compiler_params=params(12),
        cost_estimate=pl.CostEstimate(
            flops=keep.size, bytes_accessed=4 * keep.size, transcendentals=0
        ),
        name="rep_step",
    )


def rep_sum_kernel(keep_ref, got0, got1, last0, last1, own_ref, *sends):
    half = keep_ref.shape[2]
    for i, out in enumerate((own_ref,) + sends):
        path, slot = i // half, i % half
        got, last = ((got0, last0), (got1, last1))[path]
        total = keep_ref[path, 0, slot] + got[0, slot].astype(F32) + last[slot].astype(F32)
        out[...] = total.astype(out.dtype)


def rep_sum(keep, got0, got1, last0, last1, tokens):
    half, piece, count = keep.shape[2:]
    return call(
        rep_sum_kernel,
        (keep, got0, got1, last0, last1),
        [VMEM] * 5,
        tokens,
        True,
        out_shape=(struct((piece, count), F32),)
        + (struct((piece, count), BF16),) * (2 * half - 1),
        out_specs=(VMEM,) * (2 * half),
        compiler_params=params(12),
        cost_estimate=pl.CostEstimate(
            flops=keep.size, bytes_accessed=4 * keep.size, transcendentals=0
        ),
        name="rep_sum",
    )


def prepare_kernel(side, x_ref, stat_ref, vec_ref, shifted_ref):
    act = activation(x_ref, stat_ref, vec_ref)
    shifted_copies(act.astype(F32), side, shifted_ref, True)


def prepare(x, stat, vecs, side, tokens):
    pixels, chans = x.shape
    return call(
        functools.partial(prepare_kernel, side),
        (x, stat, vecs),
        [VMEM] * 3,
        tokens,
        out_shape=struct((3, pixels + 2 * side, chans), BF16),
        out_specs=VMEM,
        compiler_params=params(16),
        cost_estimate=pl.CostEstimate(
            flops=20 * x.size, bytes_accessed=8 * x.size, transcendentals=2 * x.size
        ),
        name="prepare",
    )


def arrange_kernel(source, out_ref, sems):
    rows, outs = out_ref.shape[0] // 3, source.shape[1]
    copies = [
        pltpu.make_async_copy(
            source.at[pl.ds(tap * rows, rows), :],
            out_ref.at[pl.ds(tap % 3 * rows, rows), pl.ds(tap // 3 * outs, outs)],
            sems.at[tap],
        )
        for tap in range(9)
    ]
    for c in copies:
        c.start()
    for c in copies:
        c.wait()


def arrange(weight):
    rows, outs = weight.shape
    return call(
        arrange_kernel,
        (weight,),
        [ANY],
        out_shape=struct((rows // 3, 3 * outs), BF16),
        out_specs=VMEM,
        scratch_shapes=[pltpu.SemaphoreType.DMA((9,))],
        compiler_params=params(44),
        cost_estimate=pl.CostEstimate(
            flops=0, bytes_accessed=4 * weight.size, transcendentals=0
        ),
        name="arrange_weight",
    )


def grad_kernel(
    side, chunk, raw_ref, x_ref, stat_ref, vec_ref, weight, out_ref, sum_ref, scaled, g_ref
):
    pixels, chans = x_ref.shape
    edge = jnp.zeros((side, raw_ref.shape[1]), BF16)
    g_ref[0:side, :] = edge
    g_ref[side : side + pixels, :] = raw_ref[...]
    g_ref[side + pixels :, :] = edge
    column = lax.broadcasted_iota(jnp.int32, (chunk, chans), 0) % side
    mean, inv = stat_ref[0:1, :], stat_ref[1:2, :]
    gain = vec_ref[0:1, :].astype(F32)
    shift = vec_ref[1:2, :].astype(F32)
    sum_ref[...] = jnp.zeros_like(sum_ref)

    @pl.loop(0, pixels // chunk)
    def _(i):
        rows_of = [
            g_ref[pl.ds(pl.multiple_of(i * chunk + (2 - ky) * side, side), chunk), :]
            for ky in range(3)
        ]
        total = lax.dot_general(
            jnp.concatenate(rows_of, axis=1),
            weight[...],
            (((1,), (1,)), ((), ())),
            preferred_element_type=F32,
        )
        before, same, later = (total[:, kx * chans : (kx + 1) * chans] for kx in range(3))
        total = (
            same
            + jnp.where(column == side - 1, 0.0, pltpu.roll(before, chunk - 1, 0))
            + jnp.where(column == 0, 0.0, pltpu.roll(later, 1, 0))
        )
        rows = pl.ds(pl.multiple_of(i * chunk, chunk), chunk)
        normed = (x_ref[rows, :].astype(F32) - mean) * inv
        pre = normed * gain + shift
        sig = 1.0 / (1.0 + jnp.exp(-pre))
        pre_grad = total * sig * (1.0 + pre * (1.0 - sig))
        sum_ref[0:1, :] += jnp.sum(pre_grad * normed, axis=0, keepdims=True)
        sum_ref[1:2, :] += jnp.sum(pre_grad, axis=0, keepdims=True)
        scaled[rows, :] = pre_grad * gain

    rest = jnp.zeros((6, chans), F32)
    means = group_means(jnp.concatenate([sum_ref[...] * gain, rest], axis=0), pixels)
    cross, center = means[0:1], means[1:2]

    @pl.loop(0, pixels // 128)
    def _(i):
        rows = pl.ds(pl.multiple_of(i * 128, 128), 128)
        normed = (x_ref[rows, :].astype(F32) - mean) * inv
        out_ref[rows, :] = ((scaled[rows, :] - center - normed * cross) * inv).astype(BF16)


def act_grad(g, x, stat, vecs, weight, side, tokens):
    pixels, chans = x.shape
    outs = g.shape[1]
    return call(
        functools.partial(grad_kernel, side, pixels // 2),
        (g, x, stat, vecs, weight),
        [VMEM] * 5,
        tokens,
        out_shape=(struct((pixels, chans), BF16), struct((2, chans), F32)),
        out_specs=(VMEM, VMEM),
        scratch_shapes=[
            pltpu.VMEM((pixels, chans), F32),
            pltpu.VMEM((pixels + 2 * side, outs), BF16),
        ],
        compiler_params=params(24),
        cost_estimate=pl.CostEstimate(
            flops=18 * chans * outs * pixels,
            bytes_accessed=18 * chans * outs + 12 * pixels * chans,
            transcendentals=2 * pixels * chans,
        ),
        name="act_grad",
    )


def conv_kernel(side, first, a_ref, vec_ref, weight, *rest):
    out_ref, token_ref, held, sem = rest[-4:]
    token_ref[...] = jnp.zeros_like(token_ref)
    count, outs = held.shape
    pixels = out_ref.shape[0]
    low, high = max(0, first - side), min(pixels, first + count + side)
    shifted = jnp.concatenate([a_ref[kx, side + low : side + high, :] for kx in range(3)], axis=1)
    parts = jnp.dot(shifted, weight[...], preferred_element_type=F32)
    total = None
    for ky in range(3):
        begin = first + (ky - 1) * side
        end = begin + count
        part = parts[max(begin, 0) - low : min(end, pixels) - low, ky * outs : (ky + 1) * outs]
        edge = jnp.zeros((side, outs), F32)
        if begin < 0:
            part = jnp.concatenate([edge, part], axis=0)
        if end > pixels:
            part = jnp.concatenate([part, edge], axis=0)
        total = part if total is None else total + part
    held[...] = (total + vec_ref[2:3, :].astype(F32)).astype(BF16)
    copy = pltpu.make_async_copy(held, out_ref.at[pl.ds(first, count), :], sem)
    copy.start()
    copy.wait()


def conv(shifted, vecs, weight, side, first, count, before, tokens):
    chans = shifted.shape[2]
    pixels = shifted.shape[1] - 2 * side
    outs = weight.shape[1] // 3
    operands = (shifted, vecs, weight) + (() if before is None else (before,))
    return call(
        functools.partial(conv_kernel, side, first),
        operands,
        [VMEM] * 3 + [ANY] * (len(operands) - 3),
        tokens,
        out_shape=(struct((pixels, outs), BF16), struct((1, 128), F32)),
        out_specs=(ANY, VMEM),
        input_output_aliases={} if before is None else {3: 0},
        scratch_shapes=[pltpu.VMEM((count, outs), BF16), pltpu.SemaphoreType.DMA],
        compiler_params=params(24),
        cost_estimate=pl.CostEstimate(
            flops=18 * chans * outs * count,
            bytes_accessed=18 * chans * outs + 4 * count * chans,
            transcendentals=0,
        ),
        name="conv_forward",
    )


def join_kernel(scale, piece, place_ref, p0, p1, p2, p3, out_ref):
    r = place_ref[0]
    pieces = (p0, p1, p2, p3)
    step = (out_ref.shape[0] - piece) // (len(pieces) - 1)
    for q in range(len(pieces)):
        for rel, ref in enumerate(pieces):

            @pl.when((q ^ r) == rel)
            def _():
                out_ref[step * q : step * q + piece, :] = ref[0:piece, :].astype(F32) * scale


def join(place, pieces, rows, piece, scale, tokens):
    outs = pieces[0].shape[1]
    return call(
        functools.partial(join_kernel, scale, piece),
        (place, *pieces),
        [SMEM] + [VMEM] * 4,
        tokens,
        True,
        out_shape=struct((rows, outs), F32),
        out_specs=VMEM,
        compiler_params=params(),
        cost_estimate=pl.CostEstimate(
            flops=rows * outs, bytes_accessed=6 * rows * outs, transcendentals=0
        ),
        name="join_pieces",
    )


def tree_sum(terms):
    while len(terms) > 1:
        terms = [terms[i] + terms[i + 1] for i in range(0, len(terms), 2)]
    return terms[0]


def add_kernel(*refs):
    refs[-1][...] = tree_sum([ref[...] for ref in refs[:-1]])


def add_small(terms, tokens):
    return call(
        add_kernel,
        terms,
        [VMEM] * len(terms),
        tokens,
        out_shape=struct(terms[0].shape, F32),
        out_specs=VMEM,
        compiler_params=params(2),
        cost_estimate=pl.CostEstimate(
            flops=4 * terms[0].size, bytes_accessed=16 * terms[0].size, transcendentals=0
        ),
        name="add_small",
    )


def swap(x, axis, mask):
    n = lax.axis_size(axis)
    return lax.ppermute(x, axis, [(i, i ^ mask) for i in range(n)])


def gather_small(x):
    at = lax.axis_index("fsdp")
    other = swap(x, "fsdp", 1)
    pair = jnp.where(at % 2 == 1, jnp.stack([other, x]), jnp.stack([x, other]))
    got = [pair] + [swap(pair, "fsdp", m) for m in range(2, lax.axis_size("fsdp"), 2)]
    mask = 1
    while mask < len(got):
        flip = (at // (2 * mask)) % 2 == 1
        got = [jnp.where(flip, got[i ^ mask], got[i]) for i in range(len(got))]
        mask *= 2
    return jnp.concatenate(got)


def sum_all(x, axis, masks):
    return tree_sum([x] + [swap(x, axis, m) for m in masks])


def local_fast(features, out_grad, conv_weight, conv_bias, norm_gain, norm_shift):
    side = features.shape[1]
    chans = features.shape[3]
    outs = out_grad.shape[3]
    pixels = side * side
    rows = conv_weight.shape[0]
    reps, shards = lax.axis_size("rep"), lax.axis_size("fsdp")
    r, f = lax.axis_index("rep"), lax.axis_index("fsdp")
    z, core = f // 2, f % 2
    extra = rows - chans
    piece = round_up(-(-rows // reps), 16)
    x = features.reshape(pixels, chans)
    g = out_grad.reshape(pixels, outs)
    place = jnp.stack([r, z, core]).astype(jnp.int32)

    weight = lax.all_gather(conv_weight, "fsdp", axis=0, tiled=True)
    small = gather_small(jnp.stack([norm_gain, norm_shift, conv_bias]))
    sib_g = swap(g, "fsdp", 1)

    stat = stats(x)
    vecs = jnp.transpose(small, (1, 0, 2)).reshape(3, chans)
    own_t, act_token = activate(x, stat, vecs, ())
    sib_t = swap(own_t, "fsdp", 1)
    own_shifted, bias_sum = shift_grad(g, side, (act_token,))
    sib_shifted, _ = shift_grad(sib_g, side, (act_token,))
    operands = (own_t, sib_t, own_shifted, sib_shifted)

    keep, send0, send1, weight_token = weight_by_rep(
        place, operands, side, shards // 2, extra, piece, 0, outs, ()
    )
    got0 = swap(send0, "rep", 1)
    got1 = swap(send1, "rep", 2)
    next0, next1 = rep_step(keep, got0, got1, ())
    last0 = swap(next0, "rep", 2)
    last1 = swap(next1, "rep", 1)
    own_sum, *sends, sum_token = rep_sum(keep, got0, got1, last0, last1, ())
    got = [swap(a, "fsdp", 2 * (m + 1)) for m, a in enumerate(sends)]
    act_shifted = prepare(x, stat, vecs, side, (weight_token,))
    weight = arrange(weight)
    in_grad, param_sums = act_grad(g, x, stat, vecs, weight, side, (sum_token,))
    done, done_token = finish((own_sum, *got), (bias_sum, param_sums))
    pieces_done = [done] + [swap(done, "rep", m) for m in range(1, reps)]

    conv_out, token = conv(act_shifted, vecs, weight, side, 0, pixels, None, (done_token,))
    small_sums = add_small_of(pieces_done, piece, 3, (token,))
    over_z = [small_sums] + [swap(small_sums, "fsdp", m) for m in range(2, shards, 2)]
    scale = 1.0 / math.sqrt(reps * shards * pixels)
    weight_grad, token = join(place, pieces_done, rows, piece, scale, (token,))
    small_sums = sum_all(add_small(over_z, (token,)), "fsdp", (1,)) * scale
    share = outs // shards
    mine = lax.dynamic_slice_in_dim(small_sums.reshape(3, shards, share), f, 1, axis=1)
    mine = mine.reshape(3, share)
    return (
        conv_out.reshape(1, side, side, outs),
        in_grad.reshape(1, side, side, chans),
        weight_grad,
        mine[0],
        mine[1],
        mine[2],
    )


def round_up(n, m):
    return -(-n // m) * m


def fits(mesh_shape, images, rows, chans, outs, side):
    reps, shards = mesh_shape["rep"], mesh_shape["fsdp"]
    if images != reps * shards or reps != 2 * 2 or shards != 9 - 1:
        return False
    if chans != outs or rows * shards != 9 * chans or chans % 128 or side % 16 or outs < 3 * 128:
        return False
    extra, piece = rows - chans, round_up(-(-rows // reps), 16)
    step = (rows - piece) // (reps - 1)
    return (
        extra % 16 == 0
        and step * (reps - 1) == rows - piece
        and step % 16 == 0
        and piece % 32 == 0
    )


def local(features, out_grad, conv_weight, conv_bias, norm_gain, norm_shift):
    images_here = features.shape[0]
    side_cells = features.shape[1]
    channels = features.shape[3]
    pixels = side_cells * side_cells
    group_size = channels // GROUPS
    full_weight, bias_all, gain_all, shift_all = (
        lax.all_gather(conv_weight, "fsdp", axis=0, tiled=True),
        lax.all_gather(conv_bias, "fsdp", axis=0, tiled=True),
        lax.all_gather(norm_gain, "fsdp", axis=0, tiled=True),
        lax.all_gather(norm_shift, "fsdp", axis=0, tiled=True),
    )
    out_chans = full_weight.shape[1]
    values = features.astype(jnp.float32).reshape(images_here, pixels, GROUPS, group_size)
    group_mean = jnp.mean(values, axis=(1, 3), keepdims=True)
    centered = values - group_mean
    group_var = jnp.mean(centered * centered, axis=(1, 3), keepdims=True)
    inv_std = lax.rsqrt(group_var + epsilon)
    normed = centered * inv_std
    gain_cols = gain_all.astype(jnp.float32).reshape(1, 1, GROUPS, group_size)
    shift_cols = shift_all.astype(jnp.float32).reshape(1, 1, GROUPS, group_size)
    pre_act = normed * gain_cols + shift_cols
    activated = (
        jax.nn.silu(pre_act)
        .astype(jnp.bfloat16)
        .reshape(images_here, side_cells, side_cells, channels)
    )
    padded = jnp.pad(activated, ((0, 0), (1, 1), (1, 1), (0, 0)))
    conv_sum = jnp.zeros((images_here * pixels, out_chans), jnp.float32)
    taps_list = []
    for row_off in range(3):
        for col_off in range(3):
            tap_index = 3 * row_off + col_off
            tap_piece = padded[
                :, row_off : row_off + side_cells, col_off : col_off + side_cells, :
            ].reshape(images_here * pixels, channels)
            taps_list.append(tap_piece)
            conv_sum = conv_sum + jnp.dot(
                tap_piece,
                full_weight[tap_index * channels : (tap_index + 1) * channels],
                preferred_element_type=jnp.float32,
            )
    conv_out = (
        (conv_sum + bias_all.astype(jnp.float32)[None, :])
        .astype(jnp.bfloat16)
        .reshape(images_here, side_cells, side_cells, out_chans)
    )
    back_weight, back_gain = (
        lax.all_gather(conv_weight, "fsdp", axis=0, tiled=True),
        lax.all_gather(norm_gain, "fsdp", axis=0, tiled=True),
    )
    grad_rows = out_grad.reshape(images_here * pixels, out_chans)
    grad_padded = jnp.zeros((images_here, side_cells + 2, side_cells + 2, channels), jnp.float32)
    weight_list = []
    for row_off in range(3):
        for col_off in range(3):
            tap_index = 3 * row_off + col_off
            tap_rows = back_weight[tap_index * channels : (tap_index + 1) * channels]
            tap_grad = lax.dot_general(
                grad_rows, tap_rows, (((1,), (1,)), ((), ())), preferred_element_type=jnp.float32
            )
            grad_padded = grad_padded.at[
                :, row_off : row_off + side_cells, col_off : col_off + side_cells, :
            ].add(tap_grad.reshape(images_here, side_cells, side_cells, channels))
            weight_list.append(
                lax.dot_general(
                    taps_list[tap_index],
                    grad_rows,
                    (((0,), (0,)), ((), ())),
                    preferred_element_type=jnp.float32,
                )
            )
    act_grad = grad_padded[:, 1:-1, 1:-1, :].reshape(images_here, pixels, GROUPS, group_size)
    sig_pre = jax.nn.sigmoid(pre_act)
    pre_grad = act_grad * sig_pre * (1.0 + pre_act * (1.0 - sig_pre))
    norm_grad = pre_grad * back_gain.astype(jnp.float32).reshape(1, 1, GROUPS, group_size)
    grad_mean = jnp.mean(norm_grad, axis=(1, 3), keepdims=True)
    cross_mean = jnp.mean(norm_grad * normed, axis=(1, 3), keepdims=True)
    in_grad = (
        ((norm_grad - grad_mean - normed * cross_mean) * inv_std)
        .astype(jnp.bfloat16)
        .reshape(images_here, side_cells, side_cells, channels)
    )
    rep_size = lax.axis_size("rep")
    fsdp_size = lax.axis_size("fsdp")
    grad_scale = 1.0 / math.sqrt(images_here * rep_size * fsdp_size * pixels)
    weight_term = jnp.concatenate(weight_list, axis=0) * grad_scale
    bias_term = jnp.sum(grad_rows.astype(jnp.float32), axis=0) * grad_scale
    gain_term = jnp.sum(pre_grad * normed, axis=(0, 1)).reshape(channels) * grad_scale
    shift_term = jnp.sum(pre_grad, axis=(0, 1)).reshape(channels) * grad_scale
    shards = (
        lax.psum_scatter(weight_term, "fsdp", scatter_dimension=0, tiled=True),
        lax.psum_scatter(bias_term, "fsdp", scatter_dimension=0, tiled=True),
        lax.psum_scatter(gain_term, "fsdp", scatter_dimension=0, tiled=True),
        lax.psum_scatter(shift_term, "fsdp", scatter_dimension=0, tiled=True),
    )
    weight_grad, bias_grad, gain_grad, shift_grad = lax.psum(
        (shards[0], shards[1], shards[2], shards[3]), "rep"
    )
    return (conv_out, in_grad, weight_grad, bias_grad, gain_grad, shift_grad)


def solution(mesh):
    placed = (
        P(("rep", "fsdp"), None, None, None),
        P(("rep", "fsdp"), None, None, None),
        P("fsdp", None),
        P("fsdp"),
        P("fsdp"),
        P("fsdp"),
    )
    out_placed = (
        P(("rep", "fsdp"), None, None, None),
        P(("rep", "fsdp"), None, None, None),
        P("fsdp", None),
        P("fsdp"),
        P("fsdp"),
        P("fsdp"),
    )

    def run(features, out_grad, conv_weight, *vectors):
        images, side, _, chans = features.shape
        rows, outs = conv_weight.shape
        shape = dict(mesh.shape)
        fast = fits(shape, images, rows // shape["fsdp"], chans, outs, side)
        return jax.shard_map(
            local_fast if fast else local,
            mesh=mesh,
            in_specs=placed,
            out_specs=out_placed,
            check_vma=False,
        )(features, out_grad, conv_weight, *vectors)

    return run
```

```python
import functools
import math

import jax
import jax.numpy as jnp
from jax import lax
from jax.experimental import pallas as pl
from jax.experimental.pallas import tpu as pltpu
from jax.sharding import PartitionSpec as P

GROUPS = 16


epsilon = 1e-05

F32 = jnp.float32
BF16 = jnp.bfloat16
VMEM = pl.BlockSpec(memory_space=pltpu.VMEM)
SMEM = pl.BlockSpec(memory_space=pltpu.SMEM)
ANY = pl.BlockSpec(memory_space=pl.ANY)


def params(mib=10):
    return pltpu.CompilerParams(vmem_limit_bytes=mib * 1024 * 1024)


def call(kernel, operands, in_specs, tokens=(), token=False, **options):
    given, after = len(operands), len(operands) + len(tokens)
    if token:
        out_shape, out_specs = options["out_shape"], options["out_specs"]
        if not isinstance(out_shape, tuple):
            out_shape, out_specs = (out_shape,), (out_specs,)
        options["out_shape"] = out_shape + (struct((1, 128), F32),)
        options["out_specs"] = out_specs + (VMEM,)
    outs = len(options["out_shape"]) - 1 if token else 0

    def body(*refs):
        refs = refs[:given] + refs[after:]
        if token:
            at = given + outs
            refs[at][...] = jnp.zeros_like(refs[at])
            refs = refs[:at] + refs[at + 1 :]
        kernel(*refs)

    return pl.pallas_call(
        body, in_specs=list(in_specs) + [VMEM] * len(tokens), **options
    )(*operands, *tokens)


def struct(shape, dtype):
    return jax.ShapeDtypeStruct(shape, dtype)


def shifted_copies(x, side, out_ref, first):
    pixels = x.shape[0]
    column = lax.broadcasted_iota(jnp.int32, x.shape, 0) % side
    edge = jnp.zeros((side, x.shape[1]), BF16)
    for kx in range(3):
        move = (kx - 1) if first else (1 - kx)
        if move == 0:
            moved = x
        elif move == 1:
            moved = jnp.where(column == side - 1, 0.0, pltpu.roll(x, pixels - 1, 0))
        else:
            moved = jnp.where(column == 0, 0.0, pltpu.roll(x, 1, 0))
        out_ref[kx, 0:side, :] = edge
        out_ref[kx, side : side + pixels, :] = moved.astype(BF16)
        out_ref[kx, side + pixels : 2 * side + pixels, :] = edge


def shift_kernel(side, x_ref, out_ref, sum_ref):
    x = x_ref[...].astype(F32)
    sum_ref[...] = jnp.sum(x, axis=0, keepdims=True)
    shifted_copies(x, side, out_ref, False)


def shift_grad(x, side, tokens):
    pixels, chans = x.shape
    return call(
        functools.partial(shift_kernel, side),
        (x,),
        [VMEM],
        tokens,
        out_shape=(
            struct((3, pixels + 2 * side, chans), BF16),
            struct((1, chans), F32),
        ),
        out_specs=(VMEM, VMEM),
        compiler_params=params(),
        cost_estimate=pl.CostEstimate(
            flops=8 * x.size, bytes_accessed=8 * x.size, transcendentals=0
        ),
        name="shift_grad",
    )


def group_means(sums, pixels):
    chans = sums.shape[1]
    size = chans // GROUPS
    lanes = round_up(GROUPS, 128)
    channel = lax.broadcasted_iota(jnp.int32, (chans, lanes), 0)
    first = lax.broadcasted_iota(jnp.int32, (chans, lanes), 1) * size
    member = jnp.where((channel >= first) & (channel < first + size), 1.0, 0.0).astype(F32)
    exact = {"preferred_element_type": F32, "precision": lax.Precision.HIGHEST}
    total = jnp.dot(sums, member, **exact)
    spread = lax.dot_general(total, member, (((1,), (1,)), ((), ())), **exact)
    return spread * (1.0 / (pixels * size))


def stats_kernel(x_ref, out_ref):
    pixels = x_ref.shape[0]
    x = x_ref[...].astype(F32)
    spread = (8, x.shape[1])
    column_sum = jnp.sum(x, axis=0, keepdims=True)
    mean = group_means(jnp.broadcast_to(column_sum, spread), pixels)[0:1]
    centered = x - mean
    column_sum = jnp.sum(centered * centered, axis=0, keepdims=True)
    var = group_means(jnp.broadcast_to(column_sum, spread), pixels)[0:1]
    out_ref[0:1, :] = mean
    out_ref[1:2, :] = lax.rsqrt(var + epsilon)


def stats(x):
    return pl.pallas_call(
        stats_kernel,
        out_shape=struct((2, x.shape[1]), F32),
        in_specs=[VMEM],
        out_specs=VMEM,
        compiler_params=params(),
        cost_estimate=pl.CostEstimate(
            flops=5 * x.size, bytes_accessed=2 * x.size, transcendentals=0
        ),
        name="norm_stats",
    )(x)


def activation(x_ref, stat_ref, vec_ref):
    mean, inv = stat_ref[0:1, :], stat_ref[1:2, :]
    gain = vec_ref[0:1, :].astype(F32)
    shift = vec_ref[1:2, :].astype(F32)
    pre = (x_ref[...].astype(F32) - mean) * inv * gain + shift
    return (pre / (1.0 + jnp.exp(-pre))).astype(BF16)


def act_kernel(x_ref, stat_ref, vec_ref, turned_ref):
    turned_ref[...] = activation(x_ref, stat_ref, vec_ref).T


def activate(x, stat, vecs, tokens):
    pixels, chans = x.shape
    return call(
        act_kernel,
        (x, stat, vecs),
        [VMEM, VMEM, VMEM],
        tokens,
        True,
        out_shape=struct((chans, pixels), BF16),
        out_specs=VMEM,
        compiler_params=params(),
        cost_estimate=pl.CostEstimate(
            flops=10 * x.size, bytes_accessed=4 * x.size, transcendentals=2 * x.size
        ),
        name="activate",
    )


def weight_blocks(side, extra, blocks, core, own_t, sib_t, own_g, sib_g, first, count, block_ref):
    chans, pixels = own_t.shape

    def tap_rows(ref, tap):
        start = pl.multiple_of((2 - tap // 3) * side, side)
        return ref[tap % 3, pl.ds(start, pixels), first : first + count]

    def product(low, high, tap):
        return jnp.dot(
            own_t[low:high, :], tap_rows(own_g, tap), preferred_element_type=F32
        ) + jnp.dot(sib_t[low:high, :], tap_rows(sib_g, tap), preferred_element_type=F32)

    for k in range(blocks):
        low, high = 2 * extra * k, 2 * extra * (k + 1)
        block_ref[0 : chans - low, :] = product(low, chans, 2 * k + core)
        block_ref[chans - low : chans + 2 * extra, :] = product(0, high, 2 * k + 1 + core)
        yield k


def weight_by_rep_kernel(
    side, extra, first, piece, place_ref, own_t, sib_t, own_g, sib_g,
    keep_ref, send0_ref, send1_ref, block_ref,
):
    chans = own_t.shape[0]
    r, z, core = place_ref[0], place_ref[1], place_ref[2]
    half, count = keep_ref.shape[2], keep_ref.shape[4]
    reps = 2 * keep_ref.shape[1]
    step = (chans + extra - piece) // (reps - 1)

    def rows_of(rel):
        at = extra * core + step * (r ^ rel)
        past = at % 8
        rows = block_ref[pl.ds(pl.multiple_of(at - past, 8), piece + piece % 8), :]
        return jnp.where(past == 0, rows[:piece], rows[piece % 8 :])

    for k in weight_blocks(
        side, extra, 2 * half, core, own_t, sib_t, own_g, sib_g, first, count, block_ref
    ):
        rel_z = k ^ z
        path, slot = rel_z // half, rel_z % half
        keep_ref[path, 0, slot] = rows_of(0)

        @pl.when(path == 0)
        def _():
            send0_ref[0, slot] = rows_of(1).astype(BF16)
            keep_ref[0, 1, slot] = rows_of(2)
            send0_ref[1, slot] = rows_of(3).astype(BF16)

        @pl.when(path == 1)
        def _():
            send1_ref[0, slot] = rows_of(2).astype(BF16)
            keep_ref[1, 1, slot] = rows_of(1)
            send1_ref[1, slot] = rows_of(3).astype(BF16)


def weight_call(kernel, out_shape, place, operands, extra, first, count, blocks, tokens, name):
    chans, pixels = operands[0].shape
    return call(
        kernel,
        (place,) + operands,
        [SMEM, VMEM, VMEM, VMEM, VMEM],
        tokens,
        True,
        out_shape=out_shape,
        out_specs=(VMEM,) * len(out_shape),
        scratch_shapes=[pltpu.VMEM((chans + 2 * extra, count), F32)],
        compiler_params=params(12),
        cost_estimate=pl.CostEstimate(
            flops=4 * blocks * (chans + 2 * extra) * pixels * count,
            bytes_accessed=20 * chans * pixels,
            transcendentals=0,
        ),
        name=name,
    )


def weight_by_rep(place, operands, side, blocks, extra, piece, first, count, tokens):
    half = blocks // 2
    out_shape = (
        struct((2, 2, half, piece, count), F32),
        struct((2, half, piece, count), BF16),
        struct((2, half, piece, count), BF16),
    )
    kernel = functools.partial(weight_by_rep_kernel, side, extra, first, piece)
    return weight_call(
        kernel, out_shape, place, operands, extra, first, count, blocks, tokens, "weight_grad_rep"
    )


def finish_kernel(bias_ref, param_ref, *refs):
    out_ref = refs[-1]
    total = refs[0][...]
    for ref in refs[1:-1]:
        total = total + ref[...].astype(F32)
    piece = total.shape[0]
    head = out_ref.shape[0] - piece
    out_ref[head:, :] = total.astype(BF16)
    small = jnp.concatenate([bias_ref[...], param_ref[...]], axis=0)
    high = small.astype(BF16).astype(F32)
    middle = (small - high).astype(BF16).astype(F32)
    parts = [high, middle, small - high - middle]
    spare = head - 3 * small.shape[0]
    parts.append(jnp.zeros((spare, small.shape[1]), F32))
    out_ref[0:head, :] = jnp.concatenate(parts, axis=0).astype(BF16)


def finish(terms, small):
    piece, outs = terms[0].shape
    return call(
        finish_kernel,
        (*small, *terms),
        [VMEM] * (2 + len(terms)),
        (),
        True,
        out_shape=struct((piece + 16, outs), BF16),
        out_specs=VMEM,
        compiler_params=params(8),
        cost_estimate=pl.CostEstimate(
            flops=4 * terms[0].size, bytes_accessed=12 * terms[0].size, transcendentals=0
        ),
        name="finish_sum",
    )


def add_small_kernel(piece, *refs):
    out_ref = refs[-1]
    count = out_ref.shape[0]
    terms = []
    for ref in refs[:-1]:
        rows = ref[0 : ref.shape[0] - piece, :].astype(F32)
        terms.append(rows[0:count] + rows[count : 2 * count] + rows[2 * count : 3 * count])
    out_ref[...] = tree_sum(terms)


def add_small_of(pieces, piece, count, tokens):
    return call(
        functools.partial(add_small_kernel, piece),
        pieces,
        [VMEM] * len(pieces),
        tokens,
        out_shape=struct((count, pieces[0].shape[1]), F32),
        out_specs=VMEM,
        compiler_params=params(4),
        cost_estimate=pl.CostEstimate(
            flops=4 * pieces[0].size, bytes_accessed=4 * pieces[0].size, transcendentals=0
        ),
        name="add_small_of",
    )


def rep_step_kernel(keep_ref, got0, got1, next0, next1):
    next0[...] = (keep_ref[0, 1] + got0[1].astype(F32)).astype(BF16)
    next1[...] = (keep_ref[1, 1] + got1[1].astype(F32)).astype(BF16)


def rep_step(keep, got0, got1, tokens):
    out = struct(keep.shape[2:], BF16)
    return call(
        rep_step_kernel,
        (keep, got0, got1),
        [VMEM] * 3,
        tokens,
        out_shape=(out, out),
        out_specs=(VMEM, VMEM),
        compiler_params=params(12),
        cost_estimate=pl.CostEstimate(
            flops=keep.size, bytes_accessed=4 * keep.size, transcendentals=0
        ),
        name="rep_step",
    )


def rep_sum_kernel(keep_ref, got0, got1, last0, last1, own_ref, *sends):
    half = keep_ref.shape[2]
    for i, out in enumerate((own_ref,) + sends):
        path, slot = i // half, i % half
        got, last = ((got0, last0), (got1, last1))[path]
        total = keep_ref[path, 0, slot] + got[0, slot].astype(F32) + last[slot].astype(F32)
        out[...] = total.astype(out.dtype)


def rep_sum(keep, got0, got1, last0, last1, tokens):
    half, piece, count = keep.shape[2:]
    return call(
        rep_sum_kernel,
        (keep, got0, got1, last0, last1),
        [VMEM] * 5,
        tokens,
        True,
        out_shape=(struct((piece, count), F32),)
        + (struct((piece, count), BF16),) * (2 * half - 1),
        out_specs=(VMEM,) * (2 * half),
        compiler_params=params(12),
        cost_estimate=pl.CostEstimate(
            flops=keep.size, bytes_accessed=4 * keep.size, transcendentals=0
        ),
        name="rep_sum",
    )


def prepare_kernel(side, x_ref, stat_ref, vec_ref, shifted_ref):
    act = activation(x_ref, stat_ref, vec_ref)
    shifted_copies(act.astype(F32), side, shifted_ref, True)


def prepare(x, stat, vecs, side, tokens):
    pixels, chans = x.shape
    return call(
        functools.partial(prepare_kernel, side),
        (x, stat, vecs),
        [VMEM] * 3,
        tokens,
        out_shape=struct((3, pixels + 2 * side, chans), BF16),
        out_specs=VMEM,
        compiler_params=params(16),
        cost_estimate=pl.CostEstimate(
            flops=20 * x.size, bytes_accessed=8 * x.size, transcendentals=2 * x.size
        ),
        name="prepare",
    )


def arrange_kernel(source, out_ref, sems):
    rows, outs = out_ref.shape[0] // 3, source.shape[1]
    copies = [
        pltpu.make_async_copy(
            source.at[pl.ds(tap * rows, rows), :],
            out_ref.at[pl.ds(tap % 3 * rows, rows), pl.ds(tap // 3 * outs, outs)],
            sems.at[tap],
        )
        for tap in range(9)
    ]
    for c in copies:
        c.start()
    for c in copies:
        c.wait()


def arrange(weight):
    rows, outs = weight.shape
    return call(
        arrange_kernel,
        (weight,),
        [ANY],
        out_shape=struct((rows // 3, 3 * outs), BF16),
        out_specs=VMEM,
        scratch_shapes=[pltpu.SemaphoreType.DMA((9,))],
        compiler_params=params(44),
        cost_estimate=pl.CostEstimate(
            flops=0, bytes_accessed=4 * weight.size, transcendentals=0
        ),
        name="arrange_weight",
    )


def grad_kernel(
    side, chunk, raw_ref, x_ref, stat_ref, vec_ref, weight, out_ref, sum_ref, scaled, g_ref
):
    pixels, chans = x_ref.shape
    edge = jnp.zeros((side, raw_ref.shape[1]), BF16)
    g_ref[0:side, :] = edge
    g_ref[side : side + pixels, :] = raw_ref[...]
    g_ref[side + pixels :, :] = edge
    column = lax.broadcasted_iota(jnp.int32, (chunk, chans), 0) % side
    mean, inv = stat_ref[0:1, :], stat_ref[1:2, :]
    gain = vec_ref[0:1, :].astype(F32)
    shift = vec_ref[1:2, :].astype(F32)
    sum_ref[...] = jnp.zeros_like(sum_ref)

    @pl.loop(0, pixels // chunk)
    def _(i):
        rows_of = [
            g_ref[pl.ds(pl.multiple_of(i * chunk + (2 - ky) * side, side), chunk), :]
            for ky in range(3)
        ]
        total = lax.dot_general(
            jnp.concatenate(rows_of, axis=1),
            weight[...],
            (((1,), (1,)), ((), ())),
            preferred_element_type=F32,
        )
        before, same, later = (total[:, kx * chans : (kx + 1) * chans] for kx in range(3))
        total = (
            same
            + jnp.where(column == side - 1, 0.0, pltpu.roll(before, chunk - 1, 0))
            + jnp.where(column == 0, 0.0, pltpu.roll(later, 1, 0))
        )
        rows = pl.ds(pl.multiple_of(i * chunk, chunk), chunk)
        normed = (x_ref[rows, :].astype(F32) - mean) * inv
        pre = normed * gain + shift
        sig = 1.0 / (1.0 + jnp.exp(-pre))
        pre_grad = total * sig * (1.0 + pre * (1.0 - sig))
        sum_ref[0:1, :] += jnp.sum(pre_grad * normed, axis=0, keepdims=True)
        sum_ref[1:2, :] += jnp.sum(pre_grad, axis=0, keepdims=True)
        scaled[rows, :] = pre_grad * gain

    rest = jnp.zeros((6, chans), F32)
    means = group_means(jnp.concatenate([sum_ref[...] * gain, rest], axis=0), pixels)
    cross, center = means[0:1], means[1:2]

    @pl.loop(0, pixels // 128)
    def _(i):
        rows = pl.ds(pl.multiple_of(i * 128, 128), 128)
        normed = (x_ref[rows, :].astype(F32) - mean) * inv
        out_ref[rows, :] = ((scaled[rows, :] - center - normed * cross) * inv).astype(BF16)


def act_grad(g, x, stat, vecs, weight, side, tokens):
    pixels, chans = x.shape
    outs = g.shape[1]
    return call(
        functools.partial(grad_kernel, side, pixels),
        (g, x, stat, vecs, weight),
        [VMEM] * 5,
        tokens,
        out_shape=(struct((pixels, chans), BF16), struct((2, chans), F32)),
        out_specs=(VMEM, VMEM),
        scratch_shapes=[
            pltpu.VMEM((pixels, chans), F32),
            pltpu.VMEM((pixels + 2 * side, outs), BF16),
        ],
        compiler_params=params(32),
        cost_estimate=pl.CostEstimate(
            flops=18 * chans * outs * pixels,
            bytes_accessed=18 * chans * outs + 12 * pixels * chans,
            transcendentals=2 * pixels * chans,
        ),
        name="act_grad",
    )


def conv_kernel(side, first, a_ref, vec_ref, weight, *rest):
    out_ref, token_ref, held, sem = rest[-4:]
    token_ref[...] = jnp.zeros_like(token_ref)
    count, outs = held.shape
    pixels = out_ref.shape[0]
    low, high = max(0, first - side), min(pixels, first + count + side)
    shifted = jnp.concatenate([a_ref[kx, side + low : side + high, :] for kx in range(3)], axis=1)
    parts = jnp.dot(shifted, weight[...], preferred_element_type=F32)
    total = None
    for ky in range(3):
        begin = first + (ky - 1) * side
        end = begin + count
        part = parts[max(begin, 0) - low : min(end, pixels) - low, ky * outs : (ky + 1) * outs]
        edge = jnp.zeros((side, outs), F32)
        if begin < 0:
            part = jnp.concatenate([edge, part], axis=0)
        if end > pixels:
            part = jnp.concatenate([part, edge], axis=0)
        total = part if total is None else total + part
    held[...] = (total + vec_ref[2:3, :].astype(F32)).astype(BF16)
    copy = pltpu.make_async_copy(held, out_ref.at[pl.ds(first, count), :], sem)
    copy.start()
    copy.wait()


def conv(shifted, vecs, weight, side, first, count, before, tokens):
    chans = shifted.shape[2]
    pixels = shifted.shape[1] - 2 * side
    outs = weight.shape[1] // 3
    operands = (shifted, vecs, weight) + (() if before is None else (before,))
    return call(
        functools.partial(conv_kernel, side, first),
        operands,
        [VMEM] * 3 + [ANY] * (len(operands) - 3),
        tokens,
        out_shape=(struct((pixels, outs), BF16), struct((1, 128), F32)),
        out_specs=(ANY, VMEM),
        input_output_aliases={} if before is None else {3: 0},
        scratch_shapes=[pltpu.VMEM((count, outs), BF16), pltpu.SemaphoreType.DMA],
        compiler_params=params(24),
        cost_estimate=pl.CostEstimate(
            flops=18 * chans * outs * count,
            bytes_accessed=18 * chans * outs + 4 * count * chans,
            transcendentals=0,
        ),
        name="conv_forward",
    )


def join_kernel(scale, piece, place_ref, p0, p1, p2, p3, out_ref):
    r = place_ref[0]
    pieces = (p0, p1, p2, p3)
    step = (out_ref.shape[0] - piece) // (len(pieces) - 1)
    for q in range(len(pieces)):
        for rel, ref in enumerate(pieces):

            @pl.when((q ^ r) == rel)
            def _():
                out_ref[step * q : step * q + piece, :] = ref[ref.shape[0] - piece :, :].astype(F32) * scale


def join(place, pieces, rows, piece, scale, tokens):
    outs = pieces[0].shape[1]
    return call(
        functools.partial(join_kernel, scale, piece),
        (place, *pieces),
        [SMEM] + [VMEM] * 4,
        tokens,
        True,
        out_shape=struct((rows, outs), F32),
        out_specs=VMEM,
        compiler_params=params(),
        cost_estimate=pl.CostEstimate(
            flops=rows * outs, bytes_accessed=6 * rows * outs, transcendentals=0
        ),
        name="join_pieces",
    )


def tree_sum(terms):
    while len(terms) > 1:
        terms = [terms[i] + terms[i + 1] for i in range(0, len(terms), 2)]
    return terms[0]


def add_kernel(*refs):
    refs[-1][...] = tree_sum([ref[...] for ref in refs[:-1]])


def add_small(terms, tokens):
    return call(
        add_kernel,
        terms,
        [VMEM] * len(terms),
        tokens,
        out_shape=struct(terms[0].shape, F32),
        out_specs=VMEM,
        compiler_params=params(2),
        cost_estimate=pl.CostEstimate(
            flops=4 * terms[0].size, bytes_accessed=16 * terms[0].size, transcendentals=0
        ),
        name="add_small",
    )


def swap(x, axis, mask):
    n = lax.axis_size(axis)
    return lax.ppermute(x, axis, [(i, i ^ mask) for i in range(n)])


def gather_small(x):
    at = lax.axis_index("fsdp")
    other = swap(x, "fsdp", 1)
    pair = jnp.where(at % 2 == 1, jnp.stack([other, x]), jnp.stack([x, other]))
    got = [pair] + [swap(pair, "fsdp", m) for m in range(2, lax.axis_size("fsdp"), 2)]
    mask = 1
    while mask < len(got):
        flip = (at // (2 * mask)) % 2 == 1
        got = [jnp.where(flip, got[i ^ mask], got[i]) for i in range(len(got))]
        mask *= 2
    return jnp.concatenate(got)


def sum_all(x, axis, masks):
    return tree_sum([x] + [swap(x, axis, m) for m in masks])


def local_fast(features, out_grad, conv_weight, conv_bias, norm_gain, norm_shift):
    side = features.shape[1]
    chans = features.shape[3]
    outs = out_grad.shape[3]
    pixels = side * side
    rows = conv_weight.shape[0]
    reps, shards = lax.axis_size("rep"), lax.axis_size("fsdp")
    r, f = lax.axis_index("rep"), lax.axis_index("fsdp")
    z, core = f // 2, f % 2
    extra = rows - chans
    piece = -(-rows // reps)
    x = features.reshape(pixels, chans)
    g = out_grad.reshape(pixels, outs)
    place = jnp.stack([r, z, core]).astype(jnp.int32)

    weight = lax.all_gather(conv_weight, "fsdp", axis=0, tiled=True)
    small = gather_small(jnp.stack([norm_gain, norm_shift, conv_bias]))
    sib_g = swap(g, "fsdp", 1)

    stat = stats(x)
    vecs = jnp.transpose(small, (1, 0, 2)).reshape(3, chans)
    own_t, act_token = activate(x, stat, vecs, ())
    sib_t = swap(own_t, "fsdp", 1)
    own_shifted, bias_sum = shift_grad(g, side, (act_token,))
    sib_shifted, _ = shift_grad(sib_g, side, (act_token,))
    operands = (own_t, sib_t, own_shifted, sib_shifted)

    keep, send0, send1, weight_token = weight_by_rep(
        place, operands, side, shards // 2, extra, piece, 0, outs, ()
    )
    got0 = swap(send0, "rep", 1)
    got1 = swap(send1, "rep", 2)
    next0, next1 = rep_step(keep, got0, got1, ())
    last0 = swap(next0, "rep", 2)
    last1 = swap(next1, "rep", 1)
    own_sum, *sends, sum_token = rep_sum(keep, got0, got1, last0, last1, ())
    got = [swap(a, "fsdp", 2 * (m + 1)) for m, a in enumerate(sends)]
    act_shifted = prepare(x, stat, vecs, side, (weight_token,))
    weight = arrange(weight)
    in_grad, param_sums = act_grad(g, x, stat, vecs, weight, side, (sum_token,))
    done, done_token = finish((own_sum, *got), (bias_sum, param_sums))
    pieces_done = [done] + [swap(done, "rep", m) for m in range(1, reps)]

    conv_out, token = conv(act_shifted, vecs, weight, side, 0, pixels, None, (done_token,))
    small_sums = add_small_of(pieces_done, piece, 3, (token,))
    over_z = [small_sums] + [swap(small_sums, "fsdp", m) for m in range(2, shards, 2)]
    scale = 1.0 / math.sqrt(reps * shards * pixels)
    weight_grad, token = join(place, pieces_done, rows, piece, scale, (token,))
    small_sums = sum_all(add_small(over_z, (token,)), "fsdp", (1,)) * scale
    share = outs // shards
    mine = lax.dynamic_slice_in_dim(small_sums.reshape(3, shards, share), f, 1, axis=1)
    mine = mine.reshape(3, share)
    return (
        conv_out.reshape(1, side, side, outs),
        in_grad.reshape(1, side, side, chans),
        weight_grad,
        mine[0],
        mine[1],
        mine[2],
    )


def round_up(n, m):
    return -(-n // m) * m


def fits(mesh_shape, images, rows, chans, outs, side):
    reps, shards = mesh_shape["rep"], mesh_shape["fsdp"]
    if images != reps * shards or reps != 2 * 2 or shards != 9 - 1:
        return False
    if chans != outs or rows * shards != 9 * chans or chans % 128 or side % 16 or outs < 3 * 128:
        return False
    extra, piece = rows - chans, -(-rows // reps)
    step = (rows - piece) // (reps - 1)
    return (
        extra % 16 == 0
        and step * (reps - 1) == rows - piece
        and step == piece
        and piece % 8 in (0, 4)
        and extra % 8 == 0
    )


def local(features, out_grad, conv_weight, conv_bias, norm_gain, norm_shift):
    images_here = features.shape[0]
    side_cells = features.shape[1]
    channels = features.shape[3]
    pixels = side_cells * side_cells
    group_size = channels // GROUPS
    full_weight, bias_all, gain_all, shift_all = (
        lax.all_gather(conv_weight, "fsdp", axis=0, tiled=True),
        lax.all_gather(conv_bias, "fsdp", axis=0, tiled=True),
        lax.all_gather(norm_gain, "fsdp", axis=0, tiled=True),
        lax.all_gather(norm_shift, "fsdp", axis=0, tiled=True),
    )
    out_chans = full_weight.shape[1]
    values = features.astype(jnp.float32).reshape(images_here, pixels, GROUPS, group_size)
    group_mean = jnp.mean(values, axis=(1, 3), keepdims=True)
    centered = values - group_mean
    group_var = jnp.mean(centered * centered, axis=(1, 3), keepdims=True)
    inv_std = lax.rsqrt(group_var + epsilon)
    normed = centered * inv_std
    gain_cols = gain_all.astype(jnp.float32).reshape(1, 1, GROUPS, group_size)
    shift_cols = shift_all.astype(jnp.float32).reshape(1, 1, GROUPS, group_size)
    pre_act = normed * gain_cols + shift_cols
    activated = (
        jax.nn.silu(pre_act)
        .astype(jnp.bfloat16)
        .reshape(images_here, side_cells, side_cells, channels)
    )
    padded = jnp.pad(activated, ((0, 0), (1, 1), (1, 1), (0, 0)))
    conv_sum = jnp.zeros((images_here * pixels, out_chans), jnp.float32)
    taps_list = []
    for row_off in range(3):
        for col_off in range(3):
            tap_index = 3 * row_off + col_off
            tap_piece = padded[
                :, row_off : row_off + side_cells, col_off : col_off + side_cells, :
            ].reshape(images_here * pixels, channels)
            taps_list.append(tap_piece)
            conv_sum = conv_sum + jnp.dot(
                tap_piece,
                full_weight[tap_index * channels : (tap_index + 1) * channels],
                preferred_element_type=jnp.float32,
            )
    conv_out = (
        (conv_sum + bias_all.astype(jnp.float32)[None, :])
        .astype(jnp.bfloat16)
        .reshape(images_here, side_cells, side_cells, out_chans)
    )
    back_weight, back_gain = (
        lax.all_gather(conv_weight, "fsdp", axis=0, tiled=True),
        lax.all_gather(norm_gain, "fsdp", axis=0, tiled=True),
    )
    grad_rows = out_grad.reshape(images_here * pixels, out_chans)
    grad_padded = jnp.zeros((images_here, side_cells + 2, side_cells + 2, channels), jnp.float32)
    weight_list = []
    for row_off in range(3):
        for col_off in range(3):
            tap_index = 3 * row_off + col_off
            tap_rows = back_weight[tap_index * channels : (tap_index + 1) * channels]
            tap_grad = lax.dot_general(
                grad_rows, tap_rows, (((1,), (1,)), ((), ())), preferred_element_type=jnp.float32
            )
            grad_padded = grad_padded.at[
                :, row_off : row_off + side_cells, col_off : col_off + side_cells, :
            ].add(tap_grad.reshape(images_here, side_cells, side_cells, channels))
            weight_list.append(
                lax.dot_general(
                    taps_list[tap_index],
                    grad_rows,
                    (((0,), (0,)), ((), ())),
                    preferred_element_type=jnp.float32,
                )
            )
    act_grad = grad_padded[:, 1:-1, 1:-1, :].reshape(images_here, pixels, GROUPS, group_size)
    sig_pre = jax.nn.sigmoid(pre_act)
    pre_grad = act_grad * sig_pre * (1.0 + pre_act * (1.0 - sig_pre))
    norm_grad = pre_grad * back_gain.astype(jnp.float32).reshape(1, 1, GROUPS, group_size)
    grad_mean = jnp.mean(norm_grad, axis=(1, 3), keepdims=True)
    cross_mean = jnp.mean(norm_grad * normed, axis=(1, 3), keepdims=True)
    in_grad = (
        ((norm_grad - grad_mean - normed * cross_mean) * inv_std)
        .astype(jnp.bfloat16)
        .reshape(images_here, side_cells, side_cells, channels)
    )
    rep_size = lax.axis_size("rep")
    fsdp_size = lax.axis_size("fsdp")
    grad_scale = 1.0 / math.sqrt(images_here * rep_size * fsdp_size * pixels)
    weight_term = jnp.concatenate(weight_list, axis=0) * grad_scale
    bias_term = jnp.sum(grad_rows.astype(jnp.float32), axis=0) * grad_scale
    gain_term = jnp.sum(pre_grad * normed, axis=(0, 1)).reshape(channels) * grad_scale
    shift_term = jnp.sum(pre_grad, axis=(0, 1)).reshape(channels) * grad_scale
    shards = (
        lax.psum_scatter(weight_term, "fsdp", scatter_dimension=0, tiled=True),
        lax.psum_scatter(bias_term, "fsdp", scatter_dimension=0, tiled=True),
        lax.psum_scatter(gain_term, "fsdp", scatter_dimension=0, tiled=True),
        lax.psum_scatter(shift_term, "fsdp", scatter_dimension=0, tiled=True),
    )
    weight_grad, bias_grad, gain_grad, shift_grad = lax.psum(
        (shards[0], shards[1], shards[2], shards[3]), "rep"
    )
    return (conv_out, in_grad, weight_grad, bias_grad, gain_grad, shift_grad)


def solution(mesh):
    placed = (
        P(("rep", "fsdp"), None, None, None),
        P(("rep", "fsdp"), None, None, None),
        P("fsdp", None),
        P("fsdp"),
        P("fsdp"),
        P("fsdp"),
    )
    out_placed = (
        P(("rep", "fsdp"), None, None, None),
        P(("rep", "fsdp"), None, None, None),
        P("fsdp", None),
        P("fsdp"),
        P("fsdp"),
        P("fsdp"),
    )

    def run(features, out_grad, conv_weight, *vectors):
        images, side, _, chans = features.shape
        rows, outs = conv_weight.shape
        shape = dict(mesh.shape)
        fast = fits(shape, images, rows // shape["fsdp"], chans, outs, side)
        return jax.shard_map(
            local_fast if fast else local,
            mesh=mesh,
            in_specs=placed,
            out_specs=out_placed,
            check_vma=False,
        )(features, out_grad, conv_weight, *vectors)

    return run
```

```python
import functools
import math

import jax
import jax.numpy as jnp
from jax import lax
from jax.experimental import pallas as pl
from jax.experimental.pallas import tpu as pltpu
from jax.sharding import PartitionSpec as P

GROUPS = 16


epsilon = 1e-05

F32 = jnp.float32
BF16 = jnp.bfloat16
VMEM = pl.BlockSpec(memory_space=pltpu.VMEM)
SMEM = pl.BlockSpec(memory_space=pltpu.SMEM)
ANY = pl.BlockSpec(memory_space=pl.ANY)


def params(mib=10):
    return pltpu.CompilerParams(vmem_limit_bytes=mib * 1024 * 1024)


def call(kernel, operands, in_specs, tokens=(), token=False, **options):
    given, after = len(operands), len(operands) + len(tokens)
    if token:
        out_shape, out_specs = options["out_shape"], options["out_specs"]
        if not isinstance(out_shape, tuple):
            out_shape, out_specs = (out_shape,), (out_specs,)
        options["out_shape"] = out_shape + (struct((1, 128), F32),)
        options["out_specs"] = out_specs + (VMEM,)
    outs = len(options["out_shape"]) - 1 if token else 0

    def body(*refs):
        refs = refs[:given] + refs[after:]
        if token:
            at = given + outs
            refs[at][...] = jnp.zeros_like(refs[at])
            refs = refs[:at] + refs[at + 1 :]
        kernel(*refs)

    return pl.pallas_call(
        body, in_specs=list(in_specs) + [VMEM] * len(tokens), **options
    )(*operands, *tokens)


def struct(shape, dtype):
    return jax.ShapeDtypeStruct(shape, dtype)


def shifted_copies(x, side, out_ref, first):
    pixels = x.shape[0]
    column = lax.broadcasted_iota(jnp.int32, x.shape, 0) % side
    edge = jnp.zeros((side, x.shape[1]), BF16)
    for kx in range(3):
        move = (kx - 1) if first else (1 - kx)
        if move == 0:
            moved = x
        elif move == 1:
            moved = jnp.where(column == side - 1, 0.0, pltpu.roll(x, pixels - 1, 0))
        else:
            moved = jnp.where(column == 0, 0.0, pltpu.roll(x, 1, 0))
        out_ref[kx, 0:side, :] = edge
        out_ref[kx, side : side + pixels, :] = moved.astype(BF16)
        out_ref[kx, side + pixels : 2 * side + pixels, :] = edge


def shift_kernel(side, x_ref, out_ref, sum_ref):
    x = x_ref[...].astype(F32)
    sum_ref[...] = jnp.sum(x, axis=0, keepdims=True)
    shifted_copies(x, side, out_ref, False)


def shift_grad(x, side, tokens):
    pixels, chans = x.shape
    return call(
        functools.partial(shift_kernel, side),
        (x,),
        [VMEM],
        tokens,
        out_shape=(
            struct((3, pixels + 2 * side, chans), BF16),
            struct((1, chans), F32),
        ),
        out_specs=(VMEM, VMEM),
        compiler_params=params(),
        cost_estimate=pl.CostEstimate(
            flops=8 * x.size, bytes_accessed=8 * x.size, transcendentals=0
        ),
        name="shift_grad",
    )


def group_means(sums, pixels):
    chans = sums.shape[1]
    size = chans // GROUPS
    lanes = round_up(GROUPS, 128)
    channel = lax.broadcasted_iota(jnp.int32, (chans, lanes), 0)
    first = lax.broadcasted_iota(jnp.int32, (chans, lanes), 1) * size
    member = jnp.where((channel >= first) & (channel < first + size), 1.0, 0.0).astype(F32)
    exact = {"preferred_element_type": F32, "precision": lax.Precision.HIGHEST}
    total = jnp.dot(sums, member, **exact)
    spread = lax.dot_general(total, member, (((1,), (1,)), ((), ())), **exact)
    return spread * (1.0 / (pixels * size))


def stats_kernel(x_ref, out_ref):
    pixels = x_ref.shape[0]
    x = x_ref[...].astype(F32)
    spread = (8, x.shape[1])
    column_sum = jnp.sum(x, axis=0, keepdims=True)
    mean = group_means(jnp.broadcast_to(column_sum, spread), pixels)[0:1]
    centered = x - mean
    column_sum = jnp.sum(centered * centered, axis=0, keepdims=True)
    var = group_means(jnp.broadcast_to(column_sum, spread), pixels)[0:1]
    out_ref[0:1, :] = mean
    out_ref[1:2, :] = lax.rsqrt(var + epsilon)


def stats(x):
    return pl.pallas_call(
        stats_kernel,
        out_shape=struct((2, x.shape[1]), F32),
        in_specs=[VMEM],
        out_specs=VMEM,
        compiler_params=params(),
        cost_estimate=pl.CostEstimate(
            flops=5 * x.size, bytes_accessed=2 * x.size, transcendentals=0
        ),
        name="norm_stats",
    )(x)


def activation(x_ref, stat_ref, vec_ref):
    mean, inv = stat_ref[0:1, :], stat_ref[1:2, :]
    gain = vec_ref[0:1, :].astype(F32)
    shift = vec_ref[1:2, :].astype(F32)
    pre = (x_ref[...].astype(F32) - mean) * inv * gain + shift
    return (pre / (1.0 + jnp.exp(-pre))).astype(BF16)


def act_kernel(x_ref, stat_ref, vec_ref, turned_ref):
    turned_ref[...] = activation(x_ref, stat_ref, vec_ref).T


def activate(x, stat, vecs, tokens):
    pixels, chans = x.shape
    return call(
        act_kernel,
        (x, stat, vecs),
        [VMEM, VMEM, VMEM],
        tokens,
        True,
        out_shape=struct((chans, pixels), BF16),
        out_specs=VMEM,
        compiler_params=params(),
        cost_estimate=pl.CostEstimate(
            flops=10 * x.size, bytes_accessed=4 * x.size, transcendentals=2 * x.size
        ),
        name="activate",
    )


def weight_blocks(side, extra, blocks, core, own_t, sib_t, own_g, sib_g, first, count, block_ref):
    chans, pixels = own_t.shape

    def tap_rows(ref, tap):
        start = pl.multiple_of((2 - tap // 3) * side, side)
        return ref[tap % 3, pl.ds(start, pixels), first : first + count]

    def product(low, high, tap):
        return jnp.dot(
            own_t[low:high, :], tap_rows(own_g, tap), preferred_element_type=F32
        ) + jnp.dot(sib_t[low:high, :], tap_rows(sib_g, tap), preferred_element_type=F32)

    for k in range(blocks):
        low, high = 2 * extra * k, 2 * extra * (k + 1)
        block_ref[0 : chans - low, :] = product(low, chans, 2 * k + core)
        block_ref[chans - low : chans + 2 * extra, :] = product(0, high, 2 * k + 1 + core)
        yield k


def weight_by_rep_kernel(
    side, extra, first, piece, place_ref, own_t, sib_t, own_g, sib_g,
    keep_ref, send0_ref, send1_ref, block_ref,
):
    chans = own_t.shape[0]
    r, z, core = place_ref[0], place_ref[1], place_ref[2]
    half, count = keep_ref.shape[2], keep_ref.shape[4]
    reps = 2 * keep_ref.shape[1]
    step = (chans + extra - piece) // (reps - 1)

    def rows_of(rel):
        at = extra * core + step * (r ^ rel)
        past = at % 8
        rows = block_ref[pl.ds(pl.multiple_of(at - past, 8), piece + piece % 8), :]
        return jnp.where(past == 0, rows[:piece], rows[piece % 8 :])

    for k in weight_blocks(
        side, extra, 2 * half, core, own_t, sib_t, own_g, sib_g, first, count, block_ref
    ):
        rel_z = k ^ z
        path, slot = rel_z // half, rel_z % half
        keep_ref[path, 0, slot] = rows_of(0)

        @pl.when(path == 0)
        def _():
            send0_ref[0, slot] = rows_of(1).astype(BF16)
            keep_ref[0, 1, slot] = rows_of(2)
            send0_ref[1, slot] = rows_of(3).astype(BF16)

        @pl.when(path == 1)
        def _():
            send1_ref[0, slot] = rows_of(2).astype(BF16)
            keep_ref[1, 1, slot] = rows_of(1)
            send1_ref[1, slot] = rows_of(3).astype(BF16)


def weight_call(kernel, out_shape, place, operands, extra, first, count, blocks, tokens, name):
    chans, pixels = operands[0].shape
    return call(
        kernel,
        (place,) + operands,
        [SMEM, VMEM, VMEM, VMEM, VMEM],
        tokens,
        True,
        out_shape=out_shape,
        out_specs=(VMEM,) * len(out_shape),
        scratch_shapes=[pltpu.VMEM((chans + 2 * extra, count), F32)],
        compiler_params=params(12),
        cost_estimate=pl.CostEstimate(
            flops=4 * blocks * (chans + 2 * extra) * pixels * count,
            bytes_accessed=20 * chans * pixels,
            transcendentals=0,
        ),
        name=name,
    )


def weight_by_rep(place, operands, side, blocks, extra, piece, first, count, tokens):
    half = blocks // 2
    out_shape = (
        struct((2, 2, half, piece, count), F32),
        struct((2, half, piece, count), BF16),
        struct((2, half, piece, count), BF16),
    )
    kernel = functools.partial(weight_by_rep_kernel, side, extra, first, piece)
    return weight_call(
        kernel, out_shape, place, operands, extra, first, count, blocks, tokens, "weight_grad_rep"
    )


def finish_kernel(bias_ref, param_ref, *refs):
    out_ref = refs[-1]
    total = refs[0][...]
    for ref in refs[1:-1]:
        total = total + ref[...].astype(F32)
    piece = total.shape[0]
    head = 16
    rest = jnp.zeros((out_ref.shape[0] - head - piece, total.shape[1]), F32)
    out_ref[head:, :] = jnp.concatenate([total, rest], axis=0).astype(BF16)
    small = jnp.concatenate([bias_ref[...], param_ref[...]], axis=0)
    high = small.astype(BF16).astype(F32)
    middle = (small - high).astype(BF16).astype(F32)
    parts = [high, middle, small - high - middle]
    spare = head - 3 * small.shape[0]
    parts.append(jnp.zeros((spare, small.shape[1]), F32))
    out_ref[0:head, :] = jnp.concatenate(parts, axis=0).astype(BF16)


def finish(terms, small):
    piece, outs = terms[0].shape
    return call(
        finish_kernel,
        (*small, *terms),
        [VMEM] * (2 + len(terms)),
        (),
        True,
        out_shape=struct((16 + round_up(piece, 16), outs), BF16),
        out_specs=VMEM,
        compiler_params=params(8),
        cost_estimate=pl.CostEstimate(
            flops=4 * terms[0].size, bytes_accessed=12 * terms[0].size, transcendentals=0
        ),
        name="finish_sum",
    )


def add_small_kernel(piece, *refs):
    out_ref = refs[-1]
    count = out_ref.shape[0]
    terms = []
    for ref in refs[:-1]:
        rows = ref[0:16, :].astype(F32)
        terms.append(rows[0:count] + rows[count : 2 * count] + rows[2 * count : 3 * count])
    out_ref[...] = tree_sum(terms)


def add_small_of(pieces, piece, count, tokens):
    return call(
        functools.partial(add_small_kernel, piece),
        pieces,
        [VMEM] * len(pieces),
        tokens,
        out_shape=struct((count, pieces[0].shape[1]), F32),
        out_specs=VMEM,
        compiler_params=params(4),
        cost_estimate=pl.CostEstimate(
            flops=4 * pieces[0].size, bytes_accessed=4 * pieces[0].size, transcendentals=0
        ),
        name="add_small_of",
    )


def rep_step_kernel(keep_ref, got0, got1, next0, next1):
    next0[...] = (keep_ref[0, 1] + got0[1].astype(F32)).astype(BF16)
    next1[...] = (keep_ref[1, 1] + got1[1].astype(F32)).astype(BF16)


def rep_step(keep, got0, got1, tokens):
    out = struct(keep.shape[2:], BF16)
    return call(
        rep_step_kernel,
        (keep, got0, got1),
        [VMEM] * 3,
        tokens,
        out_shape=(out, out),
        out_specs=(VMEM, VMEM),
        compiler_params=params(12),
        cost_estimate=pl.CostEstimate(
            flops=keep.size, bytes_accessed=4 * keep.size, transcendentals=0
        ),
        name="rep_step",
    )


def rep_sum_kernel(keep_ref, got0, got1, last0, last1, own_ref, *sends):
    half = keep_ref.shape[2]
    for i, out in enumerate((own_ref,) + sends):
        path, slot = i // half, i % half
        got, last = ((got0, last0), (got1, last1))[path]
        total = keep_ref[path, 0, slot] + got[0, slot].astype(F32) + last[slot].astype(F32)
        out[...] = total.astype(out.dtype)


def rep_sum(keep, got0, got1, last0, last1, tokens):
    half, piece, count = keep.shape[2:]
    return call(
        rep_sum_kernel,
        (keep, got0, got1, last0, last1),
        [VMEM] * 5,
        tokens,
        True,
        out_shape=(struct((piece, count), F32),)
        + (struct((piece, count), BF16),) * (2 * half - 1),
        out_specs=(VMEM,) * (2 * half),
        compiler_params=params(12),
        cost_estimate=pl.CostEstimate(
            flops=keep.size, bytes_accessed=4 * keep.size, transcendentals=0
        ),
        name="rep_sum",
    )


def prepare_kernel(side, x_ref, stat_ref, vec_ref, shifted_ref):
    act = activation(x_ref, stat_ref, vec_ref)
    shifted_copies(act.astype(F32), side, shifted_ref, True)


def prepare(x, stat, vecs, side, tokens):
    pixels, chans = x.shape
    return call(
        functools.partial(prepare_kernel, side),
        (x, stat, vecs),
        [VMEM] * 3,
        tokens,
        out_shape=struct((3, pixels + 2 * side, chans), BF16),
        out_specs=VMEM,
        compiler_params=params(16),
        cost_estimate=pl.CostEstimate(
            flops=20 * x.size, bytes_accessed=8 * x.size, transcendentals=2 * x.size
        ),
        name="prepare",
    )


def arrange_kernel(source, out_ref, sems):
    rows, outs = out_ref.shape[0] // 3, source.shape[1]
    copies = [
        pltpu.make_async_copy(
            source.at[pl.ds(tap * rows, rows), :],
            out_ref.at[pl.ds(tap % 3 * rows, rows), pl.ds(tap // 3 * outs, outs)],
            sems.at[tap],
        )
        for tap in range(9)
    ]
    for c in copies:
        c.start()
    for c in copies:
        c.wait()


def arrange(weight):
    rows, outs = weight.shape
    return call(
        arrange_kernel,
        (weight,),
        [ANY],
        out_shape=struct((rows // 3, 3 * outs), BF16),
        out_specs=VMEM,
        scratch_shapes=[pltpu.SemaphoreType.DMA((9,))],
        compiler_params=params(44),
        cost_estimate=pl.CostEstimate(
            flops=0, bytes_accessed=4 * weight.size, transcendentals=0
        ),
        name="arrange_weight",
    )


def grad_kernel(
    side, chunk, raw_ref, x_ref, stat_ref, vec_ref, weight, out_ref, sum_ref, scaled, g_ref
):
    pixels, chans = x_ref.shape
    edge = jnp.zeros((side, raw_ref.shape[1]), BF16)
    g_ref[0:side, :] = edge
    g_ref[side : side + pixels, :] = raw_ref[...]
    g_ref[side + pixels :, :] = edge
    column = lax.broadcasted_iota(jnp.int32, (chunk, chans), 0) % side
    mean, inv = stat_ref[0:1, :], stat_ref[1:2, :]
    gain = vec_ref[0:1, :].astype(F32)
    shift = vec_ref[1:2, :].astype(F32)
    sum_ref[...] = jnp.zeros_like(sum_ref)

    @pl.loop(0, pixels // chunk)
    def _(i):
        rows_of = [
            g_ref[pl.ds(pl.multiple_of(i * chunk + (2 - ky) * side, side), chunk), :]
            for ky in range(3)
        ]
        total = lax.dot_general(
            jnp.concatenate(rows_of, axis=1),
            weight[...],
            (((1,), (1,)), ((), ())),
            preferred_element_type=F32,
        )
        before, same, later = (total[:, kx * chans : (kx + 1) * chans] for kx in range(3))
        total = (
            same
            + jnp.where(column == side - 1, 0.0, pltpu.roll(before, chunk - 1, 0))
            + jnp.where(column == 0, 0.0, pltpu.roll(later, 1, 0))
        )
        rows = pl.ds(pl.multiple_of(i * chunk, chunk), chunk)
        normed = (x_ref[rows, :].astype(F32) - mean) * inv
        pre = normed * gain + shift
        sig = 1.0 / (1.0 + jnp.exp(-pre))
        pre_grad = total * sig * (1.0 + pre * (1.0 - sig))
        sum_ref[0:1, :] += jnp.sum(pre_grad * normed, axis=0, keepdims=True)
        sum_ref[1:2, :] += jnp.sum(pre_grad, axis=0, keepdims=True)
        scaled[rows, :] = pre_grad * gain

    rest = jnp.zeros((6, chans), F32)
    means = group_means(jnp.concatenate([sum_ref[...] * gain, rest], axis=0), pixels)
    cross, center = means[0:1], means[1:2]

    @pl.loop(0, pixels // 128)
    def _(i):
        rows = pl.ds(pl.multiple_of(i * 128, 128), 128)
        normed = (x_ref[rows, :].astype(F32) - mean) * inv
        out_ref[rows, :] = ((scaled[rows, :] - center - normed * cross) * inv).astype(BF16)


def act_grad(g, x, stat, vecs, weight, side, tokens):
    pixels, chans = x.shape
    outs = g.shape[1]
    return call(
        functools.partial(grad_kernel, side, pixels),
        (g, x, stat, vecs, weight),
        [VMEM] * 5,
        tokens,
        out_shape=(struct((pixels, chans), BF16), struct((2, chans), F32)),
        out_specs=(VMEM, VMEM),
        scratch_shapes=[
            pltpu.VMEM((pixels, chans), F32),
            pltpu.VMEM((pixels + 2 * side, outs), BF16),
        ],
        compiler_params=params(32),
        cost_estimate=pl.CostEstimate(
            flops=18 * chans * outs * pixels,
            bytes_accessed=18 * chans * outs + 12 * pixels * chans,
            transcendentals=2 * pixels * chans,
        ),
        name="act_grad",
    )


def conv_kernel(side, first, a_ref, vec_ref, weight, *rest):
    out_ref, token_ref, held, sem = rest[-4:]
    token_ref[...] = jnp.zeros_like(token_ref)
    count, outs = held.shape
    pixels = out_ref.shape[0]
    low, high = max(0, first - side), min(pixels, first + count + side)
    shifted = jnp.concatenate([a_ref[kx, side + low : side + high, :] for kx in range(3)], axis=1)
    parts = jnp.dot(shifted, weight[...], preferred_element_type=F32)
    total = None
    for ky in range(3):
        begin = first + (ky - 1) * side
        end = begin + count
        part = parts[max(begin, 0) - low : min(end, pixels) - low, ky * outs : (ky + 1) * outs]
        edge = jnp.zeros((side, outs), F32)
        if begin < 0:
            part = jnp.concatenate([edge, part], axis=0)
        if end > pixels:
            part = jnp.concatenate([part, edge], axis=0)
        total = part if total is None else total + part
    held[...] = (total + vec_ref[2:3, :].astype(F32)).astype(BF16)
    copy = pltpu.make_async_copy(held, out_ref.at[pl.ds(first, count), :], sem)
    copy.start()
    copy.wait()


def conv(shifted, vecs, weight, side, first, count, before, tokens):
    chans = shifted.shape[2]
    pixels = shifted.shape[1] - 2 * side
    outs = weight.shape[1] // 3
    operands = (shifted, vecs, weight) + (() if before is None else (before,))
    return call(
        functools.partial(conv_kernel, side, first),
        operands,
        [VMEM] * 3 + [ANY] * (len(operands) - 3),
        tokens,
        out_shape=(struct((pixels, outs), BF16), struct((1, 128), F32)),
        out_specs=(ANY, VMEM),
        input_output_aliases={} if before is None else {3: 0},
        scratch_shapes=[pltpu.VMEM((count, outs), BF16), pltpu.SemaphoreType.DMA],
        compiler_params=params(24),
        cost_estimate=pl.CostEstimate(
            flops=18 * chans * outs * count,
            bytes_accessed=18 * chans * outs + 4 * count * chans,
            transcendentals=0,
        ),
        name="conv_forward",
    )


def join_kernel(scale, piece, place_ref, p0, p1, p2, p3, out_ref):
    r = place_ref[0]
    pieces = (p0, p1, p2, p3)
    step = (out_ref.shape[0] - piece) // (len(pieces) - 1)
    for q in range(len(pieces)):
        for rel, ref in enumerate(pieces):

            @pl.when((q ^ r) == rel)
            def _():
                out_ref[step * q : step * q + piece, :] = ref[16:, :].astype(F32)[:piece] * scale


def join(place, pieces, rows, piece, scale, tokens):
    outs = pieces[0].shape[1]
    return call(
        functools.partial(join_kernel, scale, piece),
        (place, *pieces),
        [SMEM] + [VMEM] * 4,
        tokens,
        True,
        out_shape=struct((rows, outs), F32),
        out_specs=VMEM,
        compiler_params=params(),
        cost_estimate=pl.CostEstimate(
            flops=rows * outs, bytes_accessed=6 * rows * outs, transcendentals=0
        ),
        name="join_pieces",
    )


def tree_sum(terms):
    while len(terms) > 1:
        terms = [terms[i] + terms[i + 1] for i in range(0, len(terms), 2)]
    return terms[0]


def add_kernel(*refs):
    refs[-1][...] = tree_sum([ref[...] for ref in refs[:-1]])


def add_small(terms, tokens):
    return call(
        add_kernel,
        terms,
        [VMEM] * len(terms),
        tokens,
        out_shape=struct(terms[0].shape, F32),
        out_specs=VMEM,
        compiler_params=params(2),
        cost_estimate=pl.CostEstimate(
            flops=4 * terms[0].size, bytes_accessed=16 * terms[0].size, transcendentals=0
        ),
        name="add_small",
    )


def swap(x, axis, mask):
    n = lax.axis_size(axis)
    return lax.ppermute(x, axis, [(i, i ^ mask) for i in range(n)])


def gather_small(x):
    at = lax.axis_index("fsdp")
    other = swap(x, "fsdp", 1)
    pair = jnp.where(at % 2 == 1, jnp.stack([other, x]), jnp.stack([x, other]))
    got = [pair] + [swap(pair, "fsdp", m) for m in range(2, lax.axis_size("fsdp"), 2)]
    mask = 1
    while mask < len(got):
        flip = (at // (2 * mask)) % 2 == 1
        got = [jnp.where(flip, got[i ^ mask], got[i]) for i in range(len(got))]
        mask *= 2
    return jnp.concatenate(got)


def sum_all(x, axis, masks):
    return tree_sum([x] + [swap(x, axis, m) for m in masks])


def local_fast(features, out_grad, conv_weight, conv_bias, norm_gain, norm_shift):
    side = features.shape[1]
    chans = features.shape[3]
    outs = out_grad.shape[3]
    pixels = side * side
    rows = conv_weight.shape[0]
    reps, shards = lax.axis_size("rep"), lax.axis_size("fsdp")
    r, f = lax.axis_index("rep"), lax.axis_index("fsdp")
    z, core = f // 2, f % 2
    extra = rows - chans
    piece = -(-rows // reps)
    x = features.reshape(pixels, chans)
    g = out_grad.reshape(pixels, outs)
    place = jnp.stack([r, z, core]).astype(jnp.int32)

    weight = lax.all_gather(conv_weight, "fsdp", axis=0, tiled=True)
    small = gather_small(jnp.stack([norm_gain, norm_shift, conv_bias]))
    sib_g = swap(g, "fsdp", 1)

    stat = stats(x)
    vecs = jnp.transpose(small, (1, 0, 2)).reshape(3, chans)
    own_t, act_token = activate(x, stat, vecs, ())
    sib_t = swap(own_t, "fsdp", 1)
    own_shifted, bias_sum = shift_grad(g, side, (act_token,))
    sib_shifted, _ = shift_grad(sib_g, side, (act_token,))
    operands = (own_t, sib_t, own_shifted, sib_shifted)

    keep, send0, send1, weight_token = weight_by_rep(
        place, operands, side, shards // 2, extra, piece, 0, outs, ()
    )
    got0 = swap(send0, "rep", 1)
    got1 = swap(send1, "rep", 2)
    next0, next1 = rep_step(keep, got0, got1, ())
    last0 = swap(next0, "rep", 2)
    last1 = swap(next1, "rep", 1)
    own_sum, *sends, sum_token = rep_sum(keep, got0, got1, last0, last1, ())
    got = [swap(a, "fsdp", 2 * (m + 1)) for m, a in enumerate(sends)]
    act_shifted = prepare(x, stat, vecs, side, (weight_token,))
    weight = arrange(weight)
    in_grad, param_sums = act_grad(g, x, stat, vecs, weight, side, (sum_token,))
    done, done_token = finish((own_sum, *got), (bias_sum, param_sums))
    pieces_done = [done] + [swap(done, "rep", m) for m in range(1, reps)]

    conv_out, token = conv(act_shifted, vecs, weight, side, 0, pixels, None, (done_token,))
    small_sums = add_small_of(pieces_done, piece, 3, (token,))
    over_z = [small_sums] + [swap(small_sums, "fsdp", m) for m in range(2, shards, 2)]
    scale = 1.0 / math.sqrt(reps * shards * pixels)
    weight_grad, token = join(place, pieces_done, rows, piece, scale, (token,))
    small_sums = sum_all(add_small(over_z, (token,)), "fsdp", (1,)) * scale
    share = outs // shards
    mine = lax.dynamic_slice_in_dim(small_sums.reshape(3, shards, share), f, 1, axis=1)
    mine = mine.reshape(3, share)
    return (
        conv_out.reshape(1, side, side, outs),
        in_grad.reshape(1, side, side, chans),
        weight_grad,
        mine[0],
        mine[1],
        mine[2],
    )


def round_up(n, m):
    return -(-n // m) * m


def fits(mesh_shape, images, rows, chans, outs, side):
    reps, shards = mesh_shape["rep"], mesh_shape["fsdp"]
    if images != reps * shards or reps != 2 * 2 or shards != 9 - 1:
        return False
    if chans != outs or rows * shards != 9 * chans or chans % 128 or side % 16 or outs < 3 * 128:
        return False
    extra, piece = rows - chans, -(-rows // reps)
    step = (rows - piece) // (reps - 1)
    return (
        extra % 16 == 0
        and step * (reps - 1) == rows - piece
        and step == piece
        and piece % 8 in (0, 4)
        and extra % 8 == 0
    )


def local(features, out_grad, conv_weight, conv_bias, norm_gain, norm_shift):
    images_here = features.shape[0]
    side_cells = features.shape[1]
    channels = features.shape[3]
    pixels = side_cells * side_cells
    group_size = channels // GROUPS
    full_weight, bias_all, gain_all, shift_all = (
        lax.all_gather(conv_weight, "fsdp", axis=0, tiled=True),
        lax.all_gather(conv_bias, "fsdp", axis=0, tiled=True),
        lax.all_gather(norm_gain, "fsdp", axis=0, tiled=True),
        lax.all_gather(norm_shift, "fsdp", axis=0, tiled=True),
    )
    out_chans = full_weight.shape[1]
    values = features.astype(jnp.float32).reshape(images_here, pixels, GROUPS, group_size)
    group_mean = jnp.mean(values, axis=(1, 3), keepdims=True)
    centered = values - group_mean
    group_var = jnp.mean(centered * centered, axis=(1, 3), keepdims=True)
    inv_std = lax.rsqrt(group_var + epsilon)
    normed = centered * inv_std
    gain_cols = gain_all.astype(jnp.float32).reshape(1, 1, GROUPS, group_size)
    shift_cols = shift_all.astype(jnp.float32).reshape(1, 1, GROUPS, group_size)
    pre_act = normed * gain_cols + shift_cols
    activated = (
        jax.nn.silu(pre_act)
        .astype(jnp.bfloat16)
        .reshape(images_here, side_cells, side_cells, channels)
    )
    padded = jnp.pad(activated, ((0, 0), (1, 1), (1, 1), (0, 0)))
    conv_sum = jnp.zeros((images_here * pixels, out_chans), jnp.float32)
    taps_list = []
    for row_off in range(3):
        for col_off in range(3):
            tap_index = 3 * row_off + col_off
            tap_piece = padded[
                :, row_off : row_off + side_cells, col_off : col_off + side_cells, :
            ].reshape(images_here * pixels, channels)
            taps_list.append(tap_piece)
            conv_sum = conv_sum + jnp.dot(
                tap_piece,
                full_weight[tap_index * channels : (tap_index + 1) * channels],
                preferred_element_type=jnp.float32,
            )
    conv_out = (
        (conv_sum + bias_all.astype(jnp.float32)[None, :])
        .astype(jnp.bfloat16)
        .reshape(images_here, side_cells, side_cells, out_chans)
    )
    back_weight, back_gain = (
        lax.all_gather(conv_weight, "fsdp", axis=0, tiled=True),
        lax.all_gather(norm_gain, "fsdp", axis=0, tiled=True),
    )
    grad_rows = out_grad.reshape(images_here * pixels, out_chans)
    grad_padded = jnp.zeros((images_here, side_cells + 2, side_cells + 2, channels), jnp.float32)
    weight_list = []
    for row_off in range(3):
        for col_off in range(3):
            tap_index = 3 * row_off + col_off
            tap_rows = back_weight[tap_index * channels : (tap_index + 1) * channels]
            tap_grad = lax.dot_general(
                grad_rows, tap_rows, (((1,), (1,)), ((), ())), preferred_element_type=jnp.float32
            )
            grad_padded = grad_padded.at[
                :, row_off : row_off + side_cells, col_off : col_off + side_cells, :
            ].add(tap_grad.reshape(images_here, side_cells, side_cells, channels))
            weight_list.append(
                lax.dot_general(
                    taps_list[tap_index],
                    grad_rows,
                    (((0,), (0,)), ((), ())),
                    preferred_element_type=jnp.float32,
                )
            )
    act_grad = grad_padded[:, 1:-1, 1:-1, :].reshape(images_here, pixels, GROUPS, group_size)
    sig_pre = jax.nn.sigmoid(pre_act)
    pre_grad = act_grad * sig_pre * (1.0 + pre_act * (1.0 - sig_pre))
    norm_grad = pre_grad * back_gain.astype(jnp.float32).reshape(1, 1, GROUPS, group_size)
    grad_mean = jnp.mean(norm_grad, axis=(1, 3), keepdims=True)
    cross_mean = jnp.mean(norm_grad * normed, axis=(1, 3), keepdims=True)
    in_grad = (
        ((norm_grad - grad_mean - normed * cross_mean) * inv_std)
        .astype(jnp.bfloat16)
        .reshape(images_here, side_cells, side_cells, channels)
    )
    rep_size = lax.axis_size("rep")
    fsdp_size = lax.axis_size("fsdp")
    grad_scale = 1.0 / math.sqrt(images_here * rep_size * fsdp_size * pixels)
    weight_term = jnp.concatenate(weight_list, axis=0) * grad_scale
    bias_term = jnp.sum(grad_rows.astype(jnp.float32), axis=0) * grad_scale
    gain_term = jnp.sum(pre_grad * normed, axis=(0, 1)).reshape(channels) * grad_scale
    shift_term = jnp.sum(pre_grad, axis=(0, 1)).reshape(channels) * grad_scale
    shards = (
        lax.psum_scatter(weight_term, "fsdp", scatter_dimension=0, tiled=True),
        lax.psum_scatter(bias_term, "fsdp", scatter_dimension=0, tiled=True),
        lax.psum_scatter(gain_term, "fsdp", scatter_dimension=0, tiled=True),
        lax.psum_scatter(shift_term, "fsdp", scatter_dimension=0, tiled=True),
    )
    weight_grad, bias_grad, gain_grad, shift_grad = lax.psum(
        (shards[0], shards[1], shards[2], shards[3]), "rep"
    )
    return (conv_out, in_grad, weight_grad, bias_grad, gain_grad, shift_grad)


def solution(mesh):
    placed = (
        P(("rep", "fsdp"), None, None, None),
        P(("rep", "fsdp"), None, None, None),
        P("fsdp", None),
        P("fsdp"),
        P("fsdp"),
        P("fsdp"),
    )
    out_placed = (
        P(("rep", "fsdp"), None, None, None),
        P(("rep", "fsdp"), None, None, None),
        P("fsdp", None),
        P("fsdp"),
        P("fsdp"),
        P("fsdp"),
    )

    def run(features, out_grad, conv_weight, *vectors):
        images, side, _, chans = features.shape
        rows, outs = conv_weight.shape
        shape = dict(mesh.shape)
        fast = fits(shape, images, rows // shape["fsdp"], chans, outs, side)
        return jax.shard_map(
            local_fast if fast else local,
            mesh=mesh,
            in_specs=placed,
            out_specs=out_placed,
            check_vma=False,
        )(features, out_grad, conv_weight, *vectors)

    return run
```

```python
import functools
import math

import jax
import jax.numpy as jnp
from jax import lax
from jax.experimental import pallas as pl
from jax.experimental.pallas import tpu as pltpu
from jax.sharding import PartitionSpec as P

GROUPS = 16


epsilon = 1e-05

F32 = jnp.float32
BF16 = jnp.bfloat16
VMEM = pl.BlockSpec(memory_space=pltpu.VMEM)
SMEM = pl.BlockSpec(memory_space=pltpu.SMEM)
ANY = pl.BlockSpec(memory_space=pl.ANY)


def params(mib=10):
    return pltpu.CompilerParams(vmem_limit_bytes=mib * 1024 * 1024)


def call(kernel, operands, in_specs, tokens=(), token=False, **options):
    given, after = len(operands), len(operands) + len(tokens)
    if token:
        out_shape, out_specs = options["out_shape"], options["out_specs"]
        if not isinstance(out_shape, tuple):
            out_shape, out_specs = (out_shape,), (out_specs,)
        options["out_shape"] = out_shape + (struct((1, 128), F32),)
        options["out_specs"] = out_specs + (VMEM,)
    outs = len(options["out_shape"]) - 1 if token else 0

    def body(*refs):
        refs = refs[:given] + refs[after:]
        if token:
            at = given + outs
            refs[at][...] = jnp.zeros_like(refs[at])
            refs = refs[:at] + refs[at + 1 :]
        kernel(*refs)

    return pl.pallas_call(
        body, in_specs=list(in_specs) + [VMEM] * len(tokens), **options
    )(*operands, *tokens)


def struct(shape, dtype):
    return jax.ShapeDtypeStruct(shape, dtype)


def shifted_copies(x, side, out_ref, first):
    pixels = x.shape[0]
    column = lax.broadcasted_iota(jnp.int32, x.shape, 0) % side
    edge = jnp.zeros((side, x.shape[1]), BF16)
    for kx in range(3):
        move = (kx - 1) if first else (1 - kx)
        if move == 0:
            moved = x
        elif move == 1:
            moved = jnp.where(column == side - 1, 0.0, pltpu.roll(x, pixels - 1, 0))
        else:
            moved = jnp.where(column == 0, 0.0, pltpu.roll(x, 1, 0))
        out_ref[kx, 0:side, :] = edge
        out_ref[kx, side : side + pixels, :] = moved.astype(BF16)
        out_ref[kx, side + pixels : 2 * side + pixels, :] = edge


def shift_kernel(side, x_ref, out_ref, sum_ref):
    x = x_ref[...].astype(F32)
    sum_ref[...] = jnp.sum(x, axis=0, keepdims=True)
    shifted_copies(x, side, out_ref, False)


def shift_grad(x, side, tokens):
    pixels, chans = x.shape
    return call(
        functools.partial(shift_kernel, side),
        (x,),
        [VMEM],
        tokens,
        out_shape=(
            struct((3, pixels + 2 * side, chans), BF16),
            struct((1, chans), F32),
        ),
        out_specs=(VMEM, VMEM),
        compiler_params=params(),
        cost_estimate=pl.CostEstimate(
            flops=8 * x.size, bytes_accessed=8 * x.size, transcendentals=0
        ),
        name="shift_grad",
    )


def group_means(sums, pixels):
    chans = sums.shape[1]
    size = chans // GROUPS
    lanes = round_up(GROUPS, 128)
    channel = lax.broadcasted_iota(jnp.int32, (chans, lanes), 0)
    first = lax.broadcasted_iota(jnp.int32, (chans, lanes), 1) * size
    member = jnp.where((channel >= first) & (channel < first + size), 1.0, 0.0).astype(F32)
    exact = {"preferred_element_type": F32, "precision": lax.Precision.HIGHEST}
    total = jnp.dot(sums, member, **exact)
    spread = lax.dot_general(total, member, (((1,), (1,)), ((), ())), **exact)
    return spread * (1.0 / (pixels * size))


def stats_kernel(x_ref, out_ref):
    pixels = x_ref.shape[0]
    x = x_ref[...].astype(F32)
    spread = (8, x.shape[1])
    column_sum = jnp.sum(x, axis=0, keepdims=True)
    mean = group_means(jnp.broadcast_to(column_sum, spread), pixels)[0:1]
    centered = x - mean
    column_sum = jnp.sum(centered * centered, axis=0, keepdims=True)
    var = group_means(jnp.broadcast_to(column_sum, spread), pixels)[0:1]
    out_ref[0:1, :] = mean
    out_ref[1:2, :] = lax.rsqrt(var + epsilon)


def stats(x):
    return pl.pallas_call(
        stats_kernel,
        out_shape=struct((2, x.shape[1]), F32),
        in_specs=[VMEM],
        out_specs=VMEM,
        compiler_params=params(),
        cost_estimate=pl.CostEstimate(
            flops=5 * x.size, bytes_accessed=2 * x.size, transcendentals=0
        ),
        name="norm_stats",
    )(x)


def activation(x_ref, stat_ref, vec_ref):
    mean, inv = stat_ref[0:1, :], stat_ref[1:2, :]
    gain = vec_ref[0:1, :].astype(F32)
    shift = vec_ref[1:2, :].astype(F32)
    pre = (x_ref[...].astype(F32) - mean) * inv * gain + shift
    return (pre / (1.0 + jnp.exp(-pre))).astype(BF16)


def act_kernel(x_ref, stat_ref, vec_ref, turned_ref):
    turned_ref[...] = activation(x_ref, stat_ref, vec_ref).T


def activate(x, stat, vecs, tokens):
    pixels, chans = x.shape
    return call(
        act_kernel,
        (x, stat, vecs),
        [VMEM, VMEM, VMEM],
        tokens,
        True,
        out_shape=struct((chans, pixels), BF16),
        out_specs=VMEM,
        compiler_params=params(),
        cost_estimate=pl.CostEstimate(
            flops=10 * x.size, bytes_accessed=4 * x.size, transcendentals=2 * x.size
        ),
        name="activate",
    )


def weight_blocks(side, extra, blocks, core, own_t, sib_t, own_g, sib_g, first, count, block_ref):
    chans, pixels = own_t.shape

    def tap_rows(ref, tap):
        start = pl.multiple_of((2 - tap // 3) * side, side)
        return ref[tap % 3, pl.ds(start, pixels), first : first + count]

    def product(low, high, tap):
        return jnp.dot(
            own_t[low:high, :], tap_rows(own_g, tap), preferred_element_type=F32
        ) + jnp.dot(sib_t[low:high, :], tap_rows(sib_g, tap), preferred_element_type=F32)

    for k in range(blocks):
        low, high = 2 * extra * k, 2 * extra * (k + 1)
        block_ref[0 : chans - low, :] = product(low, chans, 2 * k + core)
        block_ref[chans - low : chans + 2 * extra, :] = product(0, high, 2 * k + 1 + core)
        yield k


def weight_by_rep_kernel(
    side, extra, first, piece, place_ref, own_t, sib_t, own_g, sib_g,
    keep_ref, send0_ref, send1_ref, block_ref,
):
    chans = own_t.shape[0]
    r, z, core = place_ref[0], place_ref[1], place_ref[2]
    half, count = keep_ref.shape[2], keep_ref.shape[4]
    reps = 2 * keep_ref.shape[1]
    step = (chans + extra - piece) // (reps - 1)

    def rows_of(rel):
        at = extra * core + step * (r ^ rel)
        past = at % 8
        rows = block_ref[pl.ds(pl.multiple_of(at - past, 8), piece + piece % 8), :]
        return jnp.where(past == 0, rows[:piece], rows[piece % 8 :])

    for k in weight_blocks(
        side, extra, 2 * half, core, own_t, sib_t, own_g, sib_g, first, count, block_ref
    ):
        rel_z = k ^ z
        path, slot = rel_z // half, rel_z % half
        keep_ref[path, 0, slot] = rows_of(0)

        @pl.when(path == 0)
        def _():
            send0_ref[0, slot] = rows_of(1).astype(BF16)
            keep_ref[0, 1, slot] = rows_of(2)
            send0_ref[1, slot] = rows_of(3).astype(BF16)

        @pl.when(path == 1)
        def _():
            send1_ref[0, slot] = rows_of(2).astype(BF16)
            keep_ref[1, 1, slot] = rows_of(1)
            send1_ref[1, slot] = rows_of(3).astype(BF16)


def weight_call(kernel, out_shape, place, operands, extra, first, count, blocks, tokens, name):
    chans, pixels = operands[0].shape
    return call(
        kernel,
        (place,) + operands,
        [SMEM, VMEM, VMEM, VMEM, VMEM],
        tokens,
        True,
        out_shape=out_shape,
        out_specs=(VMEM,) * len(out_shape),
        scratch_shapes=[pltpu.VMEM((chans + 2 * extra, count), F32)],
        compiler_params=params(12),
        cost_estimate=pl.CostEstimate(
            flops=4 * blocks * (chans + 2 * extra) * pixels * count,
            bytes_accessed=20 * chans * pixels,
            transcendentals=0,
        ),
        name=name,
    )


def weight_by_rep(place, operands, side, blocks, extra, piece, first, count, tokens):
    half = blocks // 2
    out_shape = (
        struct((2, 2, half, piece, count), F32),
        struct((2, half, piece, count), BF16),
        struct((2, half, piece, count), BF16),
    )
    kernel = functools.partial(weight_by_rep_kernel, side, extra, first, piece)
    return weight_call(
        kernel, out_shape, place, operands, extra, first, count, blocks, tokens, "weight_grad_rep"
    )


def finish_kernel(bias_ref, param_ref, *refs):
    out_ref = refs[-1]
    total = refs[0][...]
    for ref in refs[1:-1]:
        total = total + ref[...].astype(F32)
    piece = total.shape[0]
    head = 16
    rest = jnp.zeros((out_ref.shape[0] - head - piece, total.shape[1]), F32)
    out_ref[head:, :] = jnp.concatenate([total, rest], axis=0).astype(BF16)
    small = jnp.concatenate([bias_ref[...], param_ref[...]], axis=0)
    high = small.astype(BF16).astype(F32)
    middle = (small - high).astype(BF16).astype(F32)
    parts = [high, middle, small - high - middle]
    spare = head - 3 * small.shape[0]
    parts.append(jnp.zeros((spare, small.shape[1]), F32))
    out_ref[0:head, :] = jnp.concatenate(parts, axis=0).astype(BF16)


def finish(terms, small):
    piece, outs = terms[0].shape
    return call(
        finish_kernel,
        (*small, *terms),
        [VMEM] * (2 + len(terms)),
        (),
        True,
        out_shape=struct((16 + round_up(piece, 16), outs), BF16),
        out_specs=VMEM,
        compiler_params=params(8),
        cost_estimate=pl.CostEstimate(
            flops=4 * terms[0].size, bytes_accessed=12 * terms[0].size, transcendentals=0
        ),
        name="finish_sum",
    )


def add_small_kernel(piece, *refs):
    out_ref = refs[-1]
    count = out_ref.shape[0]
    terms = []
    for ref in refs[:-1]:
        rows = ref[0:16, :].astype(F32)
        terms.append(rows[0:count] + rows[count : 2 * count] + rows[2 * count : 3 * count])
    out_ref[...] = tree_sum(terms)


def add_small_of(pieces, piece, count, tokens):
    return call(
        functools.partial(add_small_kernel, piece),
        pieces,
        [VMEM] * len(pieces),
        tokens,
        out_shape=struct((count, pieces[0].shape[1]), F32),
        out_specs=VMEM,
        compiler_params=params(4),
        cost_estimate=pl.CostEstimate(
            flops=4 * pieces[0].size, bytes_accessed=4 * pieces[0].size, transcendentals=0
        ),
        name="add_small_of",
    )


def rep_step_kernel(keep_ref, got0, got1, next0, next1):
    next0[...] = (keep_ref[0, 1] + got0[1].astype(F32)).astype(BF16)
    next1[...] = (keep_ref[1, 1] + got1[1].astype(F32)).astype(BF16)


def rep_step(keep, got0, got1, tokens):
    out = struct(keep.shape[2:], BF16)
    return call(
        rep_step_kernel,
        (keep, got0, got1),
        [VMEM] * 3,
        tokens,
        out_shape=(out, out),
        out_specs=(VMEM, VMEM),
        compiler_params=params(12),
        cost_estimate=pl.CostEstimate(
            flops=keep.size, bytes_accessed=4 * keep.size, transcendentals=0
        ),
        name="rep_step",
    )


def rep_sum_kernel(keep_ref, got0, got1, last0, last1, own_ref, *sends):
    half = keep_ref.shape[2]
    for i, out in enumerate((own_ref,) + sends):
        path, slot = i // half, i % half
        got, last = ((got0, last0), (got1, last1))[path]
        total = keep_ref[path, 0, slot] + got[0, slot].astype(F32) + last[slot].astype(F32)
        out[...] = total.astype(out.dtype)


def rep_sum(keep, got0, got1, last0, last1, tokens):
    half, piece, count = keep.shape[2:]
    return call(
        rep_sum_kernel,
        (keep, got0, got1, last0, last1),
        [VMEM] * 5,
        tokens,
        True,
        out_shape=(struct((piece, count), F32),)
        + (struct((piece, count), BF16),) * (2 * half - 1),
        out_specs=(VMEM,) * (2 * half),
        compiler_params=params(12),
        cost_estimate=pl.CostEstimate(
            flops=keep.size, bytes_accessed=4 * keep.size, transcendentals=0
        ),
        name="rep_sum",
    )


def prepare_kernel(side, x_ref, stat_ref, vec_ref, shifted_ref):
    act = activation(x_ref, stat_ref, vec_ref)
    shifted_copies(act.astype(F32), side, shifted_ref, True)


def prepare(x, stat, vecs, side, tokens):
    pixels, chans = x.shape
    return call(
        functools.partial(prepare_kernel, side),
        (x, stat, vecs),
        [VMEM] * 3,
        tokens,
        out_shape=struct((3, pixels + 2 * side, chans), BF16),
        out_specs=VMEM,
        compiler_params=params(16),
        cost_estimate=pl.CostEstimate(
            flops=20 * x.size, bytes_accessed=8 * x.size, transcendentals=2 * x.size
        ),
        name="prepare",
    )


def arrange_kernel(source, out_ref, sems):
    rows, outs = out_ref.shape[0] // 3, source.shape[1]
    copies = [
        pltpu.make_async_copy(
            source.at[pl.ds(tap * rows, rows), :],
            out_ref.at[pl.ds(tap % 3 * rows, rows), pl.ds(tap // 3 * outs, outs)],
            sems.at[tap],
        )
        for tap in range(9)
    ]
    for c in copies:
        c.start()
    for c in copies:
        c.wait()


def arrange(weight):
    rows, outs = weight.shape
    return call(
        arrange_kernel,
        (weight,),
        [ANY],
        out_shape=struct((rows // 3, 3 * outs), BF16),
        out_specs=VMEM,
        scratch_shapes=[pltpu.SemaphoreType.DMA((9,))],
        compiler_params=params(44),
        cost_estimate=pl.CostEstimate(
            flops=0, bytes_accessed=4 * weight.size, transcendentals=0
        ),
        name="arrange_weight",
    )


def grad_kernel(
    side, chunk, raw_ref, x_ref, stat_ref, vec_ref, weight, out_ref, sum_ref, scaled, g_ref
):
    pixels, chans = x_ref.shape
    edge = jnp.zeros((side, raw_ref.shape[1]), BF16)
    g_ref[0:side, :] = edge
    g_ref[side : side + pixels, :] = raw_ref[...]
    g_ref[side + pixels :, :] = edge
    column = lax.broadcasted_iota(jnp.int32, (chunk, chans), 0) % side
    mean, inv = stat_ref[0:1, :], stat_ref[1:2, :]
    gain = vec_ref[0:1, :].astype(F32)
    shift = vec_ref[1:2, :].astype(F32)
    sum_ref[...] = jnp.zeros_like(sum_ref)

    @pl.loop(0, pixels // chunk)
    def _(i):
        rows_of = [
            g_ref[pl.ds(pl.multiple_of(i * chunk + (2 - ky) * side, side), chunk), :]
            for ky in range(3)
        ]
        total = lax.dot_general(
            jnp.concatenate(rows_of, axis=1),
            weight[...],
            (((1,), (1,)), ((), ())),
            preferred_element_type=F32,
        )
        before, same, later = (total[:, kx * chans : (kx + 1) * chans] for kx in range(3))
        total = (
            same
            + jnp.where(column == side - 1, 0.0, pltpu.roll(before, chunk - 1, 0))
            + jnp.where(column == 0, 0.0, pltpu.roll(later, 1, 0))
        )
        rows = pl.ds(pl.multiple_of(i * chunk, chunk), chunk)
        normed = (x_ref[rows, :].astype(F32) - mean) * inv
        pre = normed * gain + shift
        sig = 1.0 / (1.0 + jnp.exp(-pre))
        pre_grad = total * sig * (1.0 + pre * (1.0 - sig))
        sum_ref[0:1, :] += jnp.sum(pre_grad * normed, axis=0, keepdims=True)
        sum_ref[1:2, :] += jnp.sum(pre_grad, axis=0, keepdims=True)
        scaled[rows, :] = pre_grad * gain

    rest = jnp.zeros((6, chans), F32)
    means = group_means(jnp.concatenate([sum_ref[...] * gain, rest], axis=0), pixels)
    cross, center = means[0:1], means[1:2]

    @pl.loop(0, pixels // 256)
    def _(i):
        rows = pl.ds(pl.multiple_of(i * 256, 256), 256)
        normed = (x_ref[rows, :].astype(F32) - mean) * inv
        out_ref[rows, :] = ((scaled[rows, :] - center - normed * cross) * inv).astype(BF16)


def act_grad(g, x, stat, vecs, weight, side, tokens):
    pixels, chans = x.shape
    outs = g.shape[1]
    return call(
        functools.partial(grad_kernel, side, pixels),
        (g, x, stat, vecs, weight),
        [VMEM] * 5,
        tokens,
        out_shape=(struct((pixels, chans), BF16), struct((2, chans), F32)),
        out_specs=(VMEM, VMEM),
        scratch_shapes=[
            pltpu.VMEM((pixels, chans), F32),
            pltpu.VMEM((pixels + 2 * side, outs), BF16),
        ],
        compiler_params=params(32),
        cost_estimate=pl.CostEstimate(
            flops=18 * chans * outs * pixels,
            bytes_accessed=18 * chans * outs + 12 * pixels * chans,
            transcendentals=2 * pixels * chans,
        ),
        name="act_grad",
    )


def conv_kernel(side, first, a_ref, vec_ref, weight, *rest):
    out_ref, token_ref, held, sem = rest[-4:]
    token_ref[...] = jnp.zeros_like(token_ref)
    count, outs = held.shape
    pixels = out_ref.shape[0]
    low, high = max(0, first - side), min(pixels, first + count + side)
    shifted = jnp.concatenate([a_ref[kx, side + low : side + high, :] for kx in range(3)], axis=1)
    parts = jnp.dot(shifted, weight[...], preferred_element_type=F32)
    total = None
    for ky in range(3):
        begin = first + (ky - 1) * side
        end = begin + count
        part = parts[max(begin, 0) - low : min(end, pixels) - low, ky * outs : (ky + 1) * outs]
        edge = jnp.zeros((side, outs), F32)
        if begin < 0:
            part = jnp.concatenate([edge, part], axis=0)
        if end > pixels:
            part = jnp.concatenate([part, edge], axis=0)
        total = part if total is None else total + part
    held[...] = (total + vec_ref[2:3, :].astype(F32)).astype(BF16)
    copy = pltpu.make_async_copy(held, out_ref.at[pl.ds(first, count), :], sem)
    copy.start()
    copy.wait()


def conv(shifted, vecs, weight, side, first, count, before, tokens):
    chans = shifted.shape[2]
    pixels = shifted.shape[1] - 2 * side
    outs = weight.shape[1] // 3
    operands = (shifted, vecs, weight) + (() if before is None else (before,))
    return call(
        functools.partial(conv_kernel, side, first),
        operands,
        [VMEM] * 3 + [ANY] * (len(operands) - 3),
        tokens,
        out_shape=(struct((pixels, outs), BF16), struct((1, 128), F32)),
        out_specs=(ANY, VMEM),
        input_output_aliases={} if before is None else {3: 0},
        scratch_shapes=[pltpu.VMEM((count, outs), BF16), pltpu.SemaphoreType.DMA],
        compiler_params=params(24),
        cost_estimate=pl.CostEstimate(
            flops=18 * chans * outs * count,
            bytes_accessed=18 * chans * outs + 4 * count * chans,
            transcendentals=0,
        ),
        name="conv_forward",
    )


def join_kernel(scale, piece, place_ref, p0, p1, p2, p3, out_ref):
    r = place_ref[0]
    pieces = (p0, p1, p2, p3)
    step = (out_ref.shape[0] - piece) // (len(pieces) - 1)
    for q in range(len(pieces)):
        for rel, ref in enumerate(pieces):

            @pl.when((q ^ r) == rel)
            def _():
                out_ref[step * q : step * q + piece, :] = ref[16:, :].astype(F32)[:piece] * scale


def join(place, pieces, rows, piece, scale, tokens):
    outs = pieces[0].shape[1]
    return call(
        functools.partial(join_kernel, scale, piece),
        (place, *pieces),
        [SMEM] + [VMEM] * 4,
        tokens,
        True,
        out_shape=struct((rows, outs), F32),
        out_specs=VMEM,
        compiler_params=params(),
        cost_estimate=pl.CostEstimate(
            flops=rows * outs, bytes_accessed=6 * rows * outs, transcendentals=0
        ),
        name="join_pieces",
    )


def tree_sum(terms):
    while len(terms) > 1:
        terms = [terms[i] + terms[i + 1] for i in range(0, len(terms), 2)]
    return terms[0]


def add_kernel(*refs):
    refs[-1][...] = tree_sum([ref[...] for ref in refs[:-1]])


def add_small(terms, tokens):
    return call(
        add_kernel,
        terms,
        [VMEM] * len(terms),
        tokens,
        out_shape=struct(terms[0].shape, F32),
        out_specs=VMEM,
        compiler_params=params(2),
        cost_estimate=pl.CostEstimate(
            flops=4 * terms[0].size, bytes_accessed=16 * terms[0].size, transcendentals=0
        ),
        name="add_small",
    )


def swap(x, axis, mask):
    n = lax.axis_size(axis)
    return lax.ppermute(x, axis, [(i, i ^ mask) for i in range(n)])


def gather_small(x):
    at = lax.axis_index("fsdp")
    other = swap(x, "fsdp", 1)
    pair = jnp.where(at % 2 == 1, jnp.stack([other, x]), jnp.stack([x, other]))
    got = [pair] + [swap(pair, "fsdp", m) for m in range(2, lax.axis_size("fsdp"), 2)]
    mask = 1
    while mask < len(got):
        flip = (at // (2 * mask)) % 2 == 1
        got = [jnp.where(flip, got[i ^ mask], got[i]) for i in range(len(got))]
        mask *= 2
    return jnp.concatenate(got)


def sum_all(x, axis, masks):
    return tree_sum([x] + [swap(x, axis, m) for m in masks])


def local_fast(features, out_grad, conv_weight, conv_bias, norm_gain, norm_shift):
    side = features.shape[1]
    chans = features.shape[3]
    outs = out_grad.shape[3]
    pixels = side * side
    rows = conv_weight.shape[0]
    reps, shards = lax.axis_size("rep"), lax.axis_size("fsdp")
    r, f = lax.axis_index("rep"), lax.axis_index("fsdp")
    z, core = f // 2, f % 2
    extra = rows - chans
    piece = -(-rows // reps)
    x = features.reshape(pixels, chans)
    g = out_grad.reshape(pixels, outs)
    place = jnp.stack([r, z, core]).astype(jnp.int32)

    weight = lax.all_gather(conv_weight, "fsdp", axis=0, tiled=True)
    small = gather_small(jnp.stack([norm_gain, norm_shift, conv_bias]))
    sib_g = swap(g, "fsdp", 1)

    stat = stats(x)
    vecs = jnp.transpose(small, (1, 0, 2)).reshape(3, chans)
    own_t, act_token = activate(x, stat, vecs, ())
    sib_t = swap(own_t, "fsdp", 1)
    own_shifted, bias_sum = shift_grad(g, side, (act_token,))
    sib_shifted, _ = shift_grad(sib_g, side, (act_token,))
    operands = (own_t, sib_t, own_shifted, sib_shifted)

    keep, send0, send1, weight_token = weight_by_rep(
        place, operands, side, shards // 2, extra, piece, 0, outs, ()
    )
    got0 = swap(send0, "rep", 1)
    got1 = swap(send1, "rep", 2)
    next0, next1 = rep_step(keep, got0, got1, ())
    last0 = swap(next0, "rep", 2)
    last1 = swap(next1, "rep", 1)
    own_sum, *sends, sum_token = rep_sum(keep, got0, got1, last0, last1, ())
    got = [swap(a, "fsdp", 2 * (m + 1)) for m, a in enumerate(sends)]
    act_shifted = prepare(x, stat, vecs, side, (weight_token,))
    weight = arrange(weight)
    in_grad, param_sums = act_grad(g, x, stat, vecs, weight, side, (sum_token,))
    done, done_token = finish((own_sum, *got), (bias_sum, param_sums))
    pieces_done = [done] + [swap(done, "rep", m) for m in range(1, reps)]

    conv_out, token = conv(act_shifted, vecs, weight, side, 0, pixels, None, (done_token,))
    small_sums = add_small_of(pieces_done, piece, 3, (token,))
    over_z = [small_sums] + [swap(small_sums, "fsdp", m) for m in range(2, shards, 2)]
    scale = 1.0 / math.sqrt(reps * shards * pixels)
    weight_grad, token = join(place, pieces_done, rows, piece, scale, (token,))
    small_sums = sum_all(add_small(over_z, (token,)), "fsdp", (1,)) * scale
    share = outs // shards
    mine = lax.dynamic_slice_in_dim(small_sums.reshape(3, shards, share), f, 1, axis=1)
    mine = mine.reshape(3, share)
    return (
        conv_out.reshape(1, side, side, outs),
        in_grad.reshape(1, side, side, chans),
        weight_grad,
        mine[0],
        mine[1],
        mine[2],
    )


def round_up(n, m):
    return -(-n // m) * m


def fits(mesh_shape, images, rows, chans, outs, side):
    reps, shards = mesh_shape["rep"], mesh_shape["fsdp"]
    if images != reps * shards or reps != 2 * 2 or shards != 9 - 1:
        return False
    if chans != outs or rows * shards != 9 * chans or chans % 128 or side % 16 or outs < 3 * 128:
        return False
    extra, piece = rows - chans, -(-rows // reps)
    step = (rows - piece) // (reps - 1)
    return (
        extra % 16 == 0
        and step * (reps - 1) == rows - piece
        and step == piece
        and piece % 8 in (0, 4)
        and extra % 8 == 0
    )


def local(features, out_grad, conv_weight, conv_bias, norm_gain, norm_shift):
    images_here = features.shape[0]
    side_cells = features.shape[1]
    channels = features.shape[3]
    pixels = side_cells * side_cells
    group_size = channels // GROUPS
    full_weight, bias_all, gain_all, shift_all = (
        lax.all_gather(conv_weight, "fsdp", axis=0, tiled=True),
        lax.all_gather(conv_bias, "fsdp", axis=0, tiled=True),
        lax.all_gather(norm_gain, "fsdp", axis=0, tiled=True),
        lax.all_gather(norm_shift, "fsdp", axis=0, tiled=True),
    )
    out_chans = full_weight.shape[1]
    values = features.astype(jnp.float32).reshape(images_here, pixels, GROUPS, group_size)
    group_mean = jnp.mean(values, axis=(1, 3), keepdims=True)
    centered = values - group_mean
    group_var = jnp.mean(centered * centered, axis=(1, 3), keepdims=True)
    inv_std = lax.rsqrt(group_var + epsilon)
    normed = centered * inv_std
    gain_cols = gain_all.astype(jnp.float32).reshape(1, 1, GROUPS, group_size)
    shift_cols = shift_all.astype(jnp.float32).reshape(1, 1, GROUPS, group_size)
    pre_act = normed * gain_cols + shift_cols
    activated = (
        jax.nn.silu(pre_act)
        .astype(jnp.bfloat16)
        .reshape(images_here, side_cells, side_cells, channels)
    )
    padded = jnp.pad(activated, ((0, 0), (1, 1), (1, 1), (0, 0)))
    conv_sum = jnp.zeros((images_here * pixels, out_chans), jnp.float32)
    taps_list = []
    for row_off in range(3):
        for col_off in range(3):
            tap_index = 3 * row_off + col_off
            tap_piece = padded[
                :, row_off : row_off + side_cells, col_off : col_off + side_cells, :
            ].reshape(images_here * pixels, channels)
            taps_list.append(tap_piece)
            conv_sum = conv_sum + jnp.dot(
                tap_piece,
                full_weight[tap_index * channels : (tap_index + 1) * channels],
                preferred_element_type=jnp.float32,
            )
    conv_out = (
        (conv_sum + bias_all.astype(jnp.float32)[None, :])
        .astype(jnp.bfloat16)
        .reshape(images_here, side_cells, side_cells, out_chans)
    )
    back_weight, back_gain = (
        lax.all_gather(conv_weight, "fsdp", axis=0, tiled=True),
        lax.all_gather(norm_gain, "fsdp", axis=0, tiled=True),
    )
    grad_rows = out_grad.reshape(images_here * pixels, out_chans)
    grad_padded = jnp.zeros((images_here, side_cells + 2, side_cells + 2, channels), jnp.float32)
    weight_list = []
    for row_off in range(3):
        for col_off in range(3):
            tap_index = 3 * row_off + col_off
            tap_rows = back_weight[tap_index * channels : (tap_index + 1) * channels]
            tap_grad = lax.dot_general(
                grad_rows, tap_rows, (((1,), (1,)), ((), ())), preferred_element_type=jnp.float32
            )
            grad_padded = grad_padded.at[
                :, row_off : row_off + side_cells, col_off : col_off + side_cells, :
            ].add(tap_grad.reshape(images_here, side_cells, side_cells, channels))
            weight_list.append(
                lax.dot_general(
                    taps_list[tap_index],
                    grad_rows,
                    (((0,), (0,)), ((), ())),
                    preferred_element_type=jnp.float32,
                )
            )
    act_grad = grad_padded[:, 1:-1, 1:-1, :].reshape(images_here, pixels, GROUPS, group_size)
    sig_pre = jax.nn.sigmoid(pre_act)
    pre_grad = act_grad * sig_pre * (1.0 + pre_act * (1.0 - sig_pre))
    norm_grad = pre_grad * back_gain.astype(jnp.float32).reshape(1, 1, GROUPS, group_size)
    grad_mean = jnp.mean(norm_grad, axis=(1, 3), keepdims=True)
    cross_mean = jnp.mean(norm_grad * normed, axis=(1, 3), keepdims=True)
    in_grad = (
        ((norm_grad - grad_mean - normed * cross_mean) * inv_std)
        .astype(jnp.bfloat16)
        .reshape(images_here, side_cells, side_cells, channels)
    )
    rep_size = lax.axis_size("rep")
    fsdp_size = lax.axis_size("fsdp")
    grad_scale = 1.0 / math.sqrt(images_here * rep_size * fsdp_size * pixels)
    weight_term = jnp.concatenate(weight_list, axis=0) * grad_scale
    bias_term = jnp.sum(grad_rows.astype(jnp.float32), axis=0) * grad_scale
    gain_term = jnp.sum(pre_grad * normed, axis=(0, 1)).reshape(channels) * grad_scale
    shift_term = jnp.sum(pre_grad, axis=(0, 1)).reshape(channels) * grad_scale
    shards = (
        lax.psum_scatter(weight_term, "fsdp", scatter_dimension=0, tiled=True),
        lax.psum_scatter(bias_term, "fsdp", scatter_dimension=0, tiled=True),
        lax.psum_scatter(gain_term, "fsdp", scatter_dimension=0, tiled=True),
        lax.psum_scatter(shift_term, "fsdp", scatter_dimension=0, tiled=True),
    )
    weight_grad, bias_grad, gain_grad, shift_grad = lax.psum(
        (shards[0], shards[1], shards[2], shards[3]), "rep"
    )
    return (conv_out, in_grad, weight_grad, bias_grad, gain_grad, shift_grad)


def solution(mesh):
    placed = (
        P(("rep", "fsdp"), None, None, None),
        P(("rep", "fsdp"), None, None, None),
        P("fsdp", None),
        P("fsdp"),
        P("fsdp"),
        P("fsdp"),
    )
    out_placed = (
        P(("rep", "fsdp"), None, None, None),
        P(("rep", "fsdp"), None, None, None),
        P("fsdp", None),
        P("fsdp"),
        P("fsdp"),
        P("fsdp"),
    )

    def run(features, out_grad, conv_weight, *vectors):
        images, side, _, chans = features.shape
        rows, outs = conv_weight.shape
        shape = dict(mesh.shape)
        fast = fits(shape, images, rows // shape["fsdp"], chans, outs, side)
        return jax.shard_map(
            local_fast if fast else local,
            mesh=mesh,
            in_specs=placed,
            out_specs=out_placed,
            check_vma=False,
        )(features, out_grad, conv_weight, *vectors)

    return run
```
